32 devices in a mesh: head: 4 (over y, core), blk: 8 (over z, x).
Axes of the slice: x: 2, y: 2, z: 4, core: 2. Of those that a mesh axis runs over, the one named last changes fastest.
Arguments:
- tokens: bfloat16 [4096, 768], P(('head', 'blk')), may hold values from -6 to 6
- prev_logits: float32 [4096, 12], P(('head', 'blk')), may hold values from -4 to 4
- norm_gains: bfloat16 [2, 2, 768], P(None, None, ('head', 'blk')), may hold values from 0.5 to 1.5
- attn_in_weight: bfloat16 [2, 768, 2304], P(None, ('head', 'blk')), may hold values from -0.21875 to 0.21875
- attn_out_weight: bfloat16 [2, 768, 768], P(None, ('head', 'blk')), may hold values from -0.75 to 0.75
- router_weight: bfloat16 [2, 768, 12], P(None, ('head', 'blk')), may hold values from -0.14941406 to 0.14941406
- const_mix: bfloat16 [2, 768, 4], P(None, ('head', 'blk')), may hold values from -0.21875 to 0.21875
- const_values: bfloat16 [2, 2, 768], P(None, None, ('head', 'blk')), may hold values from -6 to 6
- expert_gate: bfloat16 [2, 8, 768, 2048], P(None, 'head', 'blk'), may hold values from -0.21875 to 0.21875
- expert_up: bfloat16 [2, 8, 768, 2048], P(None, 'head', 'blk'), may hold values from -0.21875 to 0.21875
- expert_down: bfloat16 [2, 8, 768, 2048], P(None, 'head', 'blk'), may hold values from -0.25 to 0.25
- routes: int32 [2, 4096, 2], P(None, ('head', 'blk')), may hold values from 0 to 11, all different within a row
- order: int32 [2, 4096, 2], P(None, ('head', 'blk')), may hold values from 0 to 255, as said below
- cotangent: bfloat16 [4096, 768], P(('head', 'blk')), may hold values from -6 to 6
Outputs:
- output: bfloat16 [4096, 768], P(('head', 'blk'))
- input_grad: float32 [4096, 768], P(('head', 'blk'))
- logits_grad: float32 [4096, 12], P(('head', 'blk'))
- gains_grad: float32 [2, 2, 768], P(None, None, ('head', 'blk'))
- attn_in_grad: float32 [2, 768, 2304], P(None, ('head', 'blk'))
- attn_out_grad: float32 [2, 768, 768], P(None, ('head', 'blk'))
- router_grad: float32 [2, 768, 12], P(None, ('head', 'blk'))
- mix_grad: float32 [2, 768, 4], P(None, ('head', 'blk'))
- values_grad: float32 [2, 2, 768], P(None, None, ('head', 'blk'))
- gate_grad: float32 [2, 8, 768, 2048], P(None, 'head', 'blk')
- up_grad: float32 [2, 8, 768, 2048], P(None, 'head', 'blk')
- down_grad: float32 [2, 8, 768, 2048], P(None, 'head', 'blk')
The draws below stay inside these ranges and needn't reach their ends.
Inputs may be any that keep to these rules, and one draw needn't show every extreme that they name: `routes`: each token names two different experts; ids 8, 9, 10 and 11 are the zero, copy and two constant experts. `order`: within each layer and each aligned block of 128 tokens, the 256 entries are each of 0 to 255 once.
All inputs are finite; a program needn't handle non-finite values.
Results may differ from the reference program's by a relative error of at most 0.039.
Values may be sent and summed in bfloat16 or wider, within the bound.
A program may use at most 320 MiB of HBM per device.

```python
import jax
import jax.numpy as jnp
from jax import lax

D = 768
HEADS = 12
HD = 64
FF = 2048
NF = 8
TOP = 2
LAYERS = 2
TOK_DEV = 128
NE = 12
SEQS = 4
LENGTH = 1024
TOKENS = 4096
CAP = 26


def draw_order(key, part):
    key = jax.random.fold_in(key, 11)
    blocks = LAYERS * (TOKENS // TOK_DEV)
    streams = jax.random.split(key, blocks)
    orders = jax.vmap(lambda stream: jax.random.permutation(stream, TOK_DEV * TOP))(streams)
    return orders.reshape(LAYERS, TOKENS, TOP).astype(jnp.int32)


def shard_levels(rng, shape, pieces, least, largest):
    def one(dim, blocks):
        heights = jax.random.uniform(jax.random.fold_in(jax.random.fold_in(rng, 6), dim), (blocks,), jnp.float32, least / len(pieces), largest / len(pieces))
        return jnp.repeat(jnp.exp(heights), shape[dim] // blocks).reshape((-1,) + (1,) * (len(shape) - dim - 1))

    level = one(*pieces[0])
    for cut in pieces[1:]:
        level = level * one(*cut)
    return level


def picks_of(key, rows, amount, top, lift):
    ranking = jax.random.permutation(jax.random.fold_in(key, 1), amount)
    pull = ranking
    for power in range(3):
        pull = pull * pull // amount
    pull = pull * lift // amount
    tickets = jax.random.randint(jax.random.fold_in(key, 2), (rows, amount), 0, 4096) + pull
    sure = jax.random.permutation(jax.random.fold_in(key, 3), rows)[jnp.arange(amount) % rows]
    tickets = jnp.where(jnp.arange(rows)[:, None] == sure[None, :], 1 << 14, tickets)
    score = tickets * amount + jnp.arange(amount)
    return lax.top_k(score.astype(jnp.int32), top)[1].astype(jnp.int32)


def bell_draw(own_key, shape, width, bound, cuts=(), kind=jnp.bfloat16):
    values = jax.random.normal(own_key, shape, jnp.float32) * width
    if len(cuts) > 0:
        values = shard_levels(own_key, shape, cuts, -0.22, 0.18) * values
    return jnp.clip(values, min=-bound, max=bound).astype(kind)


def setup_inputs(seed: int = 0) -> dict:
    streams_of = jax.random.split(jax.random.key(seed), 15)
    return {
        "tokens": bell_draw(streams_of[0], (TOKENS, D), 1.0, 6.0, ((0, 32),)),
        "prev_logits": bell_draw(streams_of[1], (TOKENS, NE), 0.5, 4.0, ((0, 32),), jnp.float32),
        "norm_gains": jnp.clip(1.0 + 0.1 * jax.random.normal(streams_of[2], (LAYERS, 2, D), jnp.float32), 0.5, 1.5).astype(jnp.bfloat16),
        "attn_in_weight": bell_draw(streams_of[3], (LAYERS, D, 3 * D), D ** -0.5, 0.21875, ((1, 32),)),
        "attn_out_weight": bell_draw(streams_of[4], (LAYERS, D, D), HD ** -0.5, 0.75, ((1, 32),)),
        "router_weight": bell_draw(streams_of[5], (LAYERS, D, NE), 0.025, 0.14941406, ((1, 32),)),
        "const_mix": bell_draw(streams_of[6], (LAYERS, D, 4), D ** -0.5, 0.21875, ((1, 32),)),
        "const_values": bell_draw(streams_of[7], (LAYERS, 2, D), 1.0, 6.0, ((2, 32),)),
        "expert_gate": bell_draw(streams_of[8], (LAYERS, NF, D, FF), D ** -0.5, 0.21875, ((1, 4), (2, 8))),
        "expert_up": bell_draw(streams_of[9], (LAYERS, NF, D, FF), D ** -0.5, 0.21875, ((1, 4), (2, 8))),
        "expert_down": bell_draw(streams_of[10], (LAYERS, NF, D, FF), (FF // 4) ** -0.5, 0.25, ((1, 4), (2, 8))),
        "routes": picks_of(streams_of[11], LAYERS * TOKENS, NE, TOP, 1365).reshape((LAYERS, TOKENS, TOP)),
        "order": draw_order(jax.random.fold_in(streams_of[14], 71), 0),
        "cotangent": bell_draw(streams_of[13], (TOKENS, D), 1.0, 6.0, ((0, 32),)),
    }


EPSILON = 1e-05
HIGH = lax.Precision.HIGHEST
NEGATIVE = -1e+30

@jax.custom_vjp
def low(v):
    return lax.optimization_barrier(v.astype(jnp.bfloat16)).astype(jnp.float32)

@jax.custom_vjp
def low_back(v):
    return v

def low_keep(v):
    return (low(v), None)

def low_pass(kept, grad):
    return (grad,)

def back_keep(v):
    return (v, None)

def back_low(kept, grad):
    return (low(grad),)
low.defvjp(low_keep, low_pass)
low_back.defvjp(back_keep, back_low)

def rms_norm(values, gain):
    return values * lax.rsqrt(lax.optimization_barrier(jnp.mean(values * values, axis=-1, keepdims=True)) + EPSILON) * gain

def rotary_tables(positions):
    freqs = 10000.0 ** (-jnp.arange(0, HD, 2, dtype=jnp.float32) / HD)
    angles = positions[:, None] * freqs[None, :]
    return (jnp.cos(angles)[:, None, :], jnp.sin(angles)[:, None, :])

def rotate(values, cosine, sine):
    half = HD // 2
    first = values[..., :half]
    second = values[..., half:]
    return jnp.concatenate([first * cosine - second * sine, second * cosine + first * sine], axis=-1)

def attention(queries, keys, values):
    rows = min(512, LENGTH)
    blocks = LENGTH // rows
    scale = HD ** (-0.5)
    key_pos = jnp.arange(LENGTH, dtype=jnp.int32)

    def one_block(index):
        block_q = lax.dynamic_slice_in_dim(queries, index * rows, rows, 0)
        query_pos = index * rows + jnp.arange(rows, dtype=jnp.int32)
        scores = jnp.einsum('qhd,khd->hqk', block_q, keys, precision=HIGH) * scale
        scores = low_back(scores)
        mask = (key_pos[None, :] <= query_pos[:, None])[None]
        scores = jnp.where(mask, scores, NEGATIVE)
        peak = lax.optimization_barrier(jnp.max(scores, axis=-1, keepdims=True))
        weights = jnp.where(mask, jnp.exp(scores - peak), 0.0)
        weights = weights / lax.optimization_barrier(jnp.sum(weights, axis=-1, keepdims=True))
        weights = low(weights)
        return jnp.einsum('hqk,khd->qhd', weights, values, precision=HIGH)
    outputs = lax.map(jax.checkpoint(one_block), jnp.arange(blocks, dtype=jnp.int32))
    return outputs.reshape(LENGTH, HEADS, HD)

def all_sequences(queries, keys, values):
    shape = (SEQS, LENGTH, HEADS, HD)

    def one_sequence(parts):
        return attention(parts[0], parts[1], parts[2])
    outputs = lax.map(one_sequence, (queries.reshape(shape), keys.reshape(shape), values.reshape(shape)))
    return outputs.reshape(TOKENS, D)

def slot_numbers(route_ids, ranks):
    blocks = TOKENS // TOK_DEV
    flat_ids = route_ids.reshape(blocks, TOK_DEV * TOP)
    flat_rank = ranks.reshape(blocks, TOK_DEV * TOP)
    same = (flat_ids[:, :, None] == flat_ids[:, None, :]) & (flat_rank[:, None, :] < flat_rank[:, :, None])
    return lax.optimization_barrier(jnp.sum(same.astype(jnp.int32), axis=-1)).reshape(TOKENS, TOP)

def expert_out(normed_low, gate_w, up_w, down_w):
    inputs = low_back(normed_low)
    gate = low_back(jnp.dot(inputs, gate_w, precision=HIGH))
    upper = low_back(jnp.dot(inputs, up_w, precision=HIGH))
    hidden = low(jax.nn.silu(gate) * upper)
    return low(low_back(jnp.dot(hidden, down_w.T, precision=HIGH)))

def moe_layer(normed, normed_low, logits, route_ids, kept, mix_w, const_vals, gate_w, up_w, down_w):
    picks = (route_ids[:, :, None] == jnp.arange(NE, dtype=jnp.int32)).astype(jnp.float32)
    chosen = lax.optimization_barrier(jnp.sum(picks * logits[:, None, :], axis=-1))
    gates = jax.nn.softmax(chosen, axis=-1)
    mixed = jnp.zeros((TOKENS, D), jnp.float32)
    for expert in range(NF):
        weight = lax.optimization_barrier(jnp.sum(gates * kept * picks[:, :, expert], axis=-1))
        result = jax.checkpoint(expert_out)(normed_low, gate_w[expert], up_w[expert], down_w[expert])
        mixed = mixed + weight[:, None] * result
    copy_weight = lax.optimization_barrier(jnp.sum(gates * picks[:, :, NF + 1], axis=-1))
    mixed = mixed + copy_weight[:, None] * normed
    for index in range(2):
        weight = lax.optimization_barrier(jnp.sum(gates * picks[:, :, NF + 2 + index], axis=-1))
        shares = jax.nn.softmax(jnp.dot(normed, mix_w[:, 2 * index:2 * index + 2], precision=HIGH), axis=-1)
        const_out = shares[:, 0:1] * normed + shares[:, 1:2] * const_vals[index][None, :]
        mixed = mixed + weight[:, None] * const_out
    return mixed

def reference(tokens, prev_logits, norm_gains, attn_in_weight, attn_out_weight, router_weight, const_mix, const_values, expert_gate, expert_up, expert_down, routes, order, cotangent):
    kept_all = []
    for layer in range(LAYERS):
        slots = slot_numbers(routes[layer], order[layer])
        kept_all.append(((routes[layer] < NF) & (slots < CAP)).astype(jnp.float32))
    positions = (jnp.arange(TOKENS, dtype=jnp.int32) % LENGTH).astype(jnp.float32)
    cosine, sine = rotary_tables(positions)

    def forward(state, incoming, gains, in_w, out_w, router_w, mix_w, const_vals, gate_w, up_w, down_w):
        for layer in range(LAYERS):
            normed = rms_norm(state, gains[layer, 0])
            normed_low = low(normed)
            projected = low_back(jnp.dot(normed_low, in_w[layer], precision=HIGH))
            queries = rotate(projected[:, :D].reshape(TOKENS, HEADS, HD), cosine, sine)
            keys = rotate(projected[:, D:2 * D].reshape(TOKENS, HEADS, HD), cosine, sine)
            values = projected[:, 2 * D:].reshape(TOKENS, HEADS, HD)
            queries = low(low_back(queries))
            keys = low(low_back(keys))
            values = low(low_back(values))
            attended = all_sequences(queries, keys, values)
            attended = low(low_back(attended))
            branch = low_back(jnp.dot(attended, out_w[layer], precision=HIGH))
            middle = state + branch
            normed_two = rms_norm(middle, gains[layer, 1])
            normed_two_low = low(normed_two)
            logits = jnp.dot(normed_two_low, router_w[layer], precision=HIGH) + incoming
            mixed = moe_layer(normed_two, normed_two_low, logits, routes[layer], kept_all[layer], mix_w[layer], const_vals[layer], gate_w[layer], up_w[layer], down_w[layer])
            state = middle + mixed
            incoming = logits
        return state
    floats = (tokens.astype(jnp.float32), prev_logits.astype(jnp.float32), norm_gains.astype(jnp.float32), attn_in_weight.astype(jnp.float32), attn_out_weight.astype(jnp.float32), router_weight.astype(jnp.float32), const_mix.astype(jnp.float32), const_values.astype(jnp.float32), expert_gate.astype(jnp.float32), expert_up.astype(jnp.float32), expert_down.astype(jnp.float32))
    result, pullback = jax.vjp(forward, *floats)
    grads = pullback(cotangent.astype(jnp.float32))
    return (result.astype(jnp.bfloat16), grads[0], grads[1], grads[2], grads[3], grads[4], grads[5], grads[6], grads[7], grads[8], grads[9], grads[10])
```

```python
import jax
import jax.numpy as jnp
from jax import lax
from jax.experimental import pallas as pl
from jax.experimental.pallas import tpu as pltpu
from jax.sharding import PartitionSpec as P

HEADS = 12
HD = 64
NF = 8
TOP = 2
LAYERS = 2
NE = 12
CAP = 26
SLOT = 32
GROUPS = 4
EPSILON = 1e-05
NEGATIVE = -1e30
SCALE = HD ** (-0.5)
VMEM_BYTES = 60 * 1024 * 1024

BF = jnp.bfloat16
F32 = jnp.float32
MESH = pl.DeviceIdType.MESH
VMEM = pl.BlockSpec(memory_space=pltpu.VMEM)
ANY = pl.BlockSpec(memory_space=pl.ANY)


def mm(a, b, ca=1, cb=0):
    return lax.dot_general(a, b, (((ca,), (cb,)), ((), ())), preferred_element_type=F32)


def split(v):
    high = v.astype(BF)
    return high, (v - high.astype(F32)).astype(BF)


def lanes(shape):
    return lax.broadcasted_iota(jnp.int32, shape, len(shape) - 1)


def lane_of(v, index):
    return jnp.sum(jnp.where(lanes(v.shape) == index, v, 0.0), axis=-1, keepdims=True)


def rows_of(small):
    pick = lax.broadcasted_iota(jnp.int32, (8, 128), 0) + 16 == lanes((8, 128))
    return mm(pick.astype(F32).astype(BF), small, 1, 1)


def swap_halves(v):
    width = v.shape[-1]
    low_half = lanes(v.shape) % HD < HD // 2
    return jnp.where(
        low_half, pltpu.roll(v, width - HD // 2, 1), pltpu.roll(v, HD // 2, 1)
    )


def rotate(v, cosine, sine):
    return v * cosine + swap_halves(v) * sine


def rotate_back(v, cosine, sine):
    return v * cosine - swap_halves(v) * sine


def norm_grad(v, root, gain, grad):
    scaled = grad * gain
    inner = jnp.mean(v * scaled, axis=-1, keepdims=True)
    return root * scaled - v * (root * root * root * inner)


class Links:
    def __init__(self, send, recv):
        self.send, self.recv, self.used = send, recv, 0

    def copy(self, src, dst, device):
        made = pltpu.make_async_remote_copy(
            src_ref=src,
            dst_ref=dst,
            send_sem=self.send.at[self.used],
            recv_sem=self.recv.at[self.used],
            device_id=device,
            device_id_type=MESH,
        )
        self.used += 1
        return made


def greet(devices):
    barrier = pltpu.get_barrier_semaphore()
    for device in devices:
        pl.semaphore_signal(barrier, inc=1, device_id=device, device_id_type=MESH)
    pl.semaphore_wait(barrier, len(devices))


def launch(body, number, ins, in_specs, outs, out_specs, scratch, copies):
    return pl.pallas_call(
        body,
        out_shape=outs,
        in_specs=in_specs,
        out_specs=out_specs,
        scratch_shapes=list(scratch)
        + [pltpu.SemaphoreType.DMA((copies,)), pltpu.SemaphoreType.DMA((copies,))]
        + [pltpu.SemaphoreType.DMA((8,))],
        compiler_params=pltpu.CompilerParams(
            collective_id=number, has_side_effects=True, vmem_limit_bytes=VMEM_BYTES
        ),
    )(*ins)


class Shape:
    def __init__(self, nh, nb, rows, width, hidden):
        self.nh, self.nb, self.rows, self.width = nh, nb, rows, width
        self.hh, self.hl = nh // 2, 2
        self.minor = 2 if nb <= 8 else 4
        self.major = nb // self.minor
        self.splits = nb // GROUPS
        self.nq = nb // 2
        self.ffp = hidden // self.nq
        self.hidden = hidden
        self.drow = width // nb
        self.shard = width // (nh * nb)
        self.slots = 2 * nh * SLOT


def struct(shape, kind):
    return jax.ShapeDtypeStruct(shape, kind)


def weight_copies(z, h, b, parts, layer, gathered, links, local_sem):
    copies = []
    for r in range(z.nb):
        t = lax.rem(b + r, z.nb)
        e, q = t // z.nq, lax.rem(t, z.nq)
        cols = pl.ds(pl.multiple_of(q * z.ffp, 128), z.ffp)
        for w in range(3):
            src, dst = parts[w].at[layer, e, :, cols], gathered.at[w, b]
            if r == 0:
                copies.append(pltpu.make_async_copy(src, dst, local_sem.at[w]))
            else:
                copies.append(links.copy(src, dst, (h, t)))
    return copies


def grad_copies(z, h, b, grads, landed, links, local_sem):
    e, q = b // z.nq, lax.rem(b, z.nq)
    cols = pl.ds(pl.multiple_of(q * z.ffp, 128), z.ffp)
    copies = []
    for r in range(z.nb):
        t = lax.rem(b + r, z.nb)
        for w in range(3):
            src, dst = grads.at[w, t], landed.at[w, e, :, cols]
            if r == 0:
                copies.append(pltpu.make_async_copy(src, dst, local_sem.at[w]))
            else:
                copies.append(links.copy(src, dst, (h, t)))
    return copies


def place_of(z, h, b):
    return h // z.hl, lax.rem(h, z.hl), b // z.minor, lax.rem(b, z.minor)


def gather_weights(z, number, shards, expert_parts, layer):
    pieces = len(shards)
    shape = (z.hh, z.hl, z.major, z.minor)

    def body(*refs):
        own = refs[:pieces]
        parts = refs[pieces : pieces + 3]
        full = refs[pieces + 3 : 2 * pieces + 3]
        experts = refs[2 * pieces + 3]
        send, recv, local_sem, own_sem = refs[2 * pieces + 4 :]
        h, b = lax.axis_index("head"), lax.axis_index("blk")
        y, c, m, n = place_of(z, h, b)
        blk_peers = [(h, lax.rem(b + r, z.nb)) for r in range(1, z.nb)]
        core_peer = (y * z.hl + 1 - c, b)
        y_peers = [(lax.rem(y + r, z.hh) * z.hl + c, b) for r in range(1, z.hh)]
        greet(blk_peers + [core_peer] + y_peers)
        links = Links(send, recv)
        major_peers = [(h, lax.rem(m + r, z.major) * z.minor + n) for r in range(1, z.major)]
        minor_peers = [(h, m * z.minor + lax.rem(n + r, z.minor)) for r in range(1, z.minor)]
        every = slice(None)
        stages = {
            0: [
                ((y, c, m, n), major_peers),
                ((y, c, every, n), minor_peers),
                ((y, c, every, every), y_peers),
                ((every, c, every, every), [core_peer]),
            ],
            1: [
                ((y, c, m, n), major_peers),
                ((y, c, every, n), y_peers),
                ((every, c, every, n), minor_peers),
                ((every, c, every, every), [core_peer]),
            ],
        }
        keep = []
        for p in range(pieces):
            keep.append(pltpu.make_async_copy(own[p], full[p].at[y, c, m, n], own_sem.at[p]))
            keep[p].start()
        side = []
        waiting = [[] for _ in range(pieces)]
        done = []
        for stage in range(4):
            for p in range(pieces):
                for made in waiting[p]:
                    made.wait_recv()
                if stage == 1:
                    keep[p].wait()
                at, peers = stages[p % 2][stage]
                src = own[p] if stage == 0 else full[p].at[at]
                waiting[p] = [links.copy(src, full[p].at[at], peer) for peer in peers]
                for made in waiting[p]:
                    made.start()
                done += waiting[p]
            if stage == 0:
                side = weight_copies(z, h, b, parts, layer, experts, links, local_sem)
                for made in side:
                    made.start()
        for p in range(pieces):
            for made in waiting[p]:
                made.wait_recv()
        for made in done:
            made.wait_send()
        for made in side:
            made.wait()

    steps = z.major - 1 + z.minor - 1 + z.hh - 1 + 1
    return pl.pallas_call(
        body,
        out_shape=[struct(shape + s.shape, BF) for s in shards]
        + [struct((3, z.nb, z.drow, z.ffp), BF)],
        in_specs=[ANY] * (pieces + 3),
        out_specs=[ANY] * (pieces + 1),
        scratch_shapes=[
            pltpu.SemaphoreType.DMA((pieces * steps + 3 * z.nb,)),
            pltpu.SemaphoreType.DMA((pieces * steps + 3 * z.nb,)),
            pltpu.SemaphoreType.DMA((8,)),
            pltpu.SemaphoreType.DMA((8,)),
        ],
        compiler_params=pltpu.CompilerParams(
            collective_id=number, has_side_effects=True, vmem_limit_bytes=VMEM_BYTES
        ),
    )(*shards, *expert_parts)


def head_masks(first):
    where_lane = lanes((1, 256))
    return [
        ((where_lane >= first + HD * j) & (where_lane < first + HD * (j + 1))).astype(F32)
        for j in range(3)
    ]


def window(v, g, shifted):
    start = 384 * (g // 2) + 128 * (g % 2)
    cut = v[:, start : start + 256]
    if shifted:
        if g % 2 == 0:
            cut = pltpu.roll(cut, HD, 1)
        return jnp.where(lanes(cut.shape) >= HD, cut, 0.0)
    if g % 2 == 1:
        cut = pltpu.roll(cut, 256 - HD, 1)
    return jnp.where(lanes(cut.shape) < 192, cut, 0.0)


def unwindow(even, odd):
    odd = pltpu.roll(odd, HD, 1)
    return [even[:, :128], even[:, 128:] + odd[:, :128], odd[:, 128:]]


def causal(z, i, s, keys):
    rows = lax.broadcasted_iota(jnp.int32, (3 * z.rows, keys), 0) % z.rows
    cols = lanes((3 * z.rows, keys))
    return cols <= rows + (i * z.splits + s) * z.rows


def attend(z, number, state, small, w_in, w_out, tables, expert_parts, layer):
    side_on = expert_parts is not None

    def body(*refs):
        x_ref, small_ref, win_ref, wout_ref, cq, sq, ckv, skv = refs[:8]
        at = 8
        if side_on:
            parts = refs[at : at + 3]
            at += 3
        mid_ref, low_ref, q_ref, kv_ref, o_ref, lse_ref, ret_ref = refs[at : at + 7]
        at += 7
        if side_on:
            experts = refs[at]
            at += 1
        q_out, kv_out, o_out, send, recv, local_sem = refs[at:]
        h, b = lax.axis_index("head"), lax.axis_index("blk")
        g, s = b // z.splits, lax.rem(b, z.splits)
        links = Links(send, recv)
        greet([(h, lax.rem(b + r, z.nb)) for r in range(1, z.nb)])
        x = x_ref[...]
        gain = rows_of(small_ref[...])[0:1]
        root = lax.rsqrt(jnp.mean(x * x, axis=-1, keepdims=True) + EPSILON)
        low = (x * root * gain).astype(BF)
        low_ref[...] = low
        for n in range(GROUPS):
            kv = mm(low, win_ref[:, 384 * n : 384 * (n + 1)])
            kv_out[n] = rotate(kv, ckv[...], skv[...]).astype(BF)
        q = rotate(mm(low, win_ref[:, 2 * z.width :]), cq[...], sq[...])
        for n in range(GROUPS):
            q_out[n] = window(q, n, False).astype(BF)
        moved = []
        for r in range(1, z.nb):
            t = lax.rem(b + r, z.nb)
            moved.append(links.copy(kv_out.at[t // z.splits], kv_ref.at[b], (h, t)))
        for r in range(1, GROUPS):
            n = lax.rem(g + r, GROUPS)
            moved.append(links.copy(q_out.at[n], q_ref.at[g], (h, n * z.splits + s)))
        for made in moved:
            made.start()
        kv_ref[b] = kv_out[g]
        q_ref[g] = q_out[g]
        side = []
        if side_on:
            side = weight_copies(z, h, b, parts, layer, experts, links, local_sem)
            for made in side:
                made.start()
        for made in moved:
            made.wait()
        q_masks = [m.astype(BF) for m in head_masks(0)]
        v_masks = head_masks(HD)
        for i in range(GROUPS):
            blocks = (i + 1) * z.splits
            keys = blocks * z.rows
            kv = kv_ref[0:blocks].reshape(keys, 384)
            q3 = jnp.concatenate([q_ref[i] * m for m in q_masks], axis=0)
            scores = mm(q3, kv[:, 0:256], 1, 1) * SCALE
            scores = jnp.where(causal(z, i, s, keys), scores, NEGATIVE)
            peak = jnp.max(scores, axis=-1, keepdims=True)
            weights = jnp.exp(scores - peak)
            total = jnp.sum(weights, axis=-1, keepdims=True)
            out = mm(weights.astype(BF), kv[:, 128:384]) / total
            merged = sum(out[z.rows * j : z.rows * (j + 1)] * v_masks[j] for j in range(3))
            o_ref[i] = merged
            o_out[i] = pltpu.roll(merged, 256 - HD, 1).astype(BF)
            lse_ref[i] = peak + jnp.log(total)
        moved = []
        for r in range(1, GROUPS):
            n = lax.rem(g + r, GROUPS)
            moved.append(links.copy(o_out.at[n], ret_ref.at[g], (h, n * z.splits + s)))
        for made in moved:
            made.start()
        ret_ref[g] = o_out[g]
        for made in moved:
            made.wait()
        middle = x
        for n in range(GROUPS):
            middle = middle + mm(ret_ref[n, :, 0:192], wout_ref[192 * n : 192 * (n + 1), :])
        mid_ref[...] = middle
        for made in side:
            made.wait()

    outs = [
        struct((z.rows, z.width), F32),
        struct((z.rows, z.width), BF),
        struct((GROUPS, z.rows, 256), BF),
        struct((z.nb, z.rows, 384), BF),
        struct((GROUPS, z.rows, 256), F32),
        struct((GROUPS, 3 * z.rows, 1), F32),
        struct((GROUPS, z.rows, 256), BF),
    ]
    out_specs = [VMEM] * 7
    ins = [state, small, w_in, w_out, *tables]
    in_specs = [VMEM] * 8
    if side_on:
        ins += list(expert_parts)
        in_specs += [ANY] * 3
        outs.append(struct((3, z.nb, z.drow, z.ffp), BF))
        out_specs.append(ANY)
    return launch(
        body,
        number,
        ins,
        in_specs,
        outs,
        out_specs,
        [
            pltpu.VMEM((GROUPS, z.rows, 256), BF),
            pltpu.VMEM((GROUPS, z.rows, 384), BF),
            pltpu.VMEM((GROUPS, z.rows, 256), BF),
        ],
        z.nb + 2 * GROUPS + 3 * z.nb,
    )


def attend_back(z, number, grad_mid, state, low, small, w_in, w_out, tables, saved):
    chunk = min(1024, z.nb * z.rows)

    def body(*refs):
        (dm_ref, x_ref, low_ref, small_ref, win_ref, wout_ref, cq, sq, ckv, skv) = refs[:10]
        q_ref, kv_ref, o_ref, lse_ref, ret_ref = refs[10:15]
        ds_ref, gin_ref, gout_ref, gain_ref = refs[15:19]
        (do_out, do_ref, dq_out, dkv_out, dq_ref, dkv_ref, dk_sum, dv_sum) = refs[19:27]
        send, recv, _ = refs[27:]
        h, b = lax.axis_index("head"), lax.axis_index("blk")
        g, s = b // z.splits, lax.rem(b, z.splits)
        links = Links(send, recv)
        greet([(h, lax.rem(b + r, z.nb)) for r in range(1, z.nb)])
        dm = dm_ref[...]
        branch = dm.astype(BF)
        grad_att = mm(branch, wout_ref[...], 1, 1)
        for n in range(GROUPS):
            do_out[n] = window(grad_att, n, True).astype(BF)
        moved = []
        for r in range(1, GROUPS):
            n = lax.rem(g + r, GROUPS)
            moved.append(links.copy(do_out.at[n], do_ref.at[g], (h, n * z.splits + s)))
        for made in moved:
            made.start()
        do_ref[g] = do_out[g]
        per = 192 // z.shard if 192 % z.shard == 0 else 0
        for n in range(GROUPS):
            part = mm(ret_ref[n], branch, 0, 0)[0:192]
            for k in range(192 // z.shard):
                gout_ref[n * per + k] = part[k * z.shard : (k + 1) * z.shard].astype(BF)
        dk_sum[...] = jnp.zeros_like(dk_sum)
        dv_sum[...] = jnp.zeros_like(dv_sum)
        q_masks = head_masks(0)
        v_masks = head_masks(HD)
        for made in moved:
            made.wait()
        for i in range(GROUPS):
            keys_all = (i + 1) * z.splits * z.rows
            q3 = jnp.concatenate([q_ref[i] * m.astype(BF) for m in q_masks], axis=0)
            do3 = jnp.concatenate([do_ref[i] * m.astype(BF) for m in v_masks], axis=0)
            o3 = jnp.concatenate([o_ref[i]] * 3, axis=0)
            delta = jnp.sum(do3.astype(F32) * o3, axis=-1, keepdims=True)
            lse = lse_ref[i]
            dq3 = jnp.zeros((3 * z.rows, 256), F32)
            for start in range(0, keys_all, chunk):
                keys = min(chunk, keys_all - start)
                first = start // z.rows
                kv = kv_ref[first : first + keys // z.rows].reshape(keys, 384)
                key, value = kv[:, 0:256], kv[:, 128:384]
                rows = lax.broadcasted_iota(jnp.int32, (3 * z.rows, keys), 0) % z.rows
                cols = lanes((3 * z.rows, keys)) + start
                mask = cols <= rows + (i * z.splits + s) * z.rows
                scores = mm(q3, key, 1, 1) * SCALE
                weights = jnp.where(mask, jnp.exp(scores - lse), 0.0)
                grad_weights = mm(do3, value, 1, 1)
                grad_scores = (weights * (grad_weights - delta)).astype(BF)
                dq3 = dq3 + mm(grad_scores, key)
                dk_sum[start : start + keys] += mm(grad_scores, q3, 0, 0)
                dv_sum[start : start + keys] += mm(weights.astype(BF), do3, 0, 0)
            dq = sum(dq3[z.rows * j : z.rows * (j + 1)] * q_masks[j] for j in range(3))
            dq_out[i] = (dq * SCALE).astype(BF)
        for n in range(z.nb):
            dk = dk_sum[n * z.rows : (n + 1) * z.rows] * SCALE
            dv = dv_sum[n * z.rows : (n + 1) * z.rows]
            dkv_out[n, :, 0:128] = dk[:, :128].astype(BF)
            dkv_out[n, :, 128:256] = (dk[:, 128:] + dv[:, :128]).astype(BF)
            dkv_out[n, :, 256:384] = dv[:, 128:].astype(BF)
        moved = []
        for r in range(1, z.nb):
            t = lax.rem(b + r, z.nb)
            moved.append(links.copy(dkv_out.at[t], dkv_ref.at[b], (h, t)))
        for r in range(1, GROUPS):
            n = lax.rem(g + r, GROUPS)
            moved.append(links.copy(dq_out.at[n], dq_ref.at[g], (h, n * z.splits + s)))
        for made in moved:
            made.start()
        dkv_ref[b] = dkv_out[b]
        dq_ref[g] = dq_out[g]
        for made in moved:
            made.wait()
        own = low_ref[...]
        grad_low = jnp.zeros((z.rows, z.width), F32)
        shards = z.width // z.shard
        for n in range(GROUPS):
            total = dkv_ref[n * z.splits].astype(F32)
            for k in range(1, z.splits):
                total = total + dkv_ref[n * z.splits + k].astype(F32)
            piece = rotate_back(total, ckv[...], skv[...]).astype(BF)
            grad_low = grad_low + mm(piece, win_ref[:, 384 * n : 384 * (n + 1)], 1, 1)
            part = mm(own, piece, 0, 0)
            for k in range(shards):
                gin_ref[k, :, 384 * n : 384 * (n + 1)] = part[
                    k * z.shard : (k + 1) * z.shard
                ].astype(BF)
        columns = []
        for n in range(0, GROUPS, 2):
            columns += unwindow(dq_ref[n].astype(F32), dq_ref[n + 1].astype(F32))
        piece = rotate_back(jnp.concatenate(columns, axis=1), cq[...], sq[...]).astype(BF)
        grad_low = grad_low + mm(piece, win_ref[:, 2 * z.width :], 1, 1)
        part = mm(own, piece, 0, 0)
        for k in range(shards):
            gin_ref[k, :, 2 * z.width :] = part[k * z.shard : (k + 1) * z.shard].astype(BF)
        x = x_ref[...]
        gain = rows_of(small_ref[...])[0:1]
        root = lax.rsqrt(jnp.mean(x * x, axis=-1, keepdims=True) + EPSILON)
        ds_ref[...] = dm + norm_grad(x, root, gain, grad_low)
        place = (lanes((z.rows, 128)) == 16).astype(F32).astype(BF)
        high, rest = split(grad_low * x * root)
        gain_ref[...] = mm(high, place, 0, 0) + mm(rest, place, 0, 0)

    shards = z.nh * z.nb
    return launch(
        body,
        number,
        [grad_mid, state, low, small, w_in, w_out, *tables, *saved],
        [VMEM] * 15,
        [
            struct((z.rows, z.width), F32),
            struct((shards, z.shard, 3 * z.width), BF),
            struct((shards, z.shard, z.width), BF),
            struct((z.width, 128), F32),
        ],
        [VMEM] * 4,
        [
            pltpu.VMEM((GROUPS, z.rows, 256), BF),
            pltpu.VMEM((GROUPS, z.rows, 256), BF),
            pltpu.VMEM((GROUPS, z.rows, 256), BF),
            pltpu.VMEM((z.nb, z.rows, 384), BF),
            pltpu.VMEM((GROUPS, z.rows, 256), BF),
            pltpu.VMEM((z.nb, z.rows, 384), BF),
            pltpu.VMEM((z.nb * z.rows, 256), F32),
            pltpu.VMEM((z.nb * z.rows, 256), F32),
        ],
        z.nb + 2 * GROUPS,
    )


class Mixing:
    def __init__(self, z, middle, small, routes, target):
        table = rows_of(small)
        self.gain, self.consts = table[1:2], (table[2:3], table[3:4])
        self.root = lax.rsqrt(jnp.mean(middle * middle, axis=-1, keepdims=True) + EPSILON)
        self.normed = middle * self.root * self.gain
        self.low, self.rest = split(self.normed)
        self.product = mm(self.low, small)
        shares = self.product + mm(self.rest, small)
        self.shares = []
        for index in range(2):
            one, two = lane_of(shares, 12 + 2 * index), lane_of(shares, 13 + 2 * index)
            peak = jnp.maximum(one, two)
            one, two = jnp.exp(one - peak), jnp.exp(two - peak)
            self.shares.append((one / (one + two), two / (one + two)))
        self.picks = [(lanes((z.rows, 128)) == routes[:, j : j + 1]).astype(F32) for j in range(TOP)]
        self.chosen = [
            (lanes((z.rows, z.slots)) == target[:, j : j + 1]).astype(F32) for j in range(TOP)
        ]

    def gate(self, logits):
        values = [jnp.sum(p * logits, axis=-1, keepdims=True) for p in self.picks]
        peak = jnp.maximum(values[0], values[1])
        powers = [jnp.exp(v - peak) for v in values]
        total = powers[0] + powers[1]
        self.gates = [p / total for p in powers]
        self.combine = self.gates[0] * self.chosen[0] + self.gates[1] * self.chosen[1]
        spread = self.gates[0] * self.picks[0] + self.gates[1] * self.picks[1]
        self.const_weights = [lane_of(spread, NF + 2 + index) for index in range(2)]
        self.normed_weight = lane_of(spread, NF + 1)
        for index in range(2):
            self.normed_weight = (
                self.normed_weight + self.const_weights[index] * self.shares[index][0]
            )


def expert_peers(z, h, i, q):
    others = []
    for dh in range(z.nh):
        for di in range(2):
            if dh or di:
                others.append((lax.rem(h + dh, z.nh), lax.rem(i + di, 2)))
    parts = [lax.rem(q + r, z.nq) for r in range(1, z.nq)]
    return others, parts


def spread_rows(z, links, h, i, q, others, parts, rows_ref, all_ref):
    mine = 2 * h + i
    first = []
    for oh, oi in others:
        made = links.copy(rows_ref.at[2 * oh + oi], all_ref.at[q, mine], (oh, oi * z.nq + q))
        made.start()
        first.append(made)
    all_ref[q, mine] = rows_ref[mine]
    onward = [[] for _ in parts]
    sources = [(h, i)]
    for dh in range(z.nh):
        for di in range(2):
            if dh or di:
                sources.append((lax.rem(h + z.nh - dh, z.nh), lax.rem(i + 2 - di, 2)))
    for k, (sh, si) in enumerate(sources):
        if k:
            first[k - 1].wait_recv()
        place = all_ref.at[q, 2 * sh + si]
        for n, part in enumerate(parts):
            made = links.copy(place, place, (h, i * z.nq + part))
            made.start()
            onward[n].append(made)
    return first, onward


def return_rows(z, links, h, i, q, others, sum_ref, back_ref):
    mine = 2 * h + i
    made = []
    for oh, oi in others:
        made.append(links.copy(sum_ref.at[2 * oh + oi], back_ref.at[mine], (oh, oi * z.nq + q)))
        made[-1].start()
    back_ref[mine] = sum_ref[mine]
    return made


def expert_greet(z, h, i, q, others, parts):
    greet(
        [(oh, oi * z.nq + q) for oh, oi in others] + [(h, i * z.nq + part) for part in parts]
    )


def expert_copies(z):
    return 2 * (2 * z.nh - 1) + 2 * z.nh * (z.nq - 1) + z.nq


def expert_forward(z, number, middle, small, logits_in, routes, target, weights):
    count = 2 * z.nh * SLOT

    def body(*refs):
        mid_ref, small_ref, logits_ref, routes_ref, target_ref, w_ref = refs[:6]
        state_ref, next_ref, res_ref, all_ref, gate_ref, up_ref = refs[6:12]
        rows_ref, part_ref, got_ref, sum_ref, send, recv, _ = refs[12:]
        h, b = lax.axis_index("head"), lax.axis_index("blk")
        i, q = b // z.nq, lax.rem(b, z.nq)
        others, parts = expert_peers(z, h, i, q)
        links = Links(send, recv)
        expert_greet(z, h, i, q, others, parts)
        middle = mid_ref[...]
        mixing = Mixing(z, middle, small_ref[...], routes_ref[...], target_ref[...])
        select = (mixing.chosen[0] + mixing.chosen[1]).astype(BF)
        rows_ref[...] = mm(select, mixing.low, 0, 0).astype(BF).reshape(rows_ref.shape)
        first, onward = spread_rows(z, links, h, i, q, others, parts, rows_ref, all_ref)
        logits = mixing.product + logits_ref[...]
        next_ref[...] = logits
        mixing.gate(logits)
        back = []
        own = None
        for r in range(z.nq):
            part = lax.rem(q + z.nq - r, z.nq)
            if r:
                for made in onward[r - 1]:
                    made.wait_recv()
            rows = all_ref[part].reshape(count, z.width)
            gate, up = mm(rows, w_ref[0]), mm(rows, w_ref[1])
            gate_ref[part], up_ref[part] = gate, up
            hidden = (gate / (1.0 + jnp.exp(-gate)) * up).astype(BF)
            result = mm(hidden, w_ref[2], 1, 1)
            if r == 0:
                own = result
            else:
                part_ref[r - 1] = result.astype(BF)
                made = links.copy(part_ref.at[r - 1], got_ref.at[r - 1], (h, i * z.nq + part))
                made.start()
                back.append(made)
        total = own
        for r, made in enumerate(back):
            made.wait_recv()
            total = total + got_ref[r].astype(F32)
        sum_ref[...] = total.astype(BF).reshape(sum_ref.shape)
        last = return_rows(z, links, h, i, q, others, sum_ref, res_ref)
        for made in last:
            made.wait_recv()
        results = res_ref[...].reshape(count, z.width)
        high, rest = split(mixing.combine)
        mixed = mm(high, results) + mm(rest, results) + mixing.normed_weight * mixing.normed
        for index in range(2):
            weight = mixing.const_weights[index] * mixing.shares[index][1]
            mixed = mixed + weight * mixing.consts[index]
        state_ref[...] = middle + mixed
        for made in first + back + last:
            made.wait_send()
        for group in onward:
            for made in group:
                made.wait_send()

    block = (2 * z.nh, SLOT, z.width)
    return launch(
        body,
        number,
        [middle, small, logits_in, routes, target, weights],
        [VMEM] * 6,
        [
            struct((z.rows, z.width), F32),
            struct((z.rows, 128), F32),
            struct(block, BF),
            struct((z.nq,) + block, BF),
            struct((z.nq, count, z.ffp), F32),
            struct((z.nq, count, z.ffp), F32),
        ],
        [VMEM] * 6,
        [
            pltpu.VMEM(block, BF),
            pltpu.VMEM((z.nq - 1, count, z.width), BF),
            pltpu.VMEM((z.nq - 1, count, z.width), BF),
            pltpu.VMEM(block, BF),
        ],
        expert_copies(z),
    )


def expert_back(z, number, grad, middle, small, logits, grad_logits, routes, target, weights, saved, late):
    count = 2 * z.nh * SLOT
    side_on = late is not None

    def body(*refs):
        dy_ref, mid_ref, small_ref, logits_ref, dl_ref, routes_ref, target_ref, w_ref = refs[:8]
        res_ref, all_ref, gate_ref, up_ref = refs[8:12]
        at = 12
        if side_on:
            late_ref = refs[at]
            at += 1
        dm_ref, dnext_ref, gsmall_ref, gw_ref = refs[at : at + 4]
        at += 4
        if side_on:
            landed_ref = refs[at]
            at += 1
        (rows_ref, dall_ref, part_ref, got_ref, sum_ref, back_ref, hid_ref, dg_ref, du_ref) = refs[
            at : at + 9
        ]
        send, recv, local_sem = refs[at + 9 :]
        h, b = lax.axis_index("head"), lax.axis_index("blk")
        i, q = b // z.nq, lax.rem(b, z.nq)
        others, parts = expert_peers(z, h, i, q)
        links = Links(send, recv)
        if side_on:
            more = [(h, lax.rem(b + r, z.nb)) for r in range(1, z.nb)]
            far = [
                (lax.rem(h + dh, z.nh), lax.rem(i + di, 2) * z.nq + q)
                for dh in range(1, z.nh)
                for di in range(2)
            ]
            greet(more + far)
        else:
            expert_greet(z, h, i, q, others, parts)
        grad = dy_ref[...]
        mixing = Mixing(z, mid_ref[...], small_ref[...], routes_ref[...], target_ref[...])
        mixing.gate(logits_ref[...])
        high, rest = split(grad)
        weight_high, weight_rest = split(mixing.combine)
        slot_grad = mm(weight_high, high, 0, 0) + mm(weight_rest, high, 0, 0)
        slot_grad = slot_grad + mm(weight_high, rest, 0, 0)
        rows_ref[...] = slot_grad.astype(BF).reshape(rows_ref.shape)
        first, onward = spread_rows(z, links, h, i, q, others, parts, rows_ref, dall_ref)
        side = []
        if side_on:
            side = grad_copies(z, h, b, late_ref, landed_ref, links, local_sem)
            for made in side:
                made.start()
        results = res_ref[...].reshape(count, z.width)
        along = mm(high, results, 1, 1) + mm(rest, results, 1, 1)
        normed_dot = jnp.sum(grad * mixing.normed, axis=-1, keepdims=True)
        const_dots = [jnp.sum(grad * c, axis=-1, keepdims=True) for c in mixing.consts]
        gate_grads = []
        for j in range(TOP):
            value = jnp.sum(mixing.chosen[j] * along, axis=-1, keepdims=True)
            value = value + lane_of(mixing.picks[j], NF + 1) * normed_dot
            for index in range(2):
                share = mixing.shares[index]
                value = value + lane_of(mixing.picks[j], NF + 2 + index) * (
                    share[0] * normed_dot + share[1] * const_dots[index]
                )
            gate_grads.append(value)
        inner = mixing.gates[0] * gate_grads[0] + mixing.gates[1] * gate_grads[1]
        logit_grad = dl_ref[...]
        for j in range(TOP):
            logit_grad = logit_grad + mixing.picks[j] * (mixing.gates[j] * (gate_grads[j] - inner))
        dnext_ref[...] = logit_grad
        where_lane = lanes((z.rows, 128))
        column = jnp.zeros((z.rows, 128), F32)
        const_columns = jnp.zeros((z.rows, 128), F32)
        for index in range(2):
            share, weight = mixing.shares[index], mixing.const_weights[index]
            one, two = weight * normed_dot, weight * const_dots[index]
            mean = share[0] * one + share[1] * two
            column = column + jnp.where(where_lane == 12 + 2 * index, share[0] * (one - mean), 0.0)
            column = column + jnp.where(where_lane == 13 + 2 * index, share[1] * (two - mean), 0.0)
            const_columns = const_columns + jnp.where(
                where_lane == 18 + index, weight * share[1], 0.0
            )
        both_high, both_rest = split(logit_grad + column)
        small = small_ref[...]
        grad_normed = mm(both_high, small, 1, 1) + mm(both_rest, small, 1, 1)
        grad_normed = grad_normed + mixing.normed_weight * grad
        gsmall = mm(mixing.low, both_high, 0, 0) + mm(mixing.low, both_rest, 0, 0)
        gsmall = gsmall + mm(mixing.rest, column.astype(BF), 0, 0)
        const_high, const_rest = split(const_columns)
        gsmall = gsmall + mm(high, const_high, 0, 0) + mm(rest, const_high, 0, 0)
        gsmall = gsmall + mm(high, const_rest, 0, 0)
        back = []
        own = None
        for r in range(z.nq):
            part = lax.rem(q + z.nq - r, z.nq)
            if r:
                for made in onward[r - 1]:
                    made.wait_recv()
            rows = dall_ref[part].reshape(count, z.width)
            grad_hidden = mm(rows, w_ref[2])
            gate, up = gate_ref[part], up_ref[part]
            sig = 1.0 / (1.0 + jnp.exp(-gate))
            silu = gate * sig
            hid_ref[part] = (silu * up).astype(BF)
            up_low = (grad_hidden * silu).astype(BF)
            gate_low = (grad_hidden * up * (sig * (1.0 + gate * (1.0 - sig)))).astype(BF)
            du_ref[part], dg_ref[part] = up_low, gate_low
            result = mm(gate_low, w_ref[0], 1, 1) + mm(up_low, w_ref[1], 1, 1)
            if r == 0:
                own = result
            else:
                part_ref[r - 1] = result.astype(BF)
                made = links.copy(part_ref.at[r - 1], got_ref.at[r - 1], (h, i * z.nq + part))
                made.start()
                back.append(made)
        total = own
        for r, made in enumerate(back):
            made.wait_recv()
            total = total + got_ref[r].astype(F32)
        sum_ref[...] = total.astype(BF).reshape(sum_ref.shape)
        last = return_rows(z, links, h, i, q, others, sum_ref, back_ref)
        every = z.nq * count
        rows = all_ref[...].reshape(every, z.width)
        grown = dall_ref[...].reshape(every, z.width)
        gate_all = dg_ref[...].reshape(every, z.ffp)
        up_all = du_ref[...].reshape(every, z.ffp)
        hidden_all = hid_ref[...].reshape(every, z.ffp)
        for w, (one, two) in enumerate(((rows, gate_all), (rows, up_all), (grown, hidden_all))):
            made = mm(one, two, 0, 0)
            for n in range(z.nb):
                gw_ref[w, n] = made[n * z.drow : (n + 1) * z.drow].astype(BF)
        for made in last:
            made.wait_recv()
        select = (mixing.chosen[0] + mixing.chosen[1]).astype(BF)
        grad_normed = grad_normed + mm(select, back_ref[...].reshape(count, z.width))
        middle = mid_ref[...]
        dm_ref[...] = grad + norm_grad(middle, mixing.root, mixing.gain, grad_normed)
        place = (where_lane == 17).astype(F32).astype(BF)
        high, rest = split(grad_normed * middle * mixing.root)
        gsmall_ref[...] = gsmall + mm(high, place, 0, 0) + mm(rest, place, 0, 0)
        for made in first + back + last:
            made.wait_send()
        for group in onward:
            for made in group:
                made.wait_send()
        for made in side:
            made.wait()

    block = (2 * z.nh, SLOT, z.width)
    ins = [grad, middle, small, logits, grad_logits, routes, target, weights, *saved]
    in_specs = [VMEM] * 12
    outs = [
        struct((z.rows, z.width), F32),
        struct((z.rows, 128), F32),
        struct((z.width, 128), F32),
        struct((3, z.nb, z.drow, z.ffp), BF),
    ]
    out_specs = [VMEM] * 4
    if side_on:
        ins.append(late)
        in_specs.append(ANY)
        outs.append(struct((3, 2, z.drow, z.hidden), BF))
        out_specs.append(ANY)
    return launch(
        body,
        number,
        ins,
        in_specs,
        outs,
        out_specs,
        [
            pltpu.VMEM(block, BF),
            pltpu.VMEM((z.nq,) + block, BF),
            pltpu.VMEM((z.nq - 1, count, z.width), BF),
            pltpu.VMEM((z.nq - 1, count, z.width), BF),
            pltpu.VMEM(block, BF),
            pltpu.VMEM(block, BF),
            pltpu.VMEM((z.nq, count, z.ffp), BF),
            pltpu.VMEM((z.nq, count, z.ffp), BF),
            pltpu.VMEM((z.nq, count, z.ffp), BF),
        ],
        expert_copies(z) + 3 * z.nb,
    )


def reduce_weights(z, number, pieces, late):
    count = len(pieces)

    def body(*refs):
        full = refs[:count]
        late_ref = refs[count]
        outs = refs[count + 1 : 2 * count + 1]
        landed_ref = refs[2 * count + 1]
        at = 2 * count + 2
        bufs = [refs[at + 4 * p : at + 4 * p + 4] for p in range(count)]
        send, recv, local_sem = refs[at + 4 * count :]
        h, b = lax.axis_index("head"), lax.axis_index("blk")
        y, c, m, n = place_of(z, h, b)
        blk_peers = [(h, lax.rem(b + r, z.nb)) for r in range(1, z.nb)]
        core_peer = (y * z.hl + 1 - c, b)
        ys = [lax.rem(y + r, z.hh) for r in range(1, z.hh)]
        y_peers = [(t * z.hl + c, b) for t in ys]
        greet(blk_peers + [core_peer] + y_peers)
        links = Links(send, recv)
        ns = [lax.rem(n + r, z.minor) for r in range(1, z.minor)]
        ms = [lax.rem(m + r, z.major) for r in range(1, z.major)]
        minor_peers = [(h, m * z.minor + t) for t in ns]
        major_peers = [(h, t * z.minor + n) for t in ms]
        made = [[] for _ in range(count)]
        done = []
        for p in range(count):
            made[p] = [links.copy(full[p].at[:, 1 - c], bufs[p][0], core_peer)]
            made[p][0].start()
            done += made[p]
        side = grad_copies(z, h, b, late_ref, landed_ref, links, local_sem)
        for one in side:
            one.start()
        for p in range(count):
            kind = full[p].dtype
            one, two, three, four = bufs[p]
            for copy in made[p]:
                copy.wait_recv()
            for a in range(z.hh):
                for d in range(z.major):
                    one[a, d] = (
                        one[a, d].astype(F32) + full[p][a, c, d].astype(F32)
                    ).astype(kind)
            if p % 2 == 0:
                made[p] = [
                    links.copy(one.at[t], two.at[k], peer)
                    for k, (t, peer) in enumerate(zip(ys, y_peers))
                ]
            else:
                made[p] = [
                    links.copy(one.at[:, :, t], two.at[k], peer)
                    for k, (t, peer) in enumerate(zip(ns, minor_peers))
                ]
            for copy in made[p]:
                copy.start()
            done += made[p]
        for p in range(count):
            kind = full[p].dtype
            one, two, three, four = bufs[p]
            for copy in made[p]:
                copy.wait_recv()
            if p % 2 == 0:
                for d in range(z.major):
                    total = one[y, d].astype(F32)
                    for k in range(z.hh - 1):
                        total = total + two[k, d].astype(F32)
                    two[0, d] = total.astype(kind)
                made[p] = [
                    links.copy(two.at[0, :, t], three.at[k], peer)
                    for k, (t, peer) in enumerate(zip(ns, minor_peers))
                ]
            else:
                for a in range(z.hh):
                    for d in range(z.major):
                        total = one[a, d, n].astype(F32)
                        for k in range(z.minor - 1):
                            total = total + two[k, a, d].astype(F32)
                        two[0, a, d] = total.astype(kind)
                made[p] = [
                    links.copy(two.at[0, t], three.at[k], peer)
                    for k, (t, peer) in enumerate(zip(ys, y_peers))
                ]
            for copy in made[p]:
                copy.start()
            done += made[p]
        for p in range(count):
            kind = full[p].dtype
            one, two, three, four = bufs[p]
            for copy in made[p]:
                copy.wait_recv()
            for d in range(z.major):
                if p % 2 == 0:
                    total = two[0, d, n].astype(F32)
                    for k in range(z.minor - 1):
                        total = total + three[k, d].astype(F32)
                else:
                    total = two[0, y, d].astype(F32)
                    for k in range(z.hh - 1):
                        total = total + three[k, d].astype(F32)
                three[0, d] = total.astype(kind)
            made[p] = [
                links.copy(three.at[0, t], four.at[k], peer)
                for k, (t, peer) in enumerate(zip(ms, major_peers))
            ]
            for copy in made[p]:
                copy.start()
            done += made[p]
        for p in range(count):
            one, two, three, four = bufs[p]
            for copy in made[p]:
                copy.wait_recv()
            total = three[0, m].astype(F32)
            for k in range(z.major - 1):
                total = total + four[k].astype(F32)
            outs[p][...] = total
        for copy in done:
            copy.wait_send()
        for copy in side:
            copy.wait()

    scratch = []
    for p, piece in enumerate(pieces):
        block, kind = piece.shape[4:], piece.dtype
        scratch.append(pltpu.VMEM((z.hh, z.major, z.minor) + block, kind))
        if p % 2 == 0:
            scratch.append(pltpu.VMEM((z.hh - 1, z.major, z.minor) + block, kind))
            scratch.append(pltpu.VMEM((z.minor - 1, z.major) + block, kind))
        else:
            scratch.append(pltpu.VMEM((z.minor - 1, z.hh, z.major) + block, kind))
            scratch.append(pltpu.VMEM((z.hh - 1, z.major) + block, kind))
        scratch.append(pltpu.VMEM((z.major - 1,) + block, kind))
    steps = z.major - 1 + z.minor - 1 + z.hh - 1 + 1
    return launch(
        body,
        number,
        [*pieces, late],
        [VMEM] * count + [ANY],
        [struct(p.shape[4:], F32) for p in pieces] + [struct((3, 2, z.drow, z.hidden), BF)],
        [VMEM] * count + [ANY],
        scratch,
        count * steps + 3 * z.nb,
    )


def rotary(position, columns):
    lane = jnp.arange(columns, dtype=jnp.int32) % HD
    freqs = 10000.0 ** (-(2.0 * (lane % (HD // 2)).astype(F32)) / HD)
    angles = position[:, None] * freqs[None, :]
    return jnp.cos(angles), jnp.where(lane[None, :] < HD // 2, -jnp.sin(angles), jnp.sin(angles))


def slot_targets(routes, order):
    ids, ranks = routes.reshape(LAYERS, -1), order.reshape(LAYERS, -1)
    before = (ids[:, :, None] == ids[:, None, :]) & (ranks[:, None, :] < ranks[:, :, None])
    slot = jnp.sum(before.astype(jnp.int32), axis=-1)
    kept = (ids < NF) & (slot < CAP)
    return jnp.where(kept, ids * SLOT + slot, -1).reshape(routes.shape)


def to_groups(v, axis_size):
    lead, width = v.shape[:-1], axis_size
    part = width // GROUPS
    q, k, w = v[..., :width], v[..., width : 2 * width], v[..., 2 * width :]
    k = k.reshape(lead + (GROUPS, 1, part))
    w = w.reshape(lead + (GROUPS, 1, part))
    kv = jnp.concatenate([k, w], axis=-2).reshape(lead + (2 * width,))
    return jnp.concatenate([kv, q], axis=-1)


def from_groups(v, axis_size):
    lead, width = v.shape[:-1], axis_size
    part = width // GROUPS
    kv = v[..., : 2 * width].reshape(lead + (GROUPS, 2, part))
    k = kv[..., 0, :].reshape(lead + (width,))
    w = kv[..., 1, :].reshape(lead + (width,))
    return jnp.concatenate([v[..., 2 * width :], k, w], axis=-1)


def local(
    tokens,
    prev_logits,
    norm_gains,
    attn_in_weight,
    attn_out_weight,
    router_weight,
    const_mix,
    const_values,
    expert_gate,
    expert_up,
    expert_down,
    routes,
    order,
    cotangent,
):
    rows, width = tokens.shape
    z = Shape(lax.axis_size("head"), lax.axis_size("blk"), rows, width, expert_gate.shape[3])
    b = lax.axis_index("blk")
    position = (b * rows + jnp.arange(rows, dtype=jnp.int32)).astype(F32)
    cos_q, sin_q = rotary(position, width)
    flat = jnp.arange(384) < 192
    cos_kv = jnp.where(flat[None, :], cos_q[:, :384], 1.0)
    sin_kv = jnp.where(flat[None, :], sin_q[:, :384], 0.0)
    tables = (cos_q, sin_q, cos_kv, sin_kv)
    targets = slot_targets(routes, order)
    parts = (expert_gate, expert_up, expert_down)

    in_shards = to_groups(attn_in_weight, width)
    smalls = jnp.concatenate(
        [
            router_weight,
            const_mix,
            jnp.transpose(norm_gains, (0, 2, 1)),
            jnp.transpose(const_values, (0, 2, 1)),
            jnp.zeros((LAYERS, z.shard, 128 - NE - 8), BF),
        ],
        axis=-1,
    )
    shards = []
    for layer in range(LAYERS):
        shards += [in_shards[layer], attn_out_weight[layer], smalls[layer]]
    gathered = gather_weights(z, 0, shards, parts, 0)
    whole = [v.reshape(width, v.shape[-1]) for v in gathered[:-1]]
    in_weights, out_weights, small = whole[0::3], whole[1::3], whole[2::3]
    weights = [gathered[-1].reshape(3, width, z.ffp), None]

    state = tokens.astype(F32)
    logits = jnp.pad(prev_logits, ((0, 0), (0, 128 - NE)))
    saved = []
    for layer in range(LAYERS):
        ahead = parts if layer + 1 < LAYERS else None
        made = attend(
            z,
            1 + layer,
            state,
            small[layer],
            in_weights[layer],
            out_weights[layer],
            tables,
            ahead,
            layer + 1,
        )
        middle, low = made[:2]
        if ahead is not None:
            weights[layer + 1] = made[7].reshape(3, width, z.ffp)
        after = expert_forward(
            z,
            3 + layer,
            middle,
            small[layer],
            logits,
            routes[layer],
            targets[layer],
            weights[layer],
        )
        saved.append((state, low, middle, after[1], made[2:7], after[2:6]))
        state, logits = after[:2]

    grad = cotangent.astype(F32)
    grad_logits = jnp.zeros((rows, 128), F32)
    in_grads, out_grads, small_grads, expert_grads = {}, {}, {}, {}
    late = None
    for layer in reversed(range(LAYERS)):
        state_in, low, middle, layer_logits, attention, experts = saved[layer]
        made = expert_back(
            z,
            5 + layer,
            grad,
            middle,
            small[layer],
            layer_logits,
            grad_logits,
            routes[layer],
            targets[layer],
            weights[layer],
            experts,
            late,
        )
        if late is not None:
            expert_grads[layer + 1] = made[4]
        grad_mid, grad_logits, gsmall, late = made[:4]
        grad, in_grads[layer], out_grads[layer], gain = attend_back(
            z,
            7 + layer,
            grad_mid,
            state_in,
            low,
            small[layer],
            in_weights[layer],
            out_weights[layer],
            tables,
            attention,
        )
        small_grads[layer] = gsmall + gain
    grid = (z.hh, z.hl, z.major, z.minor, z.shard)
    pieces = []
    for layer in reversed(range(LAYERS)):
        pieces += [in_grads[layer], out_grads[layer], small_grads[layer]]
    pieces = [v.reshape(grid + (v.shape[-1],)) for v in pieces]
    reduced = reduce_weights(z, 9, pieces, late)
    expert_grads[0] = reduced[-1]
    in_sum = jnp.stack([reduced[3], reduced[0]])
    out_sum = jnp.stack([reduced[4], reduced[1]])
    small_sum = jnp.stack([reduced[5], reduced[2]])
    expert_out = [
        jnp.stack([expert_grads[layer][w] for layer in range(LAYERS)]).astype(F32)
        for w in range(3)
    ]
    return (
        state.astype(BF),
        grad,
        grad_logits[:, :NE],
        jnp.transpose(small_sum[:, :, 16:18], (0, 2, 1)),
        from_groups(in_sum, width),
        out_sum,
        small_sum[:, :, :NE],
        small_sum[:, :, NE : NE + 4],
        jnp.transpose(small_sum[:, :, 18:20], (0, 2, 1)),
        expert_out[0],
        expert_out[1],
        expert_out[2],
    )


def solution(mesh):
    placed = (
        P(("head", "blk"), None),
        P(("head", "blk"), None),
        P(None, None, ("head", "blk")),
        P(None, ("head", "blk"), None),
        P(None, ("head", "blk"), None),
        P(None, ("head", "blk"), None),
        P(None, ("head", "blk"), None),
        P(None, None, ("head", "blk")),
        P(None, "head", "blk", None),
        P(None, "head", "blk", None),
        P(None, "head", "blk", None),
        P(None, ("head", "blk"), None),
        P(None, ("head", "blk"), None),
        P(("head", "blk"), None),
    )
    return jax.shard_map(
        local,
        mesh=mesh,
        in_specs=placed,
        out_specs=(
            P(("head", "blk"), None),
            P(("head", "blk"), None),
            P(("head", "blk"), None),
            P(None, None, ("head", "blk")),
            P(None, ("head", "blk"), None),
            P(None, ("head", "blk"), None),
            P(None, ("head", "blk"), None),
            P(None, ("head", "blk"), None),
            P(None, None, ("head", "blk")),
            P(None, "head", "blk", None),
            P(None, "head", "blk", None),
            P(None, "head", "blk", None),
        ),
        check_vma=False,
    )
```

```python
import jax
import jax.numpy as jnp
import numpy as np
from jax import lax
from jax.experimental import pallas as pl
from jax.experimental.pallas import tpu as pltpu
from jax.sharding import PartitionSpec as P

HEADS = 12
HD = 64
NF = 8
TOP = 2
LAYERS = 2
NE = 12
CAP = 26
SLOT = 32
GROUPS = 4
EPSILON = 1e-05
NEGATIVE = -1e30
SCALE = HD ** (-0.5)
VMEM_BYTES = 65200 * 1024

BF = jnp.bfloat16
F32 = jnp.float32
MESH = pl.DeviceIdType.MESH
VMEM = pl.BlockSpec(memory_space=pltpu.VMEM)
ANY = pl.BlockSpec(memory_space=pl.ANY)


def mm(a, b, ca=1, cb=0):
    return lax.dot_general(a, b, (((ca,), (cb,)), ((), ())), preferred_element_type=F32)


def split(v):
    high = v.astype(BF)
    return high, (v - high.astype(F32)).astype(BF)


def lanes(shape):
    return lax.broadcasted_iota(jnp.int32, shape, len(shape) - 1)


def lane_of(v, index):
    return jnp.sum(jnp.where(lanes(v.shape) == index, v, 0.0), axis=-1, keepdims=True)


def rows_of(small):
    pick = lax.broadcasted_iota(jnp.int32, (8, 128), 0) + 16 == lanes((8, 128))
    return mm(pick.astype(F32).astype(BF), small, 1, 1)


def swap_halves(v):
    width = v.shape[-1]
    low_half = lanes(v.shape) % HD < HD // 2
    return jnp.where(
        low_half, pltpu.roll(v, width - HD // 2, 1), pltpu.roll(v, HD // 2, 1)
    )


def rotate(v, cosine, sine):
    return v * cosine + swap_halves(v) * sine


def rotate_back(v, cosine, sine):
    return v * cosine - swap_halves(v) * sine


def norm_grad(v, root, gain, grad):
    scaled = grad * gain
    inner = jnp.mean(v * scaled, axis=-1, keepdims=True)
    return root * scaled - v * (root * root * root * inner)


class Shape:
    def __init__(self, nh, nb, rows, width, hidden):
        self.nh, self.nb, self.rows, self.width, self.hidden = nh, nb, rows, width, hidden
        self.hh = nh // 2
        self.splits = nb // GROUPS
        self.nq = 2 * self.splits
        self.experts = self.hh * GROUPS
        self.ffp = hidden // self.nq
        self.drow = width // nb
        self.shards = nh * nb
        self.shard = width // self.shards
        self.count = self.experts * SLOT


class Links:
    def __init__(self, z, send, recv):
        self.z, self.send, self.recv, self.used = z, send, recv, 0
        self.sent, self.sent_if = [], []
        h, b = lax.axis_index("head"), lax.axis_index("blk")
        self.h, self.b = h, b
        self.y, self.c = h // 2, lax.rem(h, 2)
        self.g, self.s = b // z.splits, lax.rem(b, z.splits)
        self.q = self.c * z.splits + self.s

    def device(self, y, c, g, s):
        return (y * 2 + c, g * self.z.splits + s)

    def near(self, dy=0, dc=0, dg=0, ds=0):
        z = self.z
        return self.device(
            lax.rem(self.y + dy, z.hh),
            lax.rem(self.c + dc, 2),
            lax.rem(self.g + dg, GROUPS),
            lax.rem(self.s + ds, z.splits),
        )

    def beside(self):
        low = lax.rem(self.g, 2)
        return self.device(self.y, self.c, self.g + 1 - 2 * low, self.s)

    def up(self, value, step, size):
        return lax.rem(value + step, size)

    def down(self, value, step, size):
        return lax.rem(value + size - step, size)

    def take(self, amount):
        first = self.used
        self.used += amount
        return first

    def remote(self, src, dst, device, send, recv):
        return pltpu.make_async_remote_copy(
            src_ref=src,
            dst_ref=dst,
            send_sem=self.send.at[send],
            recv_sem=self.recv.at[recv],
            device_id=device,
            device_id_type=MESH,
        )

    def push(self, src, dst, device):
        place = self.take(1)
        made = self.remote(src, dst, device, place, place)
        made.start()
        self.sent.append(made)
        return made

    def push_or_keep(self, src, dst, device, here, send, recv):
        made = self.remote(src, dst, device, send, recv)

        @pl.when(jnp.logical_not(here))
        def _():
            made.start()

        @pl.when(here)
        def _():
            pltpu.make_async_copy(src, dst, self.recv.at[recv]).start()

        self.sent_if.append((here, made))

    def arrived(self, place, recv):
        pltpu.make_async_copy(place, place, self.recv.at[recv]).wait()

    def settle(self):
        for made in self.sent:
            made.wait_send()
        for here, made in self.sent_if:

            @pl.when(jnp.logical_not(here))
            def _(made=made):
                made.wait_send()

        self.sent, self.sent_if = [], []


def greet(devices):
    barrier = pltpu.get_barrier_semaphore()
    for device in devices:
        pl.semaphore_signal(barrier, inc=1, device_id=device, device_id_type=MESH)
    pl.semaphore_wait(barrier, len(devices))


def greet_all(net):
    z = net.z
    known = [net.near(dg=dg, ds=ds) for dg in range(GROUPS) for ds in range(z.splits) if dg or ds]
    known += [
        net.near(dc=1, dg=dg, ds=ds) for dg in range(GROUPS) for ds in range(z.splits)
    ]
    known += [
        net.near(dy=dy, dg=dg) for dy in range(1, z.hh) for dg in range(GROUPS)
    ]
    greet(known)


class Names:
    def __init__(self, **more):
        self.__dict__.update(more)


class Beside:
    start = sent = mid = out = rows = side = last = ()
    rows_back = side_back = last_back = back_sent = back_out = ()
    back = {}

    def __init__(self, **more):
        self.__dict__.update(more)


def act(functions):
    for function in functions:
        function()


def launch(body, number, z, ins, outs, scratch, copies, same=()):
    names = list(ins) + list(outs) + list(scratch) + ["send", "recv"]

    def kernel(*refs):
        held = Names(**dict(zip(names, refs)))
        net = Links(z, held.send, held.recv)
        greet_all(net)
        body(held, net)
        net.settle()
        assert net.used <= copies, net.used

    made = pl.pallas_call(
        kernel,
        out_shape=[v[0] for v in outs.values()],
        in_specs=[v[1] for v in ins.values()],
        out_specs=[v[1] for v in outs.values()],
        scratch_shapes=list(scratch.values())
        + [pltpu.SemaphoreType.DMA((copies,)), pltpu.SemaphoreType.DMA((copies,))],
        input_output_aliases={list(ins).index(i): list(outs).index(o) for i, o in same},
        compiler_params=pltpu.CompilerParams(
            collective_id=number, has_side_effects=True, vmem_limit_bytes=VMEM_BYTES
        ),
    )(*[v[0] for v in ins.values()])
    return Names(**dict(zip(outs, made)))


def struct(shape, kind):
    return jax.ShapeDtypeStruct(shape, kind)


class NearWeights:
    def __init__(self, net, part, layer, landed):
        self.net, self.part, self.layer, self.landed = net, part, layer, landed
        self.first = net.take(GROUPS)

    def start(self):
        net = self.net
        for dc in range(2):
            for dl in range(2):
                device, src = weight_source(net, self.part, self.layer, dc, 0, dl)
                dst, place, at = self.landed.at[net.g], self.first + 2 * dc + dl, self.first + net.g
                if dc or dl:
                    made = net.remote(src, dst, device, place, at)
                    made.start()
                    net.sent.append(made)
                else:
                    net.push_or_keep(src, dst, device, net.g // 2 == net.c, place, at)

    def wait(self):
        for n in range(GROUPS):
            self.net.arrived(self.landed.at[n], self.first + n)


class FarWeights:
    def __init__(self, net, part, layer, near, landed):
        self.net, self.part, self.layer, self.landed = net, part, layer, landed
        self.first = net.take(net.z.nb)
        for n in range(GROUPS):
            at = n * net.z.splits + net.s
            pltpu.make_async_copy(near.at[n], landed.at[at], net.recv.at[self.first + at]).start()

    def start(self):
        net, z = self.net, self.net.z
        place = self.first
        for ds in range(1, z.splits):
            for dc in range(2):
                for dl in range(2):
                    device, src = weight_source(net, self.part, self.layer, dc, ds, dl)
                    dst = self.landed.at[net.b]
                    made = net.remote(src, dst, device, place, self.first + net.b)
                    made.start()
                    net.sent.append(made)
                    place += 1

    def wait(self):
        for n in range(self.net.z.nb):
            self.net.arrived(self.landed.at[n], self.first + n)


def weight_source(net, part, layer, dc, ds, dl):
    z = net.z
    e = lax.rem(net.g + dl, 2)
    c, s = net.up(net.c, dc, 2), net.up(net.s, ds, z.splits)
    cols = pl.ds(pl.multiple_of((c * z.splits + s) * z.ffp, 128), z.ffp)
    return net.device(net.y, c, 2 * net.c + e, s), part.at[layer, e, :, cols]


class GradMove:
    def __init__(self, net, grads, landed):
        self.net, self.grads, self.landed = net, grads, landed
        self.first = net.take(net.z.nb)

    def near(self):
        self.start([r for r in range(self.net.z.nb) if r % self.net.z.splits == 0])

    def far(self):
        self.start([r for r in range(self.net.z.nb) if r % self.net.z.splits])

    def start(self, steps):
        net, z = self.net, self.net.z
        e = lax.rem(net.g, 2)
        cols = pl.ds(pl.multiple_of(net.q * z.ffp, 128), z.ffp)
        at = self.first + e * z.nq + net.q
        for r in steps:
            t = net.up(net.b, r, z.nb)
            src, dst = self.grads.at[t], self.landed.at[e, :, cols]
            device = (net.y * 2 + net.g // 2, t)
            if r:
                made = net.remote(src, dst, device, self.first + r, at)
                made.start()
                net.sent.append(made)
            else:
                net.push_or_keep(src, dst, device, net.g // 2 == net.c, self.first, at)

    def wait(self, shares=(True, True)):
        net, z = self.net, self.net.z
        for e in range(2):
            for c in range(2):
                for ds in range(z.splits):
                    if shares[1 if ds else 0]:
                        n = c * z.splits + net.up(net.s, ds, z.splits)
                        cols = pl.ds(pl.multiple_of(n * z.ffp, 128), z.ffp)
                        net.arrived(self.landed.at[e, :, cols], self.first + e * z.nq + n)


def cuts_of(names, widths, size):
    return [
        (name, at, min(size, width - at))
        for name, width in zip(names, widths)
        for at in range(0, width, size)
    ]


class Gather:
    STEPS = 6

    def __init__(self, net, pieces, own_sems):
        self.net, self.pieces, self.stage = net, pieces, 0
        at = (net.y, net.c, net.g // 2, lax.rem(net.g, 2), net.s)
        self.keep = []
        for p in range(len(pieces)):
            self.keep.append(
                pltpu.make_async_copy(self.own(p), self.full(p, at), own_sems.at[p])
            )
            self.keep[-1].start()
        self.waiting = [[] for _ in pieces]

    def own(self, p):
        ref, _, first, columns = self.pieces[p]
        return ref.at[:, first : first + columns]

    def full(self, p, at):
        _, ref, first, columns = self.pieces[p]
        return ref.at[at + (slice(None), slice(first, first + columns))]

    def step(self):
        net, z, every = self.net, self.net.z, slice(None)
        y, c, s = net.y, net.c, net.s
        high, low = net.g // 2, lax.rem(net.g, 2)
        splits = [net.near(ds=d) for d in range(1, z.splits)]
        ys = [net.near(dy=d) for d in range(1, z.hh)]
        by_split = [((y, c, every, every, s), splits), ((y, c, every, every, every), ys)]
        by_y = [((y, c, every, every, s), ys), ((every, c, every, every, s), splits)]
        for p in range(len(self.pieces)):
            for made in self.waiting[p]:
                made.wait_recv()
            self.waiting[p] = []
            if self.stage == 1:
                self.keep[p].wait()
            if self.stage == 5:
                continue
            if self.stage == 0:
                at, peers = (y, c, high, low, s), [net.near(dg=2)]
            elif self.stage == 1:
                at, peers = (y, c, every, low, s), [net.beside()]
            elif self.stage == 4:
                at, peers = (every, c, every, every, every), [net.near(dc=1)]
            else:
                at, peers = (by_y if p % 2 else by_split)[self.stage - 2]
            place = self.full(p, at)
            src = self.own(p) if self.stage == 0 else place
            self.waiting[p] = [net.push(src, place, peer) for peer in peers]
        self.stage += 1


class Reduce:
    STEPS = 6

    def __init__(self, net, pieces, bufs, sems):
        self.net, self.pieces, self.bufs, self.stage = net, pieces, bufs, 0
        self.waiting = [[] for _ in pieces]
        self.mine = []
        for p, (full, _, lo, columns) in enumerate(pieces):
            own = full.at[:, net.c, :, :, :, :, slice(lo, lo + columns)]
            self.mine.append(pltpu.make_async_copy(own, bufs[p][5], sems.at[p]))

    def step(self):
        net, z = self.net, self.net.z
        y, c, s = net.y, net.c, net.s
        high, low = net.g // 2, lax.rem(net.g, 2)
        to_y = [(net.up(y, d, z.hh), net.near(dy=d)) for d in range(1, z.hh)]
        to_split = [(net.up(s, d, z.splits), net.near(ds=d)) for d in range(1, z.splits)]
        bits = [(i, j) for i in range(2) for j in range(2)]
        for p, (full, out, lo, columns) in enumerate(self.pieces):
            cut = slice(lo, lo + columns)
            one, two, three, four, five, own = self.bufs[p]
            kind = full.dtype
            for made in self.waiting[p]:
                made.wait_recv()
            moves = []
            split_first = p % 2 == 1
            firsts, seconds = (to_split, to_y) if split_first else (to_y, to_split)
            if self.stage == 0:
                moves = [(full.at[:, 1 - c, :, :, :, :, cut], one, net.near(dc=1))]
                self.mine[p].start()
            elif self.stage == 1:
                self.mine[p].wait()
                for a in range(z.hh):
                    for i, j in bits:
                        total = one[a, i, j].astype(F32) + own[a, i, j].astype(F32)
                        one[a, i, j] = total.astype(kind)
                for k, (t, peer) in enumerate(firsts):
                    moves.append((one.at[:, :, :, t] if split_first else one.at[t], two.at[k], peer))
            elif self.stage == 2:
                for i, j in bits:
                    for a in range(z.hh) if split_first else (0,):
                        at = (a, i, j) if split_first else (i, j)
                        total = (one[a, i, j, s] if split_first else one[y, i, j]).astype(F32)
                        for k in range(len(firsts)):
                            total = total + two[(k,) + at].astype(F32)
                        two[(0,) + at] = total.astype(kind)
                for k, (t, peer) in enumerate(seconds):
                    moves.append((two.at[0, t] if split_first else two.at[0, :, :, t], three.at[k], peer))
            elif self.stage == 3:
                for i, j in bits:
                    total = (two[0, y, i, j] if split_first else two[0, i, j, s]).astype(F32)
                    for k in range(len(seconds)):
                        total = total + three[k, i, j].astype(F32)
                    three[0, i, j] = total.astype(kind)
                moves = [(three.at[0, :, 1 - low], four, net.beside())]
            elif self.stage == 4:
                for i in range(2):
                    four[i] = (three[0, i, low].astype(F32) + four[i].astype(F32)).astype(kind)
                moves = [(four.at[1 - high], five, net.near(dg=2))]
            else:
                out[:, cut] = four[high].astype(F32) + five[...].astype(F32)
            self.waiting[p] = [net.push(*move) for move in moves]
        self.stage += 1


def reduce_buffers(z, columns_kinds):
    made = {}
    for p, (columns, kind) in enumerate(columns_kinds):
        block = (z.shard, columns)
        made[f"r{p}a"] = pltpu.VMEM((z.hh, 2, 2, z.splits) + block, kind)
        if p % 2 == 0:
            made[f"r{p}b"] = pltpu.VMEM((z.hh - 1, 2, 2, z.splits) + block, kind)
            made[f"r{p}c"] = pltpu.VMEM((z.splits - 1, 2, 2) + block, kind)
        else:
            made[f"r{p}b"] = pltpu.VMEM((z.splits - 1, z.hh, 2, 2) + block, kind)
            made[f"r{p}c"] = pltpu.VMEM((z.hh - 1, 2, 2) + block, kind)
        made[f"r{p}d"] = pltpu.VMEM((2,) + block, kind)
        made[f"r{p}e"] = pltpu.VMEM(block, kind)
        made[f"r{p}f"] = pltpu.VMEM((z.hh, 2, 2, z.splits) + block, kind)
    return made


def buffers_of(held, pieces):
    return [[getattr(held, f"r{p}{k}") for k in "abcdef"] for p in range(pieces)]


def head_masks(first):
    where_lane = lanes((1, 256))
    return [
        ((where_lane >= first + HD * j) & (where_lane < first + HD * (j + 1))).astype(F32)
        for j in range(3)
    ]


def window(v, g, shifted):
    start = 384 * (g // 2) + 128 * (g % 2)
    cut = v[:, start : start + 256]
    if shifted:
        if g % 2 == 0:
            cut = pltpu.roll(cut, HD, 1)
        return jnp.where(lanes(cut.shape) >= HD, cut, 0.0)
    if g % 2 == 1:
        cut = pltpu.roll(cut, 256 - HD, 1)
    return jnp.where(lanes(cut.shape) < 192, cut, 0.0)


def pack(v):
    half = v.shape[0] // 2
    last = v[:half, 128:] + pltpu.roll(v[half:, 128:], HD, 1)
    return v[:, :128].astype(BF), last.astype(BF)


def put_packed(ref, v):
    upper, last = pack(v)
    rows = v.shape[0]
    ref[:rows], ref[rows:] = upper, last


def unpack(packed):
    rows = packed.shape[0] * 2 // 3
    last = packed[rows:].astype(F32)
    keep = lanes(last.shape) < HD
    lower = jnp.concatenate(
        [jnp.where(keep, last, 0.0), jnp.where(keep, pltpu.roll(last, HD, 1), 0.0)], axis=0
    )
    return jnp.concatenate([packed[:rows].astype(F32), lower], axis=1)


def unwindow(even, odd):
    odd = pltpu.roll(odd, HD, 1)
    return [even[:, :128], even[:, 128:] + odd[:, :128], odd[:, 128:]]


def joined(key, value):
    return [key[:, :128], key[:, 128:] + value[:, :128], value[:, 128:]]


def places(net, first, last):
    z = net.z
    row = lax.broadcasted_iota(jnp.int32, ((last - first) * 3 * z.rows, 1), 0)
    block = first + row // (3 * z.rows)
    return (block * z.splits + net.s) * z.rows + row % z.rows


def attend(net, a, x, at):
    z = net.z
    act(at.start)
    gain = rows_of(a.small[...])[0:1]
    root = lax.rsqrt(jnp.mean(x * x, axis=-1, keepdims=True) + EPSILON)
    low = (x * root * gain).astype(BF)
    a.low[...] = low
    k = rotate(mm(low, a.w_in[:, z.width : 2 * z.width]), a.cq[...], a.sq[...])
    v = mm(low, a.w_in[:, 2 * z.width :])
    for n in range(GROUPS):
        for j, part in enumerate(joined(window(k, n, False), window(v, n, True))):
            a.kv_out[n, :, 128 * j : 128 * (j + 1)] = part.astype(BF)
    far = {}
    for dg in (2, 1, 3):
        t = net.up(net.g, dg, GROUPS)
        far[dg] = net.push(a.kv_out.at[t], a.kv.at[net.b], net.near(dg=dg))
    a.kv[net.b] = a.kv_out[net.g]
    q = rotate(mm(low, a.w_in[:, : z.width]), a.cq[...], a.sq[...])
    for n in range(GROUPS):
        put_packed(a.q_out.at[n], window(q, n, False))
    moved = []
    for dg in (2, 1, 3):
        t = net.up(net.g, dg, GROUPS)
        moved.append(net.push(a.q_out.at[t], a.q.at[net.g], net.near(dg=dg)))
    a.q[net.g] = a.q_out[net.g]
    act(at.sent)
    for dg in (0, 1, 3, 2):
        if dg:
            far[dg].wait_recv()
        place = a.kv.at[net.down(net.g, dg, GROUPS) * z.splits + net.s]
        for ds in range(1, z.splits):
            moved.append(net.push(place, place, net.near(ds=ds)))
    for made in moved:
        made.wait_recv()
    act(at.mid)
    q_masks = [m.astype(BF) for m in head_masks(0)]
    v_masks = head_masks(HD)
    first = net.take(GROUPS)
    chunk = z.nb * z.rows if z.nb * z.rows <= 1024 else 512
    for i in range(GROUPS):
        own = unpack(a.q[i]).astype(BF)
        q3 = jnp.concatenate([own * m for m in q_masks], axis=0)
        row = places(net, i, i + 1)
        peak = total = out = None
        for start in range(0, (i + 1) * z.splits * z.rows, chunk):
            keys = min(chunk, (i + 1) * z.splits * z.rows - start)
            kv = a.kv[start // z.rows : (start + keys) // z.rows].reshape(keys, 384)
            mask = lanes((1, keys)) + start <= row
            scores = jnp.where(mask, mm(q3, kv[:, 0:256], 1, 1) * SCALE, NEGATIVE)
            top = jnp.max(scores, axis=-1, keepdims=True)
            top = top if peak is None else jnp.maximum(top, peak)
            weights = jnp.exp(scores - top)
            more = jnp.sum(weights, axis=-1, keepdims=True)
            product = mm(weights.astype(BF), kv[:, 128:384])
            if peak is None:
                total, out = more, product
            else:
                factor = jnp.exp(peak - top)
                total, out = total * factor + more, out * factor + product
            peak = top
        out = out / total
        merged = sum(out[z.rows * j : z.rows * (j + 1)] * v_masks[j] for j in range(3))
        a.o[i] = merged
        put_packed(a.o_out.at[i], pltpu.roll(merged, 256 - HD, 1))
        a.lse[i] = peak + jnp.log(total)
        device = net.device(net.y, net.c, i, net.s)
        net.push_or_keep(
            a.o_out.at[i], a.ret.at[net.g], device, net.g == i, first + i, first + net.g
        )
    act(at.out)
    middle = x
    for n in range(GROUPS):
        net.arrived(a.ret.at[n], first + n)
        got = unpack(a.ret[n]).astype(BF)
        middle = middle + mm(got[:, 0:192], a.w_out[192 * n : 192 * (n + 1), :])
    a.middle[...] = middle
    return middle


def attend_back(net, a, x, dm, at):
    z = net.z
    branch = dm.astype(BF)
    grad_att = mm(branch, a.w_out[...], 1, 1)
    for n in range(GROUPS):
        put_packed(a.do_out.at[n], window(grad_att, n, False))
    moved = []
    for dg in (2, 1, 3):
        t = net.up(net.g, dg, GROUPS)
        moved.append(net.push(a.do_out.at[t], a.do.at[net.g], net.near(dg=dg)))
    a.do[net.g] = a.do_out[net.g]
    act(at.back_sent)
    per = 192 // z.shard
    for n in range(GROUPS):
        part = mm(unpack(a.ret[n]).astype(BF), branch, 0, 0)[0:192]
        for k in range(per):
            a.gout[n * per + k] = part[k * z.shard : (k + 1) * z.shard].astype(BF)
    q_masks = head_masks(0)
    v_masks = head_masks(HD)
    for i in range(GROUPS):
        own = unpack(a.q[i]).astype(BF)
        for j in range(3):
            a.q3[i, z.rows * j : z.rows * (j + 1)] = own * q_masks[j].astype(BF)
    a.dq_sum[...] = jnp.zeros(a.dq_sum.shape, F32)
    for made in moved:
        made.wait_recv()
    for i in range(GROUPS):
        own = pltpu.roll(unpack(a.do[i]), HD, 1)
        product = own * a.o[i]
        for j in range(3):
            span = slice(z.rows * j, z.rows * (j + 1))
            a.do3[i, span] = (own * v_masks[j]).astype(BF)
            a.delta[i, span] = jnp.sum(product * v_masks[j], axis=-1, keepdims=True)
    first_q, first_kv = net.take(GROUPS), net.take(GROUPS)
    between = {}
    size = 3 * z.rows

    def onward(i):
        total = a.dkv_out[i * z.splits + net.s].astype(F32)
        for ds, made in between[i]:
            made.wait_recv()
            total = total + a.dkv_got[ds - 1, i].astype(F32)
        a.dkv_sum[i] = total.astype(BF)
        device = net.device(net.y, net.c, i, net.s)
        net.push_or_keep(
            a.dkv_sum.at[i], a.dkv.at[net.g], device, net.g == i, first_kv + i, first_kv + net.g
        )

    some = min(4, z.splits)
    keys = some * z.rows
    for n in range(GROUPS):
        spans = [(n, GROUPS)] if keys <= 256 else [(i, i + 1) for i in range(n, GROUPS)]
        for block in range(n * z.splits, (n + 1) * z.splits, some):
            kv = a.kv[block : block + some].reshape(keys, 384)
            key, value = kv[:, 0:256], kv[:, 128:384]
            dk = jnp.zeros((keys, 256), F32)
            dv = jnp.zeros((keys, 256), F32)
            for lo, hi in spans:
                rows = (hi - lo) * size
                q3 = a.q3[lo:hi].reshape(rows, 256)
                do3 = a.do3[lo:hi].reshape(rows, 256)
                lse = a.lse[lo:hi].reshape(rows, 1)
                delta = a.delta[lo:hi].reshape(rows, 1)
                mask = lanes((1, keys)) + block * z.rows <= places(net, lo, hi)
                scores = mm(q3, key, 1, 1) * SCALE
                weights = jnp.where(mask, jnp.exp(scores - lse), 0.0)
                grad_scores = (weights * (mm(do3, value, 1, 1) - delta)).astype(BF)
                more = mm(grad_scores, key).reshape((hi - lo) * 3, z.rows, 256)
                for i in range(lo, hi):
                    at_i = 3 * (i - lo)
                    a.dq_sum[i] += sum(more[at_i + j] * q_masks[j] for j in range(3))
                dk = dk + mm(grad_scores, q3, 0, 0)
                dv = dv + mm(weights.astype(BF), do3, 0, 0)
            for j, part in enumerate(joined(dk * SCALE, dv)):
                a.dkv_out[block : block + some, :, 128 * j : 128 * (j + 1)] = part.astype(
                    BF
                ).reshape(some, z.rows, 128)
        between[n] = []
        for ds in range(1, z.splits):
            t = net.up(net.s, ds, z.splits)
            made = net.push(a.dkv_out.at[n * z.splits + t], a.dkv_got.at[ds - 1, n], net.near(ds=ds))
            between[n].append((ds, made))
        put_packed(a.dq_out.at[n], a.dq_sum[n] * SCALE)
        device = net.device(net.y, net.c, n, net.s)
        net.push_or_keep(
            a.dq_out.at[n], a.dq.at[net.g], device, net.g == n, first_q + n, first_q + net.g
        )
        if n:
            onward(n - 1)
        act(at.back.get(n, ()))
    onward(GROUPS - 1)
    act(at.back_out)
    own = a.low[...]
    grad_low = jnp.zeros((z.rows, z.width), F32)
    from_zero = lanes((1, 256)) < 192

    leaving = []

    def weigh(piece, start):
        slot = len(leaving) % 2
        if len(leaving) >= 2:
            leaving[-2].wait()
        part = mm(own, piece, 0, 0)
        for k in range(z.shards):
            a.gin_part[slot, k] = part[k * z.shard : (k + 1) * z.shard].astype(BF)
        place = a.gin.at[:, :, start : start + 384]
        leaving.append(pltpu.make_async_copy(a.gin_part.at[slot], place, a.gin_sem.at[slot]))
        leaving[-1].start()
        return mm(piece, a.w_in[:, start : start + 384], 1, 1)

    def turned(columns, n):
        cut = slice(192 * n, 192 * n + 384)
        return rotate_back(jnp.concatenate(columns, axis=1), a.cq[:, cut], a.sq[:, cut]).astype(BF)

    for n in range(0, GROUPS, 2):
        net.arrived(a.dq.at[n], first_q + n)
        net.arrived(a.dq.at[n + 1], first_q + n + 1)
        columns = unwindow(unpack(a.dq[n]), unpack(a.dq[n + 1]))
        grad_low = grad_low + weigh(turned(columns, n), 192 * n)
    for n in range(0, GROUPS, 2):
        pair = []
        for m in (n, n + 1):
            net.arrived(a.dkv.at[m], first_kv + m)
            both = a.dkv[m].astype(F32)
            key = jnp.where(from_zero, both[:, :256], 0.0)
            value = jnp.where(from_zero, pltpu.roll(both[:, 128:], 256 - HD, 1), 0.0)
            pair.append((key, value))
        columns = unwindow(pair[0][0], pair[1][0])
        grad_low = grad_low + weigh(turned(columns, n), z.width + 192 * n)
        columns = unwindow(pair[0][1], pair[1][1])
        piece = jnp.concatenate(columns, axis=1).astype(BF)
        grad_low = grad_low + weigh(piece, 2 * z.width + 192 * n)
    for copy in leaving[-2:]:
        copy.wait()
    gain = rows_of(a.small[...])[0:1]
    root = lax.rsqrt(jnp.mean(x * x, axis=-1, keepdims=True) + EPSILON)
    place = (lanes((z.rows, 128)) == 16).astype(F32).astype(BF)
    high, rest = split(grad_low * x * root)
    a.gsmall[...] += mm(high, place, 0, 0) + mm(rest, place, 0, 0)
    return dm + norm_grad(x, root, gain, grad_low)


class Mixing:
    def __init__(self, z, middle, small, plan):
        table = rows_of(small)
        self.gain, self.consts = table[1:2], (table[2:3], table[3:4])
        self.root = lax.rsqrt(jnp.mean(middle * middle, axis=-1, keepdims=True) + EPSILON)
        self.normed = middle * self.root * self.gain
        self.low, self.rest = split(self.normed)
        expert_of, slot_of = lanes((z.rows, 128)).astype(F32), lanes((z.rows, z.count)).astype(F32)
        self.picks = [(expert_of == plan[:, j : j + 1]).astype(F32) for j in range(TOP)]
        self.chosen = [(slot_of == plan[:, TOP + j : TOP + j + 1]).astype(F32) for j in range(TOP)]
        self.select = (self.chosen[0] + self.chosen[1]).astype(BF)
        self.small = small

    def share(self):
        self.product = mm(self.low, self.small)
        shares = self.product + mm(self.rest, self.small)
        self.shares = []
        for index in range(2):
            one, two = lane_of(shares, 12 + 2 * index), lane_of(shares, 13 + 2 * index)
            peak = jnp.maximum(one, two)
            one, two = jnp.exp(one - peak), jnp.exp(two - peak)
            self.shares.append((one / (one + two), two / (one + two)))

    def gate(self, logits):
        values = [jnp.sum(p * logits, axis=-1, keepdims=True) for p in self.picks]
        peak = jnp.maximum(values[0], values[1])
        powers = [jnp.exp(v - peak) for v in values]
        total = powers[0] + powers[1]
        self.gates = [p / total for p in powers]
        self.combine = self.gates[0] * self.chosen[0] + self.gates[1] * self.chosen[1]

    def weigh(self):
        spread = self.gates[0] * self.picks[0] + self.gates[1] * self.picks[1]
        self.const_weights = [lane_of(spread, NF + 2 + index) for index in range(2)]
        self.normed_weight = lane_of(spread, NF + 1)
        for index in range(2):
            self.normed_weight = (
                self.normed_weight + self.const_weights[index] * self.shares[index][0]
            )


class ExpertRun:
    def __init__(self, net, e, rows_ref, all_ref, chunk):
        self.net, self.e, self.rows_ref, self.all_ref, self.chunk = net, e, rows_ref, all_ref, chunk
        self.mine = net.y * GROUPS + net.g

    def send(self):
        net, z = self.net, self.net.z
        steps = [(dy, dg) for dg in (2, 1, 3, 0) for dy in range(z.hh) if dy or dg]
        first = []
        for dy, dg in steps:
            target = net.up(net.y, dy, z.hh) * GROUPS + net.up(net.g, dg, GROUPS)
            place = self.all_ref.at[net.q, self.mine]
            first.append(net.push(self.rows_ref.at[target], place, net.near(dy=dy, dg=dg)))
        self.all_ref[net.q, self.mine] = self.rows_ref[self.mine]
        self.sources = [(0, 0, None)] + [
            (dy, dg, made) for (dy, dg), made in zip(reversed(steps), reversed(first))
        ]

    def relay(self, while_first):
        net, z = self.net, self.net.z
        self.slots = []
        self.aside, self.across = [[] for _ in range(z.splits)], [[] for _ in range(z.splits)]
        for k, (dy, dg, made) in enumerate(self.sources):
            if made is not None:
                made.wait_recv()
            self.slots.append(net.down(net.y, dy, z.hh) * GROUPS + net.down(net.g, dg, GROUPS))
            place = self.all_ref.at[net.q, self.slots[k]]
            for ds in range(1, z.splits):
                self.aside[ds].append(net.push(place, place, net.near(ds=ds)))
            self.across[0].append(net.push(place, place, net.near(dc=1)))
            if k == 0:
                while_first()

    def compute(self):
        net, z, e = self.net, self.net.z, self.e
        block = (z.experts, SLOT, z.width)
        e.base[...] = self.chunk(net.q).reshape(block)
        other = 1 - net.c
        for ds in range(1, z.splits):
            s = net.down(net.s, ds, z.splits)
            for k, made in enumerate(self.aside[ds]):
                made.wait_recv()
                place = self.all_ref.at[net.c * z.splits + s, self.slots[k]]
                self.across[ds].append(net.push(place, place, net.near(dc=1)))
        self.halves = {}
        for ds in range(z.splits):
            s = net.down(net.s, ds, z.splits)
            for made in self.across[ds]:
                made.wait_recv()
            e.part[ds] = self.chunk(other * z.splits + s).astype(BF).reshape(block)
            to_core = net.push(e.part.at[ds], e.got.at[ds], net.near(dc=1))
            if ds == 0:
                self.first_core = to_core
                continue
            kept = self.chunk(net.c * z.splits + s)
            to_core.wait_recv()
            net.sent = [made for made in net.sent if made is not to_core]
            to_core.wait_send()
            e.part[ds] = (kept.reshape(block) + e.got[ds].astype(F32)).astype(BF)
            for dy in reversed(range(z.hh)):
                span = pl.ds(net.up(net.y, dy, z.hh) * GROUPS, GROUPS)
                device = net.near(ds=z.splits - ds)
                made = net.push(e.part.at[ds, span], e.side_got.at[ds - 1, span], device)
                self.halves[ds, dy] = made

    def give_back(self):
        net, z, e = self.net, self.net.z, self.e
        self.first_core.wait_recv()
        e.base[...] += e.got[0].astype(F32)
        self.last = []
        for dy in reversed(range(z.hh)):
            y = net.up(net.y, dy, z.hh)
            span = pl.ds(y * GROUPS, GROUPS)
            total = e.base[span]
            for ds in range(1, z.splits):
                self.halves[ds, dy].wait_recv()
                total = total + e.side_got[ds - 1, span].astype(F32)
            e.sum[span] = total.astype(BF)
            for dg in (2, 1, 3, 0):
                if dy or dg:
                    src = e.sum.at[y * GROUPS + net.up(net.g, dg, GROUPS)]
                    made = net.push(src, e.back.at[self.mine], net.near(dy=dy, dg=dg))
                    self.last.append(made)
        e.back[self.mine] = e.sum[self.mine]

    def wait(self):
        for made in self.last:
            made.wait_recv()


def weight_of(z, e, w):
    e.wait_weight(w)
    ref = e.weights[w]
    if z.drow % 16 == 0:
        return ref[...].reshape(z.width, z.ffp)
    return jnp.concatenate([ref[n].astype(F32) for n in range(z.nb)], axis=0).astype(BF)


def held_weights(net, e):
    held = {}

    def weight(w):
        if w not in held:
            held[w] = weight_of(net.z, e, w)
        return held[w]

    return weight


def forward_chunk(net, e, weight):
    z = net.z

    def chunk(part):
        rows = e.all[part].reshape(z.count, z.width)
        gate, up = mm(rows, weight(0)), mm(rows, weight(1))
        e.gate[part], e.up[part] = gate.astype(BF), up.astype(BF)
        hidden = (gate / (1.0 + jnp.exp(-gate)) * up).astype(BF)
        return mm(hidden, weight(2), 1, 1)

    return chunk


def backward_chunk(net, e, weight):
    z = net.z

    def chunk(part):
        weight(0), weight(1)
        rows = e.dall[part].reshape(z.count, z.width)
        grad_hidden = mm(rows, weight(2))
        gate, up = e.gate[part].astype(F32), e.up[part].astype(F32)
        sig = 1.0 / (1.0 + jnp.exp(-gate))
        silu = gate * sig
        e.hid[part] = (silu * up).astype(BF)
        up_low = (grad_hidden * silu).astype(BF)
        gate_low = (grad_hidden * up * (sig * (1.0 + gate * (1.0 - sig)))).astype(BF)
        e.du[part], e.dg[part] = up_low, gate_low
        return mm(gate_low, weight(0), 1, 1) + mm(up_low, weight(1), 1, 1)

    return chunk


def weight_grads(net, e):
    z = net.z
    step = min(4, z.nq)
    for w, one, two in ((0, e.all, e.dg), (1, e.all, e.du), (2, e.dall, e.hid)):
        product = None
        for first in range(0, z.nq, step):
            span = slice(first, first + step)
            left = one[span].reshape(step * z.count, z.width)
            more = mm(left, two[span].reshape(step * z.count, z.ffp), 0, 0)
            product = more if product is None else product + more
        for n in range(z.nb):
            e.gw[w][n] = product[n * z.drow : (n + 1) * z.drow].astype(BF)


def put_rows(mixing, e):
    e.rows[...] = mm(mixing.select, mixing.low, 0, 0).astype(BF).reshape(e.rows.shape)


def put_grad_rows(mixing, e, high, rest):
    weight_high, weight_rest = split(mixing.combine)
    slot_grad = mm(weight_high, high, 0, 0) + mm(weight_rest, high, 0, 0)
    slot_grad = slot_grad + mm(weight_high, rest, 0, 0)
    e.rows[...] = slot_grad.astype(BF).reshape(e.rows.shape)


def mixture(z, mixing, middle, results):
    high, rest = split(mixing.combine)
    mixed = mm(high, results) + mm(rest, results) + mixing.normed_weight * mixing.normed
    for index in range(2):
        weight = mixing.const_weights[index] * mixing.shares[index][1]
        mixed = mixed + weight * mixing.consts[index]
    return middle + mixed


def mixture_grads(z, mixing, grad, grad_logits, high, rest, results):
    where_lane = lanes((z.rows, 128))
    along = mm(high, results, 1, 1) + mm(rest, results, 1, 1)
    normed_dot = jnp.sum(grad * mixing.normed, axis=-1, keepdims=True)
    const_dots = [jnp.sum(grad * c, axis=-1, keepdims=True) for c in mixing.consts]
    gate_grads = []
    for j in range(TOP):
        value = jnp.sum(mixing.chosen[j] * along, axis=-1, keepdims=True)
        value = value + lane_of(mixing.picks[j], NF + 1) * normed_dot
        for index in range(2):
            share = mixing.shares[index]
            value = value + lane_of(mixing.picks[j], NF + 2 + index) * (
                share[0] * normed_dot + share[1] * const_dots[index]
            )
        gate_grads.append(value)
    inner = mixing.gates[0] * gate_grads[0] + mixing.gates[1] * gate_grads[1]
    logit_grad = grad_logits
    for j in range(TOP):
        logit_grad = logit_grad + mixing.picks[j] * (mixing.gates[j] * (gate_grads[j] - inner))
    column = jnp.zeros((z.rows, 128), F32)
    const_columns = jnp.zeros((z.rows, 128), F32)
    for index in range(2):
        share, weight = mixing.shares[index], mixing.const_weights[index]
        one, two = weight * normed_dot, weight * const_dots[index]
        mean = share[0] * one + share[1] * two
        column = column + jnp.where(where_lane == 12 + 2 * index, share[0] * (one - mean), 0.0)
        column = column + jnp.where(where_lane == 13 + 2 * index, share[1] * (two - mean), 0.0)
        const_columns = const_columns + jnp.where(where_lane == 18 + index, weight * share[1], 0.0)
    both_high, both_rest = split(logit_grad + column)
    grad_normed = mm(both_high, mixing.small, 1, 1) + mm(both_rest, mixing.small, 1, 1)
    grad_normed = grad_normed + mixing.normed_weight * grad
    gsmall = mm(mixing.low, both_high, 0, 0) + mm(mixing.low, both_rest, 0, 0)
    gsmall = gsmall + mm(mixing.rest, column.astype(BF), 0, 0)
    const_high, const_rest = split(const_columns)
    gsmall = gsmall + mm(high, const_high, 0, 0) + mm(rest, const_high, 0, 0)
    return logit_grad, grad_normed, gsmall + mm(high, const_rest, 0, 0)


def middle_grads(z, mixing, e, middle, grad, grad_normed, gsmall):
    grad_normed = grad_normed + mm(mixing.select, e.back[...].reshape(z.count, z.width))
    place = (lanes((z.rows, 128)) == 17).astype(F32).astype(BF)
    high, rest = split(grad_normed * middle * mixing.root)
    e.gsmall[...] = gsmall + mm(high, place, 0, 0) + mm(rest, place, 0, 0)
    return grad + norm_grad(middle, mixing.root, mixing.gain, grad_normed)


def experts(net, e, middle, logits_in, at):
    z = net.z
    mixing = Mixing(z, middle, e.small[...], e.plan[...])
    put_rows(mixing, e)
    run = ExpertRun(net, e, e.rows, e.all, forward_chunk(net, e, held_weights(net, e)))

    def while_first():
        mixing.share()
        logits = mixing.product + logits_in
        e.logits[...] = logits
        mixing.gate(logits)
        mixing.weigh()
        act(at.rows)

    run.send()
    run.relay(while_first)
    run.compute()
    act(at.side)
    run.give_back()
    act(at.last)
    run.wait()
    e.results[...] = e.back[...]
    return mixture(z, mixing, middle, e.back[...].reshape(z.count, z.width))


def experts_back(net, e, middle, grad, grad_logits, at):
    z = net.z
    mixing = Mixing(z, middle, e.small[...], e.plan[...])
    mixing.gate(e.logits[...])
    high, rest = split(grad)
    put_grad_rows(mixing, e, high, rest)
    run = ExpertRun(net, e, e.rows, e.dall, backward_chunk(net, e, held_weights(net, e)))
    made = []

    def while_first():
        mixing.share()
        mixing.weigh()
        results = e.results[...].reshape(z.count, z.width)
        made.extend(mixture_grads(z, mixing, grad, grad_logits, high, rest, results))
        act(at.rows_back)

    run.send()
    run.relay(while_first)
    run.compute()
    weight_grads(net, e)
    act(at.side_back)
    run.give_back()
    act(at.last_back)
    run.wait()
    logit_grad, grad_normed, gsmall = made
    return middle_grads(z, mixing, e, middle, grad, grad_normed, gsmall), logit_grad


def experts_both(net, e, later, middle, logits_in, grad, grad_logits, at):
    z = net.z
    mixing = Mixing(z, middle, e.small[...], e.plan[...])
    put_rows(mixing, e)
    weight = held_weights(net, e)
    run = ExpertRun(net, e, e.rows, e.all, forward_chunk(net, e, weight))
    back = ExpertRun(net, later, later.rows, e.dall, backward_chunk(net, e, weight))
    run.send()
    act(at.rows)
    mixing.share()
    mixing.gate(mixing.product + logits_in)
    high, rest = split(grad)
    put_grad_rows(mixing, later, high, rest)
    back.send()
    mixing.weigh()
    run.relay(lambda: None)
    run.compute()
    back.relay(lambda: None)
    back.compute()
    run.give_back()
    weight_grads(net, e)
    act(at.side_back)
    back.give_back()
    act(at.last_back)
    run.wait()
    results = e.back[...].reshape(z.count, z.width)
    result = mixture(z, mixing, middle, results)
    made = mixture_grads(z, mixing, grad, grad_logits, high, rest, results)
    back.wait()
    logit_grad, grad_normed, gsmall = made
    return result, middle_grads(z, mixing, later, middle, grad, grad_normed, gsmall), logit_grad


def attend_kept(z):
    return dict(
        middle=struct((z.rows, z.width), F32),
        low=struct((z.rows, z.width), BF),
        q=struct((GROUPS, 3 * z.rows // 2, 128), BF),
        kv=struct((z.nb, z.rows, 384), BF),
        o=struct((GROUPS, z.rows, 256), F32),
        lse=struct((GROUPS, 3 * z.rows, 1), F32),
        ret=struct((GROUPS, 3 * z.rows // 2, 128), BF),
    )


def experts_kept(z):
    block = (z.experts, SLOT, z.width)
    return dict(
        logits=struct((z.rows, 128), F32),
        results=struct(block, BF),
        all=struct((z.nq,) + block, BF),
        gate=struct((z.nq, z.count, z.ffp), BF),
        up=struct((z.nq, z.count, z.ffp), BF),
    )


def attend_scratch(z):
    return dict(
        q_out=pltpu.VMEM((GROUPS, 3 * z.rows // 2, 128), BF),
        kv_out=pltpu.VMEM((GROUPS, z.rows, 384), BF),
        o_out=pltpu.VMEM((GROUPS, 3 * z.rows // 2, 128), BF),
    )


def attend_back_scratch(z, own_output=True):
    one = pltpu.VMEM((GROUPS, 3 * z.rows // 2, 128), BF)
    three = pltpu.VMEM((GROUPS, 3 * z.rows, 256), BF)
    two = pltpu.VMEM((GROUPS, z.rows, 384), BF)
    made = dict(
        do_out=one,
        do=one,
        dq_out=one,
        dq=one,
        dkv_out=pltpu.VMEM((z.nb, z.rows, 384), BF),
        dkv_got=pltpu.VMEM((z.splits - 1, GROUPS, z.rows, 384), BF),
        dkv_sum=two,
        dkv=two,
        q3=three,
        do3=three,
        dq_sum=pltpu.VMEM((GROUPS, z.rows, 256), F32),
        gin_part=pltpu.VMEM((2, z.shards, z.shard, 384), BF),
        gin_sem=pltpu.SemaphoreType.DMA((2,)),
        delta=pltpu.VMEM((GROUPS, 3 * z.rows, 1), F32),
    )
    if not own_output:
        del made["dkv_out"]
    return made


def experts_scratch(z):
    block = (z.experts, SLOT, z.width)
    flat = pltpu.VMEM((z.splits,) + block, BF)
    return dict(
        rows=pltpu.VMEM(block, BF),
        part=flat,
        got=flat,
        side_got=pltpu.VMEM((z.splits - 1,) + block, BF),
        base=pltpu.VMEM(block, F32),
        sum=pltpu.VMEM(block, BF),
        back=pltpu.VMEM(block, BF),
    )


def experts_back_scratch(z, both=True):
    part = pltpu.VMEM((z.nq, z.count, z.ffp), BF)
    block = (z.experts, SLOT, z.width)
    made = dict(dall=pltpu.VMEM((z.nq,) + block, BF), hid=part)
    if both:
        made.update(dict(dg=part, du=part))
    return made


def scratch_of(kept):
    return {name: pltpu.VMEM(v.shape, v.dtype) for name, v in kept.items()}


def view(held, **more):
    return Names(**{**held.__dict__, **more})


def landing(z):
    return struct((z.nb, z.drow, z.ffp), BF)


def near_landing(z):
    return struct((GROUPS, z.drow, z.ffp), BF)


def grad_landing(z):
    return struct((2, z.drow, z.hidden), BF)


def nothing():
    pass


CUT = 384


def in_vmem(arrays):
    return {name: (array, VMEM) for name, array in arrays.items()}


def in_place(arrays):
    return {name: (array, ANY) for name, array in arrays.items()}


def weight_pieces(z, owns, wholes):
    widths = (3 * z.width, z.width)
    return [
        (owns[which], wholes[which], first, columns)
        for which, first, columns in cuts_of((0, 1), widths, CUT)
    ]


def pieces_sems(z, pieces):
    return pieces * (2 + z.splits + z.hh)


def eye(size):
    shape = (size, size)
    return lax.broadcasted_iota(jnp.int32, shape, 0) == lax.broadcasted_iota(jnp.int32, shape, 1)


def upright(row, same):
    return jnp.sum(jnp.where(same, row, 0.0), axis=1, keepdims=True)


def plan_of(z, routes, order):
    same, lane = eye(z.rows), lanes((z.rows, 128))
    ids, ranks = routes.astype(F32), order.astype(F32)
    plan = jnp.zeros((z.rows, 128), F32)
    for j in range(TOP):
        own, rank = upright(ids[j : j + 1], same), upright(ranks[j : j + 1], same)
        before = jnp.zeros((z.rows, 1), F32)
        for k in range(TOP):
            counts = (own == ids[k : k + 1]) & (ranks[k : k + 1] < rank)
            before = before + jnp.sum(counts.astype(F32), axis=1, keepdims=True)
        slot = jnp.where((own < NF) & (before < CAP), own * SLOT + before, -1.0)
        plan = plan + jnp.where(lane == j, own, 0.0) + jnp.where(lane == TOP + j, slot, 0.0)
    return plan


def grid_of(z):
    return (z.hh, 2, 2, 2, z.splits, z.shard)


def gather_first(z, large, little):
    def body(k, net):
        owns, wholes = (k.attn_in.at[0], k.attn_out.at[0]), (k.w_in, k.w_out)
        pieces = weight_pieces(z, owns, wholes)
        gather = Gather(net, pieces, k.own)
        gather.step()
        moves = [
            NearWeights(net, k.expert_0, 0, k.near_0),
            NearWeights(net, k.expert_1, 0, k.near_1),
            NearWeights(net, k.expert_2, 0, k.near_2),
        ]
        same, lane = eye(z.shard), lanes((z.shard, 128))
        for layer in range(LAYERS):
            rows = [k.router[n][layer : layer + 1] for n in range(NE)]
            rows += [k.mix[layer][n : n + 1] for n in range(4)]
            rows += [k.gains[layer][n : n + 1] for n in range(2)]
            rows += [k.consts[layer][n : n + 1] for n in range(2)]
            table = jnp.zeros((z.shard, 128), F32)
            for n, row in enumerate(rows):
                table = table + jnp.where(lane == n, upright(row.astype(F32), same), 0.0)
            k.small_own[layer] = table.astype(BF)
        smalls = [
            (k.small_own.at[layer], whole, 0, 128)
            for layer, whole in enumerate((k.small_0, k.small_1))
        ]
        other = Gather(net, smalls, k.own_too)
        other.step()
        gather.step()
        moves[0].start()
        for layer, plan in enumerate((k.plan_0, k.plan_1)):
            plan[...] = plan_of(z, k.routes[layer], k.order[layer])
        same, lane = eye(z.rows), lanes((z.rows, 128))
        table = jnp.zeros((z.rows, 128), F32)
        for n in range(NE):
            table = table + jnp.where(lane == n, upright(k.prev[n : n + 1], same), 0.0)
        k.logits[...] = table
        gather.step()
        other.step()
        moves[1].start()
        moves[2].start()
        row = lax.broadcasted_iota(jnp.int32, (z.rows, 1), 0) + net.b * z.rows
        angles = row.astype(F32) * k.freqs[...]
        cosine, sine = jnp.cos(angles), jnp.sin(angles)
        sine = jnp.where(lane % HD < HD // 2, -sine, sine)
        for n in range(z.width // 128):
            k.cq[:, 128 * n : 128 * (n + 1)] = cosine
            k.sq[:, 128 * n : 128 * (n + 1)] = sine
        for _ in range(3):
            gather.step()
            other.step()
        other.step()
        for move in moves:
            move.wait()

    ins = {**in_place(large), **in_vmem(little)}
    outs = in_place(
        dict(
            w_in=struct(grid_of(z) + (3 * z.width,), BF),
            w_out=struct(grid_of(z) + (z.width,), BF),
            small_0=struct(grid_of(z) + (128,), BF),
            small_1=struct(grid_of(z) + (128,), BF),
            near_0=near_landing(z),
            near_1=near_landing(z),
            near_2=near_landing(z),
        )
    )
    table, wide = struct((z.rows, 128), F32), struct((z.rows, z.width), F32)
    outs.update(in_vmem(dict(plan_0=table, plan_1=table, logits=table, cq=wide, sq=wide)))
    pieces = len(weight_pieces(z, (0, 0), (0, 0)))
    scratch = dict(
        small_own=pltpu.VMEM((LAYERS, z.shard, 128), BF),
        own=pltpu.SemaphoreType.DMA((pieces,)),
        own_too=pltpu.SemaphoreType.DMA((LAYERS,)),
    )
    return launch(body, 0, z, ins, outs, scratch, pieces_sems(z, pieces + LAYERS) + 3 * GROUPS)


def layer_sems(z):
    attention = 6 + GROUPS * (z.splits - 1) + GROUPS
    expert = (z.experts - 1) * 2 + z.experts * (2 * z.splits - 1) + z.splits + z.hh * z.splits
    back = 3 + GROUPS * (z.splits - 1) + 2 * GROUPS
    return attention, expert, back


def waiting(*moves):
    held = list(moves)

    def wait(w):
        if held[w] is not None:
            held[w].wait()
            held[w] = None

    return wait


def layer_forward(z, values, tables, weights, near, shards, parts):
    def body(k, net):
        owns, wholes = (k.attn_in.at[1], k.attn_out.at[1]), (k.next_in, k.next_out)
        gather = Gather(net, weight_pieces(z, owns, wholes), k.own)
        far = [
            FarWeights(net, k.expert_0, 0, k.near_0, k.weight_0),
            FarWeights(net, k.expert_1, 0, k.near_1, k.weight_1),
            FarWeights(net, k.expert_2, 0, k.near_2, k.weight_2),
        ]
        ahead = [
            NearWeights(net, k.expert_0, 1, k.next_0),
            NearWeights(net, k.expert_1, 1, k.next_1),
            NearWeights(net, k.expert_2, 1, k.next_2),
        ]
        at = Beside(
            start=[gather.step, far[0].start],
            sent=[gather.step, far[1].start],
            out=[gather.step],
            rows=[far[2].start, gather.step, ahead[0].start],
            side=[gather.step, ahead[1].start],
            last=[gather.step, ahead[2].start],
        )
        middle = attend(net, k, k.tokens[...].astype(F32), at)
        e = view(k, weights=(k.weight_0, k.weight_1, k.weight_2), wait_weight=waiting(*far))
        k.state[...] = experts(net, e, middle, k.logits_in[...], at)
        for move in ahead:
            move.wait()

    ins = {**in_vmem(values), **in_vmem(tables), **in_vmem(weights)}
    ins.update({**in_place(shards), **in_place(parts), **in_place(near)})
    whole = landing(z)
    outs = dict(state=struct((z.rows, z.width), F32))
    outs.update(dict(weight_0=whole, weight_1=whole, weight_2=whole))
    outs = in_vmem({**outs, **attend_kept(z), **experts_kept(z)})
    ahead = dict(
        next_in=struct(grid_of(z) + (3 * z.width,), BF),
        next_out=struct(grid_of(z) + (z.width,), BF),
        next_0=near_landing(z),
        next_1=near_landing(z),
        next_2=near_landing(z),
    )
    outs.update(in_place(ahead))
    pieces = len(weight_pieces(z, (0, 0), (0, 0)))
    own = dict(own=pltpu.SemaphoreType.DMA((pieces,)))
    scratch = {**attend_scratch(z), **experts_scratch(z), **own}
    attention, expert, _ = layer_sems(z)
    count = attention + expert + pieces_sems(z, pieces) + 3 * z.nb + 3 * GROUPS
    return launch(body, 1, z, ins, outs, scratch, count)


def back_outputs(z, more):
    outs = dict(
        grad=struct((z.rows, z.width), F32),
        grad_logits=struct((z.rows, 128), F32),
        gout=struct((z.shards, z.shard, z.width), BF),
        gsmall=struct((z.width, 128), F32),
        gw_2=landing(z),
    )
    rest = dict(
        gin=struct((z.shards, z.shard, 3 * z.width), BF),
        grad_0=grad_landing(z),
        grad_1=grad_landing(z),
    )
    return {**in_vmem({**outs, **more}), **in_place(rest)}


def layer_both(z, values, tables, weights, near, parts):
    together = z.nb <= 8

    def body(k, net):
        far = [
            FarWeights(net, k.expert_0, 1, k.near_0, k.weight_0),
            FarWeights(net, k.expert_1, 1, k.near_1, k.weight_1),
            FarWeights(net, k.expert_2, 1, k.near_2, k.weight_2),
        ]
        grads = [GradMove(net, k.gw_0, k.grad_0), GradMove(net, k.gw_1, k.grad_1)]
        at = Beside(
            start=[far[0].start],
            sent=[far[1].start],
            rows=[far[2].start],
            side_back=[grads[0].near],
            last_back=[grads[0].far],
            back_sent=[grads[1].near],
            back_out=[grads[1].far],
        )
        middle = attend(net, k, k.state[...], at)
        e = view(
            k,
            weights=(k.weight_0, k.weight_1, k.weight_2),
            gw=(k.gw_0, k.gw_1, k.gw_2),
            wait_weight=waiting(*far),
            dg=k.gate,
            du=k.up,
        )
        none = jnp.zeros((z.rows, 128), F32)
        grad = k.cotangent[...].astype(F32)
        if together:
            later = view(
                e,
                rows=k.rows_2,
                part=k.part_2,
                got=k.got_2,
                side_got=k.side_got_2,
                base=k.base_2,
                sum=k.sum_2,
                back=k.back_2,
            )
            result, dm, grad_logits = experts_both(
                net, e, later, middle, k.logits_in[...], grad, none, at
            )
        else:
            result = experts(net, e, middle, k.logits_in[...], at)
            net.settle()
            dm, grad_logits = experts_back(net, e, k.middle[...], grad, none, at)
        k.output[...] = result.astype(BF)
        k.grad_logits[...] = grad_logits
        net.settle()
        k.grad[...] = attend_back(net, view(k, dkv_out=k.kv), k.state[...], dm, at)
        for move in grads:
            move.wait()

    ins = {**in_vmem(values), **in_vmem(tables), **in_vmem(weights)}
    ins.update({**in_place(parts), **in_place(near)})
    outs = back_outputs(z, dict(output=struct((z.rows, z.width), BF)))
    scratch = {
        **scratch_of(attend_kept(z)),
        **scratch_of(experts_kept(z)),
        **attend_scratch(z),
        **attend_back_scratch(z, False),
        **experts_scratch(z),
        **experts_back_scratch(z, False),
    }
    if together:
        scratch.update({name + "_2": memory for name, memory in experts_scratch(z).items()})
    place = pltpu.VMEM(landing(z).shape, BF)
    scratch.update(dict(weight_0=place, weight_1=place, weight_2=place, gw_0=place, gw_1=place))
    attention, expert, back = layer_sems(z)
    count = attention + 2 * expert + back + 5 * z.nb
    return launch(body, 2, z, ins, outs, scratch, count)


def sum_pieces(z, k):
    wholes, sums = (k.up_in, k.up_out), (k.sum_in, k.sum_out)
    return weight_pieces(z, wholes, sums) + [(k.up_small, k.sum_small, 0, 128)]


def sum_parts(z, made):
    def grid(v):
        return v.reshape(grid_of(z) + (v.shape[-1],))

    ins = dict(up_in=grid(made.gin), up_out=grid(made.gout), up_small=grid(made.gsmall))
    outs = dict(
        sum_in=struct((z.shard, 3 * z.width), F32),
        sum_out=struct((z.shard, z.width), F32),
        sum_small=struct((z.shard, 128), F32),
    )
    columns = [(c, BF) for _, _, _, c in weight_pieces(z, (0, 0), (0, 0))] + [(128, F32)]
    buffers = reduce_buffers(z, columns)
    buffers.update(dict(mine=pltpu.SemaphoreType.DMA((len(columns),))))
    return ins, outs, buffers, len(columns)


def layer_back(z, values, tables, weights, first, upper):
    ups, sums, buffers, pieces = sum_parts(z, upper)

    def body(k, net):
        reduce = Reduce(net, sum_pieces(z, k), buffers_of(k, pieces), k.mine)
        late = GradMove(net, k.late, k.late_grad)
        own = [
            GradMove(net, k.gw_0, k.grad_0),
            GradMove(net, k.gw_1, k.grad_1),
            GradMove(net, k.gw_2, k.grad_2),
        ]
        at = Beside(
            rows_back=[reduce.step, late.near, late.far],
            side_back=[reduce.step],
            last_back=[own[0].far],
            back_sent=[reduce.step, own[1].far],
            back={1: [own[2].far]},
            back_out=[reduce.step],
        )
        pairs = ((k.far_gate, k.gate), (k.far_up, k.up), (k.far_kv, k.kv))
        loads = [
            pltpu.make_async_copy(far, near, k.load.at[n]) for n, (far, near) in enumerate(pairs)
        ]
        for load in loads:
            load.start()
        reduce.step()

        def wait(w):
            if w == 0:
                loads[0].wait()
                loads[1].wait()

        e = view(
            k,
            weights=(k.weight_0, k.weight_1, k.weight_2),
            gw=(k.gw_0, k.gw_1, k.gw_2),
            wait_weight=wait,
            dg=k.gate,
            du=k.up,
        )
        dm, grad_logits = experts_back(
            net, e, k.middle[...], k.grad_in[...], k.grad_logits_in[...], at
        )
        k.grad_logits[...] = grad_logits
        loads[2].wait()
        x = k.tokens[...].astype(F32)
        k.grad[...] = attend_back(net, view(k, dkv_out=k.kv), x, dm, at)
        reduce.step()
        late.wait()
        for move in own:
            move.wait((False, True))

    kept = {**attend_kept(z), **experts_kept(z)}
    far = dict(far_gate=kept.pop("gate"), far_up=kept.pop("up"), far_kv=kept.pop("kv"))
    loaded = {name[4:]: pltpu.VMEM(v.shape, v.dtype) for name, v in far.items()}
    ins = {**in_vmem(values), **in_vmem(tables), **in_vmem(weights)}
    ins.update(in_vmem({name: getattr(first, name) for name in kept}))
    ins.update(in_place({name: getattr(first, name[4:]) for name in far}))
    ins.update(in_place({**ups, **dict(late=upper.gw_2)}))
    outs = back_outputs(z, {**sums, **dict(gw_0=landing(z), gw_1=landing(z))})
    outs.update(in_place(dict(grad_2=grad_landing(z), late_grad=grad_landing(z))))
    scratch = {
        **attend_back_scratch(z, False),
        **experts_scratch(z),
        **experts_back_scratch(z, False),
        **loaded,
        **buffers,
        **dict(load=pltpu.SemaphoreType.DMA((3,))),
    }
    _, expert, back = layer_sems(z)
    count = expert + back + 4 * z.nb + pieces_sems(z, pieces)
    return launch(body, 3, z, ins, outs, scratch, count)


def reduce_last(z, lower):
    ups, sums, buffers, pieces = sum_parts(z, lower)

    def body(k, net):
        reduce = Reduce(net, sum_pieces(z, k), buffers_of(k, pieces), k.mine)
        reduce.step()
        own = [
            GradMove(net, k.gw_0, k.grad_0),
            GradMove(net, k.gw_1, k.grad_1),
            GradMove(net, k.gw_2, k.grad_2),
        ]
        for move in own:
            move.near()
        for _ in range(5):
            reduce.step()
        for move in own:
            move.wait((True, False))

    half = dict(half_0=lower.grad_0, half_1=lower.grad_1, half_2=lower.grad_2)
    ins = in_place({**ups, **dict(gw_0=lower.gw_0, gw_1=lower.gw_1, gw_2=lower.gw_2), **half})
    whole = grad_landing(z)
    outs = {**in_place(dict(grad_0=whole, grad_1=whole, grad_2=whole)), **in_vmem(sums)}
    same = list(zip(half, outs))
    return launch(body, 4, z, ins, outs, buffers, 3 * z.nb + pieces_sems(z, pieces), same)


def local(
    tokens,
    prev_logits,
    norm_gains,
    attn_in_weight,
    attn_out_weight,
    router_weight,
    const_mix,
    const_values,
    expert_gate,
    expert_up,
    expert_down,
    routes,
    order,
    cotangent,
):
    rows, width = tokens.shape
    z = Shape(lax.axis_size("head"), lax.axis_size("blk"), rows, width, expert_gate.shape[3])
    lane = np.arange(128) % (HD // 2)
    freqs = np.float32(10000.0) ** (-(2 * lane).astype(np.float32) / np.float32(HD))
    shards = dict(attn_in=attn_in_weight, attn_out=attn_out_weight)
    little = dict(
        router=jnp.transpose(router_weight, (2, 0, 1)),
        mix=jnp.transpose(const_mix, (0, 2, 1)),
        gains=norm_gains,
        consts=const_values,
        routes=jnp.transpose(routes, (0, 2, 1)),
        order=jnp.transpose(order, (0, 2, 1)),
        prev=jnp.transpose(prev_logits),
        freqs=jnp.asarray(freqs.astype(np.float32))[None],
    )
    parts = dict(expert_0=expert_gate, expert_1=expert_up, expert_2=expert_down)
    made = gather_first(z, {**shards, **parts}, little)
    tables = dict(cq=made.cq, sq=made.sq)

    def flat(v):
        return v.reshape(width, v.shape[-1])

    weights = dict(
        w_in=flat(made.w_in),
        w_out=flat(made.w_out),
        small=flat(made.small_0),
    )
    near = dict(near_0=made.near_0, near_1=made.near_1, near_2=made.near_2)
    values = dict(tokens=tokens, logits_in=made.logits, plan=made.plan_0)
    first = layer_forward(z, values, tables, weights, near, shards, parts)
    weights_1 = dict(
        w_in=flat(first.next_in),
        w_out=flat(first.next_out),
        small=flat(made.small_1),
    )
    near = dict(near_0=first.next_0, near_1=first.next_1, near_2=first.next_2)
    values = dict(
        state=first.state, logits_in=first.logits, plan=made.plan_1, cotangent=cotangent
    )
    upper = layer_both(z, values, tables, weights_1, near, parts)
    weights.update(
        dict(weight_0=first.weight_0, weight_1=first.weight_1, weight_2=first.weight_2)
    )
    values = dict(
        tokens=tokens, plan=made.plan_0, grad_in=upper.grad, grad_logits_in=upper.grad_logits
    )
    lower = layer_back(z, values, tables, weights, first, upper)
    final = reduce_last(z, lower)
    in_sum = jnp.stack([final.sum_in, lower.sum_in])
    out_sum = jnp.stack([final.sum_out, lower.sum_out])
    small_sum = jnp.stack([final.sum_small, lower.sum_small])
    expert_out = [
        jnp.stack(pair).astype(F32)
        for pair in (
            (final.grad_0, upper.grad_0),
            (final.grad_1, upper.grad_1),
            (final.grad_2, lower.late_grad),
        )
    ]
    return (
        upper.output,
        lower.grad,
        lower.grad_logits[:, :NE],
        jnp.transpose(small_sum[:, :, 16:18], (0, 2, 1)),
        in_sum,
        out_sum,
        small_sum[:, :, :NE],
        small_sum[:, :, NE : NE + 4],
        jnp.transpose(small_sum[:, :, 18:20], (0, 2, 1)),
        expert_out[0],
        expert_out[1],
        expert_out[2],
    )


def solution(mesh):
    placed = (
        P(("head", "blk"), None),
        P(("head", "blk"), None),
        P(None, None, ("head", "blk")),
        P(None, ("head", "blk"), None),
        P(None, ("head", "blk"), None),
        P(None, ("head", "blk"), None),
        P(None, ("head", "blk"), None),
        P(None, None, ("head", "blk")),
        P(None, "head", "blk", None),
        P(None, "head", "blk", None),
        P(None, "head", "blk", None),
        P(None, ("head", "blk"), None),
        P(None, ("head", "blk"), None),
        P(("head", "blk"), None),
    )
    return jax.shard_map(
        local,
        mesh=mesh,
        in_specs=placed,
        out_specs=(
            P(("head", "blk"), None),
            P(("head", "blk"), None),
            P(("head", "blk"), None),
            P(None, None, ("head", "blk")),
            P(None, ("head", "blk"), None),
            P(None, ("head", "blk"), None),
            P(None, ("head", "blk"), None),
            P(None, ("head", "blk"), None),
            P(None, None, ("head", "blk")),
            P(None, "head", "blk", None),
            P(None, "head", "blk", None),
            P(None, "head", "blk", None),
        ),
        check_vma=False,
    )
```

```python
import jax
import jax.numpy as jnp
import numpy as np
from jax import lax
from jax.experimental import pallas as pl
from jax.experimental.pallas import tpu as pltpu
from jax.sharding import PartitionSpec as P

HEADS = 12
HD = 64
NF = 8
TOP = 2
LAYERS = 2
NE = 12
CAP = 26
SLOT = 32
GROUPS = 4
EPSILON = 1e-05
NEGATIVE = -1e30
SCALE = HD ** (-0.5)
VMEM_BYTES = 65200 * 1024

BF = jnp.bfloat16
F32 = jnp.float32
MESH = pl.DeviceIdType.MESH
VMEM = pl.BlockSpec(memory_space=pltpu.VMEM)
ANY = pl.BlockSpec(memory_space=pl.ANY)


def mm(a, b, ca=1, cb=0):
    return lax.dot_general(a, b, (((ca,), (cb,)), ((), ())), preferred_element_type=F32)


def split(v):
    high = v.astype(BF)
    return high, (v - high.astype(F32)).astype(BF)


def lanes(shape):
    return lax.broadcasted_iota(jnp.int32, shape, len(shape) - 1)


def lane_of(v, index):
    return jnp.sum(jnp.where(lanes(v.shape) == index, v, 0.0), axis=-1, keepdims=True)


def rows_of(small):
    pick = lax.broadcasted_iota(jnp.int32, (8, 128), 0) + 16 == lanes((8, 128))
    return mm(pick.astype(F32).astype(BF), small, 1, 1)


def swap_halves(v):
    width = v.shape[-1]
    low_half = lanes(v.shape) % HD < HD // 2
    return jnp.where(
        low_half, pltpu.roll(v, width - HD // 2, 1), pltpu.roll(v, HD // 2, 1)
    )


def rotate(v, cosine, sine):
    return v * cosine + swap_halves(v) * sine


def rotate_back(v, cosine, sine):
    return v * cosine - swap_halves(v) * sine


def norm_grad(v, root, gain, grad):
    scaled = grad * gain
    inner = jnp.mean(v * scaled, axis=-1, keepdims=True)
    return root * scaled - v * (root * root * root * inner)


class Shape:
    def __init__(self, nh, nb, rows, width, hidden):
        self.nh, self.nb, self.rows, self.width, self.hidden = nh, nb, rows, width, hidden
        self.hh = nh // 2
        self.splits = nb // GROUPS
        self.nq = 2 * self.splits
        self.experts = self.hh * GROUPS
        self.ffp = hidden // self.nq
        self.drow = width // nb
        self.shards = nh * nb
        self.shard = width // self.shards
        self.count = self.experts * SLOT


class Links:
    def __init__(self, z, send, recv):
        self.z, self.send, self.recv, self.used = z, send, recv, 0
        self.sent, self.sent_if = [], []
        h, b = lax.axis_index("head"), lax.axis_index("blk")
        self.h, self.b = h, b
        self.y, self.c = h // 2, lax.rem(h, 2)
        self.g, self.s = b // z.splits, lax.rem(b, z.splits)
        self.q = self.c * z.splits + self.s

    def device(self, y, c, g, s):
        return (y * 2 + c, g * self.z.splits + s)

    def near(self, dy=0, dc=0, dg=0, ds=0):
        z = self.z
        return self.device(
            lax.rem(self.y + dy, z.hh),
            lax.rem(self.c + dc, 2),
            lax.rem(self.g + dg, GROUPS),
            lax.rem(self.s + ds, z.splits),
        )

    def beside(self):
        low = lax.rem(self.g, 2)
        return self.device(self.y, self.c, self.g + 1 - 2 * low, self.s)

    def up(self, value, step, size):
        return lax.rem(value + step, size)

    def down(self, value, step, size):
        return lax.rem(value + size - step, size)

    def take(self, amount):
        first = self.used
        self.used += amount
        return first

    def remote(self, src, dst, device, send, recv):
        return pltpu.make_async_remote_copy(
            src_ref=src,
            dst_ref=dst,
            send_sem=self.send.at[send],
            recv_sem=self.recv.at[recv],
            device_id=device,
            device_id_type=MESH,
        )

    def push(self, src, dst, device):
        place = self.take(1)
        made = self.remote(src, dst, device, place, place)
        made.start()
        self.sent.append(made)
        return made

    def push_or_keep(self, src, dst, device, here, send, recv):
        made = self.remote(src, dst, device, send, recv)

        @pl.when(jnp.logical_not(here))
        def _():
            made.start()

        @pl.when(here)
        def _():
            pltpu.make_async_copy(src, dst, self.recv.at[recv]).start()

        self.sent_if.append((here, made))

    def arrived(self, place, recv):
        pltpu.make_async_copy(place, place, self.recv.at[recv]).wait()

    def settle(self):
        for made in self.sent:
            made.wait_send()
        for here, made in self.sent_if:

            @pl.when(jnp.logical_not(here))
            def _(made=made):
                made.wait_send()

        self.sent, self.sent_if = [], []


def greet(devices):
    barrier = pltpu.get_barrier_semaphore()
    for device in devices:
        pl.semaphore_signal(barrier, inc=1, device_id=device, device_id_type=MESH)
    pl.semaphore_wait(barrier, len(devices))


def greet_all(net):
    z = net.z
    known = [net.near(dg=dg, ds=ds) for dg in range(GROUPS) for ds in range(z.splits) if dg or ds]
    known += [
        net.near(dc=1, dg=dg, ds=ds) for dg in range(GROUPS) for ds in range(z.splits)
    ]
    known += [
        net.near(dy=dy, dg=dg) for dy in range(1, z.hh) for dg in range(GROUPS)
    ]
    greet(known)


class Names:
    def __init__(self, **more):
        self.__dict__.update(more)


class Beside:
    start = sent = mid = out = rows = side = last = ()
    rows_back = side_back = last_back = back_sent = back_out = ()
    back = {}

    def __init__(self, **more):
        self.__dict__.update(more)


def act(functions):
    for function in functions:
        function()


def launch(body, number, z, ins, outs, scratch, copies, same=()):
    names = list(ins) + list(outs) + list(scratch) + ["send", "recv"]

    def kernel(*refs):
        held = Names(**dict(zip(names, refs)))
        net = Links(z, held.send, held.recv)
        greet_all(net)
        body(held, net)
        net.settle()
        assert net.used <= copies, net.used

    made = pl.pallas_call(
        kernel,
        out_shape=[v[0] for v in outs.values()],
        in_specs=[v[1] for v in ins.values()],
        out_specs=[v[1] for v in outs.values()],
        scratch_shapes=list(scratch.values())
        + [pltpu.SemaphoreType.DMA((copies,)), pltpu.SemaphoreType.DMA((copies,))],
        input_output_aliases={list(ins).index(i): list(outs).index(o) for i, o in same},
        compiler_params=pltpu.CompilerParams(
            collective_id=number, has_side_effects=True, vmem_limit_bytes=VMEM_BYTES
        ),
    )(*[v[0] for v in ins.values()])
    return Names(**dict(zip(outs, made)))


def struct(shape, kind):
    return jax.ShapeDtypeStruct(shape, kind)


class NearWeights:
    def __init__(self, net, part, layer, landed):
        self.net, self.part, self.layer, self.landed = net, part, layer, landed
        self.first = net.take(GROUPS)

    def start(self):
        net = self.net
        for dc in range(2):
            for dl in range(2):
                device, src = weight_source(net, self.part, self.layer, dc, 0, dl)
                dst, place, at = self.landed.at[net.g], self.first + 2 * dc + dl, self.first + net.g
                if dc or dl:
                    made = net.remote(src, dst, device, place, at)
                    made.start()
                    net.sent.append(made)
                else:
                    net.push_or_keep(src, dst, device, net.g // 2 == net.c, place, at)

    def wait(self):
        for n in range(GROUPS):
            self.net.arrived(self.landed.at[n], self.first + n)


class FarWeights:
    def __init__(self, net, part, layer, near, landed):
        self.net, self.part, self.layer, self.landed = net, part, layer, landed
        self.first = net.take(net.z.nb)
        for n in range(GROUPS):
            at = n * net.z.splits + net.s
            pltpu.make_async_copy(near.at[n], landed.at[at], net.recv.at[self.first + at]).start()

    def start(self):
        net, z = self.net, self.net.z
        place = self.first
        for ds in range(1, z.splits):
            for dc in range(2):
                for dl in range(2):
                    device, src = weight_source(net, self.part, self.layer, dc, ds, dl)
                    dst = self.landed.at[net.b]
                    made = net.remote(src, dst, device, place, self.first + net.b)
                    made.start()
                    net.sent.append(made)
                    place += 1

    def wait(self):
        for n in range(self.net.z.nb):
            self.net.arrived(self.landed.at[n], self.first + n)


def weight_source(net, part, layer, dc, ds, dl):
    z = net.z
    e = lax.rem(net.g + dl, 2)
    c, s = net.up(net.c, dc, 2), net.up(net.s, ds, z.splits)
    cols = pl.ds(pl.multiple_of((c * z.splits + s) * z.ffp, 128), z.ffp)
    return net.device(net.y, c, 2 * net.c + e, s), part.at[layer, e, :, cols]


class GradMove:
    def __init__(self, net, grads, landed):
        self.net, self.grads, self.landed = net, grads, landed
        self.first = net.take(net.z.nb)

    def near(self):
        self.start([r for r in range(self.net.z.nb) if r % self.net.z.splits == 0])

    def far(self):
        self.start([r for r in range(self.net.z.nb) if r % self.net.z.splits])

    def start(self, steps):
        net, z = self.net, self.net.z
        e = lax.rem(net.g, 2)
        cols = pl.ds(pl.multiple_of(net.q * z.ffp, 128), z.ffp)
        at = self.first + e * z.nq + net.q
        for r in steps:
            t = net.up(net.b, r, z.nb)
            src, dst = self.grads.at[t], self.landed.at[e, :, cols]
            device = (net.y * 2 + net.g // 2, t)
            if r:
                made = net.remote(src, dst, device, self.first + r, at)
                made.start()
                net.sent.append(made)
            else:
                net.push_or_keep(src, dst, device, net.g // 2 == net.c, self.first, at)

    def wait(self, shares=(True, True)):
        net, z = self.net, self.net.z
        for e in range(2):
            for c in range(2):
                for ds in range(z.splits):
                    if shares[1 if ds else 0]:
                        n = c * z.splits + net.up(net.s, ds, z.splits)
                        cols = pl.ds(pl.multiple_of(n * z.ffp, 128), z.ffp)
                        net.arrived(self.landed.at[e, :, cols], self.first + e * z.nq + n)


def cuts_of(names, widths, size):
    return [
        (name, at, min(size, width - at))
        for name, width in zip(names, widths)
        for at in range(0, width, size)
    ]


class Gather:
    STEPS = 6

    def __init__(self, net, pieces, own_sems):
        self.net, self.pieces, self.stage = net, pieces, 0
        at = (net.y, net.c, net.g // 2, lax.rem(net.g, 2), net.s)
        self.keep = []
        for p in range(len(pieces)):
            self.keep.append(
                pltpu.make_async_copy(self.own(p), self.full(p, at), own_sems.at[p])
            )
            self.keep[-1].start()
        self.waiting = [[] for _ in pieces]

    def own(self, p):
        ref, _, first, columns = self.pieces[p]
        return ref.at[:, first : first + columns]

    def full(self, p, at):
        _, ref, first, columns = self.pieces[p]
        return ref.at[at + (slice(None), slice(first, first + columns))]

    def step(self):
        net, z, every = self.net, self.net.z, slice(None)
        y, c, s = net.y, net.c, net.s
        high, low = net.g // 2, lax.rem(net.g, 2)
        splits = [net.near(ds=d) for d in range(1, z.splits)]
        ys = [net.near(dy=d) for d in range(1, z.hh)]
        by_split = [((y, c, every, every, s), splits), ((y, c, every, every, every), ys)]
        by_y = [((y, c, every, every, s), ys), ((every, c, every, every, s), splits)]
        for p in range(len(self.pieces)):
            for made in self.waiting[p]:
                made.wait_recv()
            self.waiting[p] = []
            if self.stage == 1:
                self.keep[p].wait()
            if self.stage == 5:
                continue
            if self.stage == 0:
                at, peers = (y, c, high, low, s), [net.near(dg=2)]
            elif self.stage == 1:
                at, peers = (y, c, every, low, s), [net.beside()]
            elif self.stage == 4:
                at, peers = (every, c, every, every, every), [net.near(dc=1)]
            else:
                at, peers = (by_y if p % 2 else by_split)[self.stage - 2]
            place = self.full(p, at)
            src = self.own(p) if self.stage == 0 else place
            self.waiting[p] = [net.push(src, place, peer) for peer in peers]
        self.stage += 1


class Reduce:
    STEPS = 6

    def __init__(self, net, pieces, bufs, sems):
        self.net, self.pieces, self.bufs, self.stage = net, pieces, bufs, 0
        self.waiting = [[] for _ in pieces]
        self.mine = []
        for p, (full, _, lo, columns) in enumerate(pieces):
            own = full.at[:, net.c, :, :, :, :, slice(lo, lo + columns)]
            self.mine.append(pltpu.make_async_copy(own, bufs[p][5], sems.at[p]))

    def step(self):
        net, z = self.net, self.net.z
        y, c, s = net.y, net.c, net.s
        high, low = net.g // 2, lax.rem(net.g, 2)
        to_y = [(net.up(y, d, z.hh), net.near(dy=d)) for d in range(1, z.hh)]
        to_split = [(net.up(s, d, z.splits), net.near(ds=d)) for d in range(1, z.splits)]
        bits = [(i, j) for i in range(2) for j in range(2)]
        for p, (full, out, lo, columns) in enumerate(self.pieces):
            cut = slice(lo, lo + columns)
            one, two, three, four, five, own = self.bufs[p]
            kind = full.dtype
            for made in self.waiting[p]:
                made.wait_recv()
            moves = []
            split_first = p % 2 == 1
            firsts, seconds = (to_split, to_y) if split_first else (to_y, to_split)
            if self.stage == 0:
                moves = [(full.at[:, 1 - c, :, :, :, :, cut], one, net.near(dc=1))]
                self.mine[p].start()
            elif self.stage == 1:
                self.mine[p].wait()
                for a in range(z.hh):
                    for i, j in bits:
                        total = one[a, i, j].astype(F32) + own[a, i, j].astype(F32)
                        one[a, i, j] = total.astype(kind)
                for k, (t, peer) in enumerate(firsts):
                    moves.append((one.at[:, :, :, t] if split_first else one.at[t], two.at[k], peer))
            elif self.stage == 2:
                for i, j in bits:
                    for a in range(z.hh) if split_first else (0,):
                        at = (a, i, j) if split_first else (i, j)
                        total = (one[a, i, j, s] if split_first else one[y, i, j]).astype(F32)
                        for k in range(len(firsts)):
                            total = total + two[(k,) + at].astype(F32)
                        two[(0,) + at] = total.astype(kind)
                for k, (t, peer) in enumerate(seconds):
                    moves.append((two.at[0, t] if split_first else two.at[0, :, :, t], three.at[k], peer))
            elif self.stage == 3:
                for i, j in bits:
                    total = (two[0, y, i, j] if split_first else two[0, i, j, s]).astype(F32)
                    for k in range(len(seconds)):
                        total = total + three[k, i, j].astype(F32)
                    three[0, i, j] = total.astype(kind)
                moves = [(three.at[0, :, 1 - low], four, net.beside())]
            elif self.stage == 4:
                for i in range(2):
                    four[i] = (three[0, i, low].astype(F32) + four[i].astype(F32)).astype(kind)
                moves = [(four.at[1 - high], five, net.near(dg=2))]
            else:
                out[:, cut] = four[high].astype(F32) + five[...].astype(F32)
            self.waiting[p] = [net.push(*move) for move in moves]
        self.stage += 1


def reduce_buffers(z, columns_kinds):
    made = {}
    for p, (columns, kind) in enumerate(columns_kinds):
        block = (z.shard, columns)
        made[f"r{p}a"] = pltpu.VMEM((z.hh, 2, 2, z.splits) + block, kind)
        if p % 2 == 0:
            made[f"r{p}b"] = pltpu.VMEM((z.hh - 1, 2, 2, z.splits) + block, kind)
            made[f"r{p}c"] = pltpu.VMEM((z.splits - 1, 2, 2) + block, kind)
        else:
            made[f"r{p}b"] = pltpu.VMEM((z.splits - 1, z.hh, 2, 2) + block, kind)
            made[f"r{p}c"] = pltpu.VMEM((z.hh - 1, 2, 2) + block, kind)
        made[f"r{p}d"] = pltpu.VMEM((2,) + block, kind)
        made[f"r{p}e"] = pltpu.VMEM(block, kind)
        made[f"r{p}f"] = pltpu.VMEM((z.hh, 2, 2, z.splits) + block, kind)
    return made


def buffers_of(held, pieces):
    return [[getattr(held, f"r{p}{k}") for k in "abcdef"] for p in range(pieces)]


def head_masks(first):
    where_lane = lanes((1, 256))
    return [
        ((where_lane >= first + HD * j) & (where_lane < first + HD * (j + 1))).astype(F32)
        for j in range(3)
    ]


def window(v, g, shifted):
    start = 384 * (g // 2) + 128 * (g % 2)
    cut = v[:, start : start + 256]
    if shifted:
        if g % 2 == 0:
            cut = pltpu.roll(cut, HD, 1)
        return jnp.where(lanes(cut.shape) >= HD, cut, 0.0)
    if g % 2 == 1:
        cut = pltpu.roll(cut, 256 - HD, 1)
    return jnp.where(lanes(cut.shape) < 192, cut, 0.0)


def pack(v):
    half = v.shape[0] // 2
    last = v[:half, 128:] + pltpu.roll(v[half:, 128:], HD, 1)
    return v[:, :128].astype(BF), last.astype(BF)


def put_packed(ref, v):
    upper, last = pack(v)
    rows = v.shape[0]
    ref[:rows], ref[rows:] = upper, last


def unpack(packed):
    rows = packed.shape[0] * 2 // 3
    last = packed[rows:].astype(F32)
    keep = lanes(last.shape) < HD
    lower = jnp.concatenate(
        [jnp.where(keep, last, 0.0), jnp.where(keep, pltpu.roll(last, HD, 1), 0.0)], axis=0
    )
    return jnp.concatenate([packed[:rows].astype(F32), lower], axis=1)


def unwindow(even, odd):
    odd = pltpu.roll(odd, HD, 1)
    return [even[:, :128], even[:, 128:] + odd[:, :128], odd[:, 128:]]


def joined(key, value):
    return [key[:, :128], key[:, 128:] + value[:, :128], value[:, 128:]]


def places(net, first, last):
    z = net.z
    row = lax.broadcasted_iota(jnp.int32, ((last - first) * 3 * z.rows, 1), 0)
    block = first + row // (3 * z.rows)
    return (block * z.splits + net.s) * z.rows + row % z.rows


def attend(net, a, x, at):
    z = net.z
    act(at.start)
    gain = rows_of(a.small[...])[0:1]
    root = lax.rsqrt(jnp.mean(x * x, axis=-1, keepdims=True) + EPSILON)
    low = (x * root * gain).astype(BF)
    a.low[...] = low
    k = rotate(mm(low, a.w_in[:, z.width : 2 * z.width]), a.cq[...], a.sq[...])
    v = mm(low, a.w_in[:, 2 * z.width :])
    for n in range(GROUPS):
        for j, part in enumerate(joined(window(k, n, False), window(v, n, True))):
            a.kv_out[n, :, 128 * j : 128 * (j + 1)] = part.astype(BF)
    far = {}
    for dg in (2, 1, 3):
        t = net.up(net.g, dg, GROUPS)
        far[dg] = net.push(a.kv_out.at[t], a.kv.at[net.b], net.near(dg=dg))
    a.kv[net.b] = a.kv_out[net.g]
    q = rotate(mm(low, a.w_in[:, : z.width]), a.cq[...], a.sq[...])
    for n in range(GROUPS):
        put_packed(a.q_out.at[n], window(q, n, False))
    moved = []
    for dg in (2, 1, 3):
        t = net.up(net.g, dg, GROUPS)
        moved.append(net.push(a.q_out.at[t], a.q.at[net.g], net.near(dg=dg)))
    a.q[net.g] = a.q_out[net.g]
    act(at.sent)
    for dg in (0, 1, 3, 2):
        if dg:
            far[dg].wait_recv()
        place = a.kv.at[net.down(net.g, dg, GROUPS) * z.splits + net.s]
        for ds in range(1, z.splits):
            moved.append(net.push(place, place, net.near(ds=ds)))
    for made in moved:
        made.wait_recv()
    act(at.mid)
    q_masks = [m.astype(BF) for m in head_masks(0)]
    v_masks = head_masks(HD)
    first = net.take(GROUPS)
    chunk = z.nb * z.rows if z.nb * z.rows <= 1024 else 512
    for i in range(GROUPS):
        own = unpack(a.q[i]).astype(BF)
        q3 = jnp.concatenate([own * m for m in q_masks], axis=0)
        row = places(net, i, i + 1)
        peak = total = out = None
        for start in range(0, (i + 1) * z.splits * z.rows, chunk):
            keys = min(chunk, (i + 1) * z.splits * z.rows - start)
            kv = a.kv[start // z.rows : (start + keys) // z.rows].reshape(keys, 384)
            mask = lanes((1, keys)) + start <= row
            scores = jnp.where(mask, mm(q3, kv[:, 0:256], 1, 1) * SCALE, NEGATIVE)
            top = jnp.max(scores, axis=-1, keepdims=True)
            top = top if peak is None else jnp.maximum(top, peak)
            weights = jnp.exp(scores - top)
            more = jnp.sum(weights, axis=-1, keepdims=True)
            product = mm(weights.astype(BF), kv[:, 128:384])
            if peak is None:
                total, out = more, product
            else:
                factor = jnp.exp(peak - top)
                total, out = total * factor + more, out * factor + product
            peak = top
        out = out / total
        merged = sum(out[z.rows * j : z.rows * (j + 1)] * v_masks[j] for j in range(3))
        a.o[i] = merged
        put_packed(a.o_out.at[i], pltpu.roll(merged, 256 - HD, 1))
        a.lse[i] = peak + jnp.log(total)
        device = net.device(net.y, net.c, i, net.s)
        net.push_or_keep(
            a.o_out.at[i], a.ret.at[net.g], device, net.g == i, first + i, first + net.g
        )
    act(at.out)
    middle = x
    for n in range(GROUPS):
        net.arrived(a.ret.at[n], first + n)
        got = unpack(a.ret[n]).astype(BF)
        middle = middle + mm(got[:, 0:192], a.w_out[192 * n : 192 * (n + 1), :])
    a.middle[...] = middle
    return middle


def attend_back(net, a, x, dm, at):
    z = net.z
    branch = dm.astype(BF)
    grad_att = mm(branch, a.w_out[...], 1, 1)
    for n in range(GROUPS):
        put_packed(a.do_out.at[n], window(grad_att, n, False))
    moved = []
    for dg in (2, 1, 3):
        t = net.up(net.g, dg, GROUPS)
        moved.append(net.push(a.do_out.at[t], a.do.at[net.g], net.near(dg=dg)))
    a.do[net.g] = a.do_out[net.g]
    act(at.back_sent)
    per = 192 // z.shard
    for n in range(GROUPS):
        part = mm(unpack(a.ret[n]).astype(BF), branch, 0, 0)[0:192]
        for k in range(per):
            a.gout[n * per + k] = part[k * z.shard : (k + 1) * z.shard].astype(BF)
    q_masks = head_masks(0)
    v_masks = head_masks(HD)
    for i in range(GROUPS):
        own = unpack(a.q[i]).astype(BF)
        for j in range(3):
            a.q3[i, z.rows * j : z.rows * (j + 1)] = own * q_masks[j].astype(BF)
    a.dq_sum[...] = jnp.zeros(a.dq_sum.shape, F32)
    for made in moved:
        made.wait_recv()
    for i in range(GROUPS):
        own = pltpu.roll(unpack(a.do[i]), HD, 1)
        product = own * a.o[i]
        for j in range(3):
            span = slice(z.rows * j, z.rows * (j + 1))
            a.do3[i, span] = (own * v_masks[j]).astype(BF)
            a.delta[i, span] = jnp.sum(product * v_masks[j], axis=-1, keepdims=True)
    first_q, first_kv = net.take(GROUPS), net.take(GROUPS)
    between = {}
    size = 3 * z.rows

    def onward(i):
        total = a.dkv_out[i * z.splits + net.s].astype(F32)
        for ds, made in between[i]:
            made.wait_recv()
            total = total + a.dkv_got[ds - 1, i].astype(F32)
        a.dkv_sum[i] = total.astype(BF)
        device = net.device(net.y, net.c, i, net.s)
        net.push_or_keep(
            a.dkv_sum.at[i], a.dkv.at[net.g], device, net.g == i, first_kv + i, first_kv + net.g
        )

    some = min(4, z.splits)
    keys = some * z.rows
    for n in range(GROUPS):
        spans = [(n, GROUPS)] if keys <= 256 else [(i, i + 1) for i in range(n, GROUPS)]
        for block in range(n * z.splits, (n + 1) * z.splits, some):
            kv = a.kv[block : block + some].reshape(keys, 384)
            key, value = kv[:, 0:256], kv[:, 128:384]
            dk = jnp.zeros((keys, 256), F32)
            dv = jnp.zeros((keys, 256), F32)
            for lo, hi in spans:
                rows = (hi - lo) * size
                q3 = a.q3[lo:hi].reshape(rows, 256)
                do3 = a.do3[lo:hi].reshape(rows, 256)
                lse = a.lse[lo:hi].reshape(rows, 1)
                delta = a.delta[lo:hi].reshape(rows, 1)
                mask = lanes((1, keys)) + block * z.rows <= places(net, lo, hi)
                scores = mm(q3, key, 1, 1) * SCALE
                weights = jnp.where(mask, jnp.exp(scores - lse), 0.0)
                grad_scores = (weights * (mm(do3, value, 1, 1) - delta)).astype(BF)
                more = mm(grad_scores, key).reshape((hi - lo) * 3, z.rows, 256)
                for i in range(lo, hi):
                    at_i = 3 * (i - lo)
                    a.dq_sum[i] += sum(more[at_i + j] * q_masks[j] for j in range(3))
                dk = dk + mm(grad_scores, q3, 0, 0)
                dv = dv + mm(weights.astype(BF), do3, 0, 0)
            for j, part in enumerate(joined(dk * SCALE, dv)):
                a.dkv_out[block : block + some, :, 128 * j : 128 * (j + 1)] = part.astype(
                    BF
                ).reshape(some, z.rows, 128)
        between[n] = []
        for ds in range(1, z.splits):
            t = net.up(net.s, ds, z.splits)
            made = net.push(a.dkv_out.at[n * z.splits + t], a.dkv_got.at[ds - 1, n], net.near(ds=ds))
            between[n].append((ds, made))
        put_packed(a.dq_out.at[n], a.dq_sum[n] * SCALE)
        device = net.device(net.y, net.c, n, net.s)
        net.push_or_keep(
            a.dq_out.at[n], a.dq.at[net.g], device, net.g == n, first_q + n, first_q + net.g
        )
        if n:
            onward(n - 1)
        act(at.back.get(n, ()))
    onward(GROUPS - 1)
    act(at.back_out)
    own = a.low[...]
    grad_low = jnp.zeros((z.rows, z.width), F32)
    from_zero = lanes((1, 256)) < 192

    leaving = []

    def weigh(piece, start):
        slot = len(leaving) % 2
        if len(leaving) >= 2:
            leaving[-2].wait()
        part = mm(own, piece, 0, 0)
        for k in range(z.shards):
            a.gin_part[slot, k] = part[k * z.shard : (k + 1) * z.shard].astype(BF)
        place = a.gin.at[:, :, start : start + 384]
        leaving.append(pltpu.make_async_copy(a.gin_part.at[slot], place, a.gin_sem.at[slot]))
        leaving[-1].start()
        return mm(piece, a.w_in[:, start : start + 384], 1, 1)

    def turned(columns, n):
        cut = slice(192 * n, 192 * n + 384)
        return rotate_back(jnp.concatenate(columns, axis=1), a.cq[:, cut], a.sq[:, cut]).astype(BF)

    for n in range(0, GROUPS, 2):
        net.arrived(a.dq.at[n], first_q + n)
        net.arrived(a.dq.at[n + 1], first_q + n + 1)
        columns = unwindow(unpack(a.dq[n]), unpack(a.dq[n + 1]))
        grad_low = grad_low + weigh(turned(columns, n), 192 * n)
    for n in range(0, GROUPS, 2):
        pair = []
        for m in (n, n + 1):
            net.arrived(a.dkv.at[m], first_kv + m)
            both = a.dkv[m].astype(F32)
            key = jnp.where(from_zero, both[:, :256], 0.0)
            value = jnp.where(from_zero, pltpu.roll(both[:, 128:], 256 - HD, 1), 0.0)
            pair.append((key, value))
        columns = unwindow(pair[0][0], pair[1][0])
        grad_low = grad_low + weigh(turned(columns, n), z.width + 192 * n)
        columns = unwindow(pair[0][1], pair[1][1])
        piece = jnp.concatenate(columns, axis=1).astype(BF)
        grad_low = grad_low + weigh(piece, 2 * z.width + 192 * n)
    for copy in leaving[-2:]:
        copy.wait()
    gain = rows_of(a.small[...])[0:1]
    root = lax.rsqrt(jnp.mean(x * x, axis=-1, keepdims=True) + EPSILON)
    place = (lanes((z.rows, 128)) == 16).astype(F32).astype(BF)
    high, rest = split(grad_low * x * root)
    a.gsmall[...] += mm(high, place, 0, 0) + mm(rest, place, 0, 0)
    return dm + norm_grad(x, root, gain, grad_low)


class Mixing:
    def __init__(self, z, middle, small, plan):
        table = rows_of(small)
        self.gain, self.consts = table[1:2], (table[2:3], table[3:4])
        self.root = lax.rsqrt(jnp.mean(middle * middle, axis=-1, keepdims=True) + EPSILON)
        self.normed = middle * self.root * self.gain
        self.low, self.rest = split(self.normed)
        expert_of, slot_of = lanes((z.rows, 128)).astype(F32), lanes((z.rows, z.count)).astype(F32)
        self.picks = [(expert_of == plan[:, j : j + 1]).astype(F32) for j in range(TOP)]
        self.chosen = [(slot_of == plan[:, TOP + j : TOP + j + 1]).astype(F32) for j in range(TOP)]
        self.select = (self.chosen[0] + self.chosen[1]).astype(BF)
        self.small = small

    def share(self):
        self.product = mm(self.low, self.small)
        shares = self.product + mm(self.rest, self.small)
        self.shares = []
        for index in range(2):
            one, two = lane_of(shares, 12 + 2 * index), lane_of(shares, 13 + 2 * index)
            peak = jnp.maximum(one, two)
            one, two = jnp.exp(one - peak), jnp.exp(two - peak)
            self.shares.append((one / (one + two), two / (one + two)))

    def gate(self, logits):
        values = [jnp.sum(p * logits, axis=-1, keepdims=True) for p in self.picks]
        peak = jnp.maximum(values[0], values[1])
        powers = [jnp.exp(v - peak) for v in values]
        total = powers[0] + powers[1]
        self.gates = [p / total for p in powers]
        self.combine = self.gates[0] * self.chosen[0] + self.gates[1] * self.chosen[1]

    def weigh(self):
        spread = self.gates[0] * self.picks[0] + self.gates[1] * self.picks[1]
        self.const_weights = [lane_of(spread, NF + 2 + index) for index in range(2)]
        self.normed_weight = lane_of(spread, NF + 1)
        for index in range(2):
            self.normed_weight = (
                self.normed_weight + self.const_weights[index] * self.shares[index][0]
            )


class ExpertRun:
    def __init__(self, net, e, rows_ref, all_ref, chunk):
        self.net, self.e, self.rows_ref, self.all_ref, self.chunk = net, e, rows_ref, all_ref, chunk
        self.mine = net.y * GROUPS + net.g

    def send(self):
        net, z = self.net, self.net.z
        steps = [(dy, dg) for dg in (2, 1, 3, 0) for dy in range(z.hh) if dy or dg]
        first = []
        for dy, dg in steps:
            target = net.up(net.y, dy, z.hh) * GROUPS + net.up(net.g, dg, GROUPS)
            place = self.all_ref.at[net.q, self.mine]
            first.append(net.push(self.rows_ref.at[target], place, net.near(dy=dy, dg=dg)))
        self.all_ref[net.q, self.mine] = self.rows_ref[self.mine]
        self.sources = [(0, 0, None)] + [
            (dy, dg, made) for (dy, dg), made in zip(reversed(steps), reversed(first))
        ]

    def relay(self, while_first):
        net, z = self.net, self.net.z
        self.slots = []
        self.aside, self.across = [[] for _ in range(z.splits)], [[] for _ in range(z.splits)]
        for k, (dy, dg, made) in enumerate(self.sources):
            if made is not None:
                made.wait_recv()
            self.slots.append(net.down(net.y, dy, z.hh) * GROUPS + net.down(net.g, dg, GROUPS))
            place = self.all_ref.at[net.q, self.slots[k]]
            for ds in range(1, z.splits):
                self.aside[ds].append(net.push(place, place, net.near(ds=ds)))
            self.across[0].append(net.push(place, place, net.near(dc=1)))
            if k == 0:
                while_first()

    def compute(self):
        net, z, e = self.net, self.net.z, self.e
        block = (z.experts, SLOT, z.width)
        e.base[...] = self.chunk(net.q).reshape(block)
        other = 1 - net.c
        for ds in range(1, z.splits):
            s = net.down(net.s, ds, z.splits)
            for k, made in enumerate(self.aside[ds]):
                made.wait_recv()
                place = self.all_ref.at[net.c * z.splits + s, self.slots[k]]
                self.across[ds].append(net.push(place, place, net.near(dc=1)))
        self.halves = {}
        for ds in range(z.splits):
            s = net.down(net.s, ds, z.splits)
            for made in self.across[ds]:
                made.wait_recv()
            e.part[ds] = self.chunk(other * z.splits + s).astype(BF).reshape(block)
            to_core = net.push(e.part.at[ds], e.got.at[ds], net.near(dc=1))
            if ds == 0:
                self.first_core = to_core
                continue
            kept = self.chunk(net.c * z.splits + s)
            to_core.wait_recv()
            net.sent = [made for made in net.sent if made is not to_core]
            to_core.wait_send()
            e.part[ds] = (kept.reshape(block) + e.got[ds].astype(F32)).astype(BF)
            for dy in reversed(range(z.hh)):
                span = pl.ds(net.up(net.y, dy, z.hh) * GROUPS, GROUPS)
                device = net.near(ds=z.splits - ds)
                made = net.push(e.part.at[ds, span], e.side_got.at[ds - 1, span], device)
                self.halves[ds, dy] = made

    def give_back(self):
        net, z, e = self.net, self.net.z, self.e
        self.first_core.wait_recv()
        e.base[...] += e.got[0].astype(F32)
        self.last = []
        for dy in reversed(range(z.hh)):
            y = net.up(net.y, dy, z.hh)
            span = pl.ds(y * GROUPS, GROUPS)
            total = e.base[span]
            for ds in range(1, z.splits):
                self.halves[ds, dy].wait_recv()
                total = total + e.side_got[ds - 1, span].astype(F32)
            e.sum[span] = total.astype(BF)
            for dg in (2, 1, 3, 0):
                if dy or dg:
                    src = e.sum.at[y * GROUPS + net.up(net.g, dg, GROUPS)]
                    made = net.push(src, e.back.at[self.mine], net.near(dy=dy, dg=dg))
                    self.last.append(made)
        e.back[self.mine] = e.sum[self.mine]

    def wait(self):
        for made in self.last:
            made.wait_recv()


def weight_of(z, e, w):
    e.wait_weight(w)
    ref = e.weights[w]
    if z.drow % 16 == 0:
        return ref[...].reshape(z.width, z.ffp)
    return jnp.concatenate([ref[n].astype(F32) for n in range(z.nb)], axis=0).astype(BF)


def held_weights(net, e):
    held = {}

    def weight(w):
        if w not in held:
            held[w] = weight_of(net.z, e, w)
        return held[w]

    return weight


def forward_chunk(net, e, weight):
    z = net.z

    def chunk(part):
        rows = e.all[part].reshape(z.count, z.width)
        gate, up = mm(rows, weight(0)), mm(rows, weight(1))
        e.gate[part], e.up[part] = gate.astype(BF), up.astype(BF)
        hidden = (gate / (1.0 + jnp.exp(-gate)) * up).astype(BF)
        return mm(hidden, weight(2), 1, 1)

    return chunk


def backward_chunk(net, e, weight):
    z = net.z

    def chunk(part):
        weight(0), weight(1)
        rows = e.dall[part].reshape(z.count, z.width)
        grad_hidden = mm(rows, weight(2))
        gate, up = e.gate[part].astype(F32), e.up[part].astype(F32)
        sig = 1.0 / (1.0 + jnp.exp(-gate))
        silu = gate * sig
        e.hid[part] = (silu * up).astype(BF)
        up_low = (grad_hidden * silu).astype(BF)
        gate_low = (grad_hidden * up * (sig * (1.0 + gate * (1.0 - sig)))).astype(BF)
        e.du[part], e.dg[part] = up_low, gate_low
        return mm(gate_low, weight(0), 1, 1) + mm(up_low, weight(1), 1, 1)

    return chunk


def weight_grads(net, e):
    z = net.z
    step = min(4, z.nq)
    for w, one, two in ((0, e.all, e.dg), (1, e.all, e.du), (2, e.dall, e.hid)):
        product = None
        for first in range(0, z.nq, step):
            span = slice(first, first + step)
            left = one[span].reshape(step * z.count, z.width)
            more = mm(left, two[span].reshape(step * z.count, z.ffp), 0, 0)
            product = more if product is None else product + more
        for n in range(z.nb):
            e.gw[w][n] = product[n * z.drow : (n + 1) * z.drow].astype(BF)


def put_rows(mixing, e):
    e.rows[...] = mm(mixing.select, mixing.low, 0, 0).astype(BF).reshape(e.rows.shape)


def put_grad_rows(mixing, e, high, rest):
    weight_high, weight_rest = split(mixing.combine)
    slot_grad = mm(weight_high, high, 0, 0) + mm(weight_rest, high, 0, 0)
    slot_grad = slot_grad + mm(weight_high, rest, 0, 0)
    e.rows[...] = slot_grad.astype(BF).reshape(e.rows.shape)


def mixture(z, mixing, middle, results):
    high, rest = split(mixing.combine)
    mixed = mm(high, results) + mm(rest, results) + mixing.normed_weight * mixing.normed
    for index in range(2):
        weight = mixing.const_weights[index] * mixing.shares[index][1]
        mixed = mixed + weight * mixing.consts[index]
    return middle + mixed


def mixture_grads(z, mixing, grad, grad_logits, high, rest, results):
    where_lane = lanes((z.rows, 128))
    along = mm(high, results, 1, 1) + mm(rest, results, 1, 1)
    normed_dot = jnp.sum(grad * mixing.normed, axis=-1, keepdims=True)
    const_dots = [jnp.sum(grad * c, axis=-1, keepdims=True) for c in mixing.consts]
    gate_grads = []
    for j in range(TOP):
        value = jnp.sum(mixing.chosen[j] * along, axis=-1, keepdims=True)
        value = value + lane_of(mixing.picks[j], NF + 1) * normed_dot
        for index in range(2):
            share = mixing.shares[index]
            value = value + lane_of(mixing.picks[j], NF + 2 + index) * (
                share[0] * normed_dot + share[1] * const_dots[index]
            )
        gate_grads.append(value)
    inner = mixing.gates[0] * gate_grads[0] + mixing.gates[1] * gate_grads[1]
    logit_grad = grad_logits
    for j in range(TOP):
        logit_grad = logit_grad + mixing.picks[j] * (mixing.gates[j] * (gate_grads[j] - inner))
    column = jnp.zeros((z.rows, 128), F32)
    const_columns = jnp.zeros((z.rows, 128), F32)
    for index in range(2):
        share, weight = mixing.shares[index], mixing.const_weights[index]
        one, two = weight * normed_dot, weight * const_dots[index]
        mean = share[0] * one + share[1] * two
        column = column + jnp.where(where_lane == 12 + 2 * index, share[0] * (one - mean), 0.0)
        column = column + jnp.where(where_lane == 13 + 2 * index, share[1] * (two - mean), 0.0)
        const_columns = const_columns + jnp.where(where_lane == 18 + index, weight * share[1], 0.0)
    both_high, both_rest = split(logit_grad + column)
    grad_normed = mm(both_high, mixing.small, 1, 1) + mm(both_rest, mixing.small, 1, 1)
    grad_normed = grad_normed + mixing.normed_weight * grad
    gsmall = mm(mixing.low, both_high, 0, 0) + mm(mixing.low, both_rest, 0, 0)
    gsmall = gsmall + mm(mixing.rest, column.astype(BF), 0, 0)
    const_high, const_rest = split(const_columns)
    gsmall = gsmall + mm(high, const_high, 0, 0) + mm(rest, const_high, 0, 0)
    return logit_grad, grad_normed, gsmall + mm(high, const_rest, 0, 0)


def middle_grads(z, mixing, e, middle, grad, grad_normed, gsmall):
    grad_normed = grad_normed + mm(mixing.select, e.back[...].reshape(z.count, z.width))
    place = (lanes((z.rows, 128)) == 17).astype(F32).astype(BF)
    high, rest = split(grad_normed * middle * mixing.root)
    e.gsmall[...] = gsmall + mm(high, place, 0, 0) + mm(rest, place, 0, 0)
    return grad + norm_grad(middle, mixing.root, mixing.gain, grad_normed)


def experts(net, e, middle, logits_in, at):
    z = net.z
    mixing = Mixing(z, middle, e.small[...], e.plan[...])
    put_rows(mixing, e)
    run = ExpertRun(net, e, e.rows, e.all, forward_chunk(net, e, held_weights(net, e)))

    def while_first():
        mixing.share()
        logits = mixing.product + logits_in
        e.logits[...] = logits
        mixing.gate(logits)
        mixing.weigh()
        act(at.rows)

    run.send()
    run.relay(while_first)
    run.compute()
    act(at.side)
    run.give_back()
    act(at.last)
    run.wait()
    e.results[...] = e.back[...]
    return mixture(z, mixing, middle, e.back[...].reshape(z.count, z.width))


def experts_back(net, e, middle, grad, grad_logits, at):
    z = net.z
    mixing = Mixing(z, middle, e.small[...], e.plan[...])
    mixing.gate(e.logits[...])
    high, rest = split(grad)
    put_grad_rows(mixing, e, high, rest)
    run = ExpertRun(net, e, e.rows, e.dall, backward_chunk(net, e, held_weights(net, e)))
    made = []

    def while_first():
        mixing.share()
        mixing.weigh()
        results = e.results[...].reshape(z.count, z.width)
        made.extend(mixture_grads(z, mixing, grad, grad_logits, high, rest, results))
        act(at.rows_back)

    run.send()
    run.relay(while_first)
    run.compute()
    weight_grads(net, e)
    act(at.side_back)
    run.give_back()
    act(at.last_back)
    run.wait()
    logit_grad, grad_normed, gsmall = made
    return middle_grads(z, mixing, e, middle, grad, grad_normed, gsmall), logit_grad


def experts_both(net, e, later, middle, logits_in, grad, grad_logits, at):
    z = net.z
    mixing = Mixing(z, middle, e.small[...], e.plan[...])
    put_rows(mixing, e)
    weight = held_weights(net, e)
    run = ExpertRun(net, e, e.rows, e.all, forward_chunk(net, e, weight))
    back = ExpertRun(net, later, later.rows, e.dall, backward_chunk(net, e, weight))
    run.send()
    act(at.rows)
    mixing.share()
    mixing.gate(mixing.product + logits_in)
    high, rest = split(grad)
    put_grad_rows(mixing, later, high, rest)
    back.send()
    mixing.weigh()
    run.relay(lambda: None)
    run.compute()
    back.relay(lambda: None)
    back.compute()
    run.give_back()
    weight_grads(net, e)
    act(at.side_back)
    back.give_back()
    act(at.last_back)
    run.wait()
    results = e.back[...].reshape(z.count, z.width)
    result = mixture(z, mixing, middle, results)
    made = mixture_grads(z, mixing, grad, grad_logits, high, rest, results)
    back.wait()
    logit_grad, grad_normed, gsmall = made
    return result, middle_grads(z, mixing, later, middle, grad, grad_normed, gsmall), logit_grad


def attend_kept(z):
    return dict(
        middle=struct((z.rows, z.width), F32),
        low=struct((z.rows, z.width), BF),
        q=struct((GROUPS, 3 * z.rows // 2, 128), BF),
        kv=struct((z.nb, z.rows, 384), BF),
        o=struct((GROUPS, z.rows, 256), F32),
        lse=struct((GROUPS, 3 * z.rows, 1), F32),
        ret=struct((GROUPS, 3 * z.rows // 2, 128), BF),
    )


def experts_kept(z):
    block = (z.experts, SLOT, z.width)
    return dict(
        logits=struct((z.rows, 128), F32),
        results=struct(block, BF),
        all=struct((z.nq,) + block, BF),
        gate=struct((z.nq, z.count, z.ffp), BF),
        up=struct((z.nq, z.count, z.ffp), BF),
    )


def attend_scratch(z):
    return dict(
        q_out=pltpu.VMEM((GROUPS, 3 * z.rows // 2, 128), BF),
        kv_out=pltpu.VMEM((GROUPS, z.rows, 384), BF),
        o_out=pltpu.VMEM((GROUPS, 3 * z.rows // 2, 128), BF),
    )


def attend_back_scratch(z, own_output=True):
    one = pltpu.VMEM((GROUPS, 3 * z.rows // 2, 128), BF)
    three = pltpu.VMEM((GROUPS, 3 * z.rows, 256), BF)
    two = pltpu.VMEM((GROUPS, z.rows, 384), BF)
    made = dict(
        do_out=one,
        do=one,
        dq_out=one,
        dq=one,
        dkv_out=pltpu.VMEM((z.nb, z.rows, 384), BF),
        dkv_got=pltpu.VMEM((z.splits - 1, GROUPS, z.rows, 384), BF),
        dkv_sum=two,
        dkv=two,
        q3=three,
        do3=three,
        dq_sum=pltpu.VMEM((GROUPS, z.rows, 256), F32),
        gin_part=pltpu.VMEM((2, z.shards, z.shard, 384), BF),
        gin_sem=pltpu.SemaphoreType.DMA((2,)),
        delta=pltpu.VMEM((GROUPS, 3 * z.rows, 1), F32),
    )
    if not own_output:
        del made["dkv_out"]
    return made


def experts_scratch(z):
    block = (z.experts, SLOT, z.width)
    flat = pltpu.VMEM((z.splits,) + block, BF)
    return dict(
        rows=pltpu.VMEM(block, BF),
        part=flat,
        got=flat,
        side_got=pltpu.VMEM((z.splits - 1,) + block, BF),
        base=pltpu.VMEM(block, F32),
        sum=pltpu.VMEM(block, BF),
        back=pltpu.VMEM(block, BF),
    )


def experts_back_scratch(z, both=True):
    part = pltpu.VMEM((z.nq, z.count, z.ffp), BF)
    block = (z.experts, SLOT, z.width)
    made = dict(dall=pltpu.VMEM((z.nq,) + block, BF), hid=part)
    if both:
        made.update(dict(dg=part, du=part))
    return made


def scratch_of(kept):
    return {name: pltpu.VMEM(v.shape, v.dtype) for name, v in kept.items()}


def view(held, **more):
    return Names(**{**held.__dict__, **more})


def landing(z):
    return struct((z.nb, z.drow, z.ffp), BF)


def near_landing(z):
    return struct((GROUPS, z.drow, z.ffp), BF)


def grad_landing(z):
    return struct((2, z.drow, z.hidden), BF)


def nothing():
    pass


CUT = 384


def in_vmem(arrays):
    return {name: (array, VMEM) for name, array in arrays.items()}


def in_place(arrays):
    return {name: (array, ANY) for name, array in arrays.items()}


def weight_pieces(z, owns, wholes):
    widths = (3 * z.width, z.width)
    return [
        (owns[which], wholes[which], first, columns)
        for which, first, columns in cuts_of((0, 1), widths, CUT)
    ]


def pieces_sems(z, pieces):
    return pieces * (2 + z.splits + z.hh)


def eye(size):
    shape = (size, size)
    return lax.broadcasted_iota(jnp.int32, shape, 0) == lax.broadcasted_iota(jnp.int32, shape, 1)


def upright(row, same):
    return jnp.sum(jnp.where(same, row, 0.0), axis=1, keepdims=True)


def plan_of(z, routes, order):
    same, lane = eye(z.rows), lanes((z.rows, 128))
    ids, ranks = routes.astype(F32), order.astype(F32)
    plan = jnp.zeros((z.rows, 128), F32)
    for j in range(TOP):
        own, rank = upright(ids[j : j + 1], same), upright(ranks[j : j + 1], same)
        before = jnp.zeros((z.rows, 1), F32)
        for k in range(TOP):
            counts = (own == ids[k : k + 1]) & (ranks[k : k + 1] < rank)
            before = before + jnp.sum(counts.astype(F32), axis=1, keepdims=True)
        slot = jnp.where((own < NF) & (before < CAP), own * SLOT + before, -1.0)
        plan = plan + jnp.where(lane == j, own, 0.0) + jnp.where(lane == TOP + j, slot, 0.0)
    return plan


def grid_of(z):
    return (z.hh, 2, 2, 2, z.splits, z.shard)


def gather_first(z, large, little):
    def body(k, net):
        owns, wholes = (k.attn_in.at[0], k.attn_out.at[0]), (k.w_in, k.w_out)
        pieces = weight_pieces(z, owns, wholes)
        gather = Gather(net, pieces, k.own)
        gather.step()
        moves = [
            NearWeights(net, k.expert_0, 0, k.near_0),
            NearWeights(net, k.expert_1, 0, k.near_1),
            NearWeights(net, k.expert_2, 0, k.near_2),
        ]
        same, lane = eye(z.shard), lanes((z.shard, 128))
        for layer in range(LAYERS):
            rows = [k.router[n][layer : layer + 1] for n in range(NE)]
            rows += [k.mix[layer][n : n + 1] for n in range(4)]
            rows += [k.gains[layer][n : n + 1] for n in range(2)]
            rows += [k.consts[layer][n : n + 1] for n in range(2)]
            table = jnp.zeros((z.shard, 128), F32)
            for n, row in enumerate(rows):
                table = table + jnp.where(lane == n, upright(row.astype(F32), same), 0.0)
            k.small_own[layer] = table.astype(BF)
        smalls = [
            (k.small_own.at[layer], whole, 0, 128)
            for layer, whole in enumerate((k.small_0, k.small_1))
        ]
        other = Gather(net, smalls, k.own_too)
        other.step()
        gather.step()
        moves[0].start()
        for layer, plan in enumerate((k.plan_0, k.plan_1)):
            plan[...] = plan_of(z, k.routes[layer], k.order[layer])
        same, lane = eye(z.rows), lanes((z.rows, 128))
        table = jnp.zeros((z.rows, 128), F32)
        for n in range(NE):
            table = table + jnp.where(lane == n, upright(k.prev[n : n + 1], same), 0.0)
        k.logits[...] = table
        gather.step()
        other.step()
        moves[1].start()
        moves[2].start()
        row = lax.broadcasted_iota(jnp.int32, (z.rows, 1), 0) + net.b * z.rows
        angles = row.astype(F32) * k.freqs[...]
        cosine, sine = jnp.cos(angles), jnp.sin(angles)
        sine = jnp.where(lane % HD < HD // 2, -sine, sine)
        for n in range(z.width // 128):
            k.cq[:, 128 * n : 128 * (n + 1)] = cosine
            k.sq[:, 128 * n : 128 * (n + 1)] = sine
        for _ in range(3):
            gather.step()
            other.step()
        other.step()
        for move in moves:
            move.wait()

    ins = {**in_place(large), **in_vmem(little)}
    outs = in_place(
        dict(
            w_in=struct(grid_of(z) + (3 * z.width,), BF),
            w_out=struct(grid_of(z) + (z.width,), BF),
            small_0=struct(grid_of(z) + (128,), BF),
            small_1=struct(grid_of(z) + (128,), BF),
            near_0=near_landing(z),
            near_1=near_landing(z),
            near_2=near_landing(z),
        )
    )
    table, wide = struct((z.rows, 128), F32), struct((z.rows, z.width), F32)
    outs.update(in_vmem(dict(plan_0=table, plan_1=table, logits=table, cq=wide, sq=wide)))
    pieces = len(weight_pieces(z, (0, 0), (0, 0)))
    scratch = dict(
        small_own=pltpu.VMEM((LAYERS, z.shard, 128), BF),
        own=pltpu.SemaphoreType.DMA((pieces,)),
        own_too=pltpu.SemaphoreType.DMA((LAYERS,)),
    )
    return launch(body, 0, z, ins, outs, scratch, pieces_sems(z, pieces + LAYERS) + 3 * GROUPS)


def layer_sems(z):
    attention = 6 + GROUPS * (z.splits - 1) + GROUPS
    expert = (z.experts - 1) * 2 + z.experts * (2 * z.splits - 1) + z.splits + z.hh * z.splits
    back = 3 + GROUPS * (z.splits - 1) + 2 * GROUPS
    return attention, expert, back


def waiting(*moves):
    held = list(moves)

    def wait(w):
        if held[w] is not None:
            held[w].wait()
            held[w] = None

    return wait


def layer_forward(z, values, tables, weights, near, shards, parts):
    def body(k, net):
        owns, wholes = (k.attn_in.at[1], k.attn_out.at[1]), (k.next_in, k.next_out)
        gather = Gather(net, weight_pieces(z, owns, wholes), k.own)
        far = [
            FarWeights(net, k.expert_0, 0, k.near_0, k.weight_0),
            FarWeights(net, k.expert_1, 0, k.near_1, k.weight_1),
            FarWeights(net, k.expert_2, 0, k.near_2, k.weight_2),
        ]
        ahead = [
            NearWeights(net, k.expert_0, 1, k.next_0),
            NearWeights(net, k.expert_1, 1, k.next_1),
            NearWeights(net, k.expert_2, 1, k.next_2),
        ]
        at = Beside(
            start=[gather.step, far[0].start],
            sent=[gather.step, far[1].start],
            mid=[gather.step],
            out=[gather.step],
            rows=[far[2].start, ahead[0].start],
            side=[gather.step, ahead[1].start],
            last=[gather.step, ahead[2].start],
        )
        middle = attend(net, k, k.tokens[...].astype(F32), at)
        e = view(k, weights=(k.weight_0, k.weight_1, k.weight_2), wait_weight=waiting(*far))
        k.state[...] = experts(net, e, middle, k.logits_in[...], at)
        for move in ahead:
            move.wait()

    ins = {**in_vmem(values), **in_vmem(tables), **in_vmem(weights)}
    ins.update({**in_place(shards), **in_place(parts), **in_place(near)})
    whole = landing(z)
    outs = dict(state=struct((z.rows, z.width), F32))
    outs.update(dict(weight_0=whole, weight_1=whole, weight_2=whole))
    outs = in_vmem({**outs, **attend_kept(z), **experts_kept(z)})
    ahead = dict(
        next_in=struct(grid_of(z) + (3 * z.width,), BF),
        next_out=struct(grid_of(z) + (z.width,), BF),
        next_0=near_landing(z),
        next_1=near_landing(z),
        next_2=near_landing(z),
    )
    outs.update(in_place(ahead))
    pieces = len(weight_pieces(z, (0, 0), (0, 0)))
    own = dict(own=pltpu.SemaphoreType.DMA((pieces,)))
    scratch = {**attend_scratch(z), **experts_scratch(z), **own}
    attention, expert, _ = layer_sems(z)
    count = attention + expert + pieces_sems(z, pieces) + 3 * z.nb + 3 * GROUPS
    return launch(body, 1, z, ins, outs, scratch, count)


def back_outputs(z, more):
    outs = dict(
        grad=struct((z.rows, z.width), F32),
        grad_logits=struct((z.rows, 128), F32),
        gout=struct((z.shards, z.shard, z.width), BF),
        gsmall=struct((z.width, 128), F32),
        gw_2=landing(z),
    )
    rest = dict(
        gin=struct((z.shards, z.shard, 3 * z.width), BF),
        grad_0=grad_landing(z),
        grad_1=grad_landing(z),
    )
    return {**in_vmem({**outs, **more}), **in_place(rest)}


def layer_both(z, values, tables, weights, near, parts):
    together = z.nb <= 8

    def body(k, net):
        far = [
            FarWeights(net, k.expert_0, 1, k.near_0, k.weight_0),
            FarWeights(net, k.expert_1, 1, k.near_1, k.weight_1),
            FarWeights(net, k.expert_2, 1, k.near_2, k.weight_2),
        ]
        grads = [GradMove(net, k.gw_0, k.grad_0), GradMove(net, k.gw_1, k.grad_1)]
        at = Beside(
            start=[far[0].start],
            sent=[far[1].start],
            rows=[far[2].start],
            side_back=[grads[0].near],
            last_back=[grads[0].far],
            back_sent=[grads[1].near],
            back_out=[grads[1].far],
        )
        middle = attend(net, k, k.state[...], at)
        e = view(
            k,
            weights=(k.weight_0, k.weight_1, k.weight_2),
            gw=(k.gw_0, k.gw_1, k.gw_2),
            wait_weight=waiting(*far),
            dg=k.gate,
            du=k.up,
        )
        none = jnp.zeros((z.rows, 128), F32)
        grad = k.cotangent[...].astype(F32)
        if together:
            later = view(
                e,
                rows=k.rows_2,
                part=k.part_2,
                got=k.got_2,
                side_got=k.side_got_2,
                base=k.base_2,
                sum=k.sum_2,
                back=k.back_2,
            )
            result, dm, grad_logits = experts_both(
                net, e, later, middle, k.logits_in[...], grad, none, at
            )
        else:
            result = experts(net, e, middle, k.logits_in[...], at)
            net.settle()
            dm, grad_logits = experts_back(net, e, k.middle[...], grad, none, at)
        k.output[...] = result.astype(BF)
        k.grad_logits[...] = grad_logits
        net.settle()
        k.grad[...] = attend_back(net, view(k, dkv_out=k.kv), k.state[...], dm, at)
        for move in grads:
            move.wait()

    ins = {**in_vmem(values), **in_vmem(tables), **in_vmem(weights)}
    ins.update({**in_place(parts), **in_place(near)})
    outs = back_outputs(z, dict(output=struct((z.rows, z.width), BF)))
    scratch = {
        **scratch_of(attend_kept(z)),
        **scratch_of(experts_kept(z)),
        **attend_scratch(z),
        **attend_back_scratch(z, False),
        **experts_scratch(z),
        **experts_back_scratch(z, False),
    }
    if together:
        scratch.update({name + "_2": memory for name, memory in experts_scratch(z).items()})
    place = pltpu.VMEM(landing(z).shape, BF)
    scratch.update(dict(weight_0=place, weight_1=place, weight_2=place, gw_0=place, gw_1=place))
    attention, expert, back = layer_sems(z)
    count = attention + 2 * expert + back + 5 * z.nb
    return launch(body, 2, z, ins, outs, scratch, count)


def sum_pieces(z, k):
    wholes, sums = (k.up_in, k.up_out), (k.sum_in, k.sum_out)
    return weight_pieces(z, wholes, sums) + [(k.up_small, k.sum_small, 0, 128)]


def sum_parts(z, made):
    def grid(v):
        return v.reshape(grid_of(z) + (v.shape[-1],))

    ins = dict(up_in=grid(made.gin), up_out=grid(made.gout), up_small=grid(made.gsmall))
    outs = dict(
        sum_in=struct((z.shard, 3 * z.width), F32),
        sum_out=struct((z.shard, z.width), F32),
        sum_small=struct((z.shard, 128), F32),
    )
    columns = [(c, BF) for _, _, _, c in weight_pieces(z, (0, 0), (0, 0))] + [(128, F32)]
    buffers = reduce_buffers(z, columns)
    buffers.update(dict(mine=pltpu.SemaphoreType.DMA((len(columns),))))
    return ins, outs, buffers, len(columns)


def layer_back(z, values, tables, weights, first, upper):
    ups, sums, buffers, pieces = sum_parts(z, upper)

    def body(k, net):
        reduce = Reduce(net, sum_pieces(z, k), buffers_of(k, pieces), k.mine)
        late = GradMove(net, k.late, k.late_grad)
        own = [
            GradMove(net, k.gw_0, k.grad_0),
            GradMove(net, k.gw_1, k.grad_1),
            GradMove(net, k.gw_2, k.grad_2),
        ]
        at = Beside(
            rows_back=[reduce.step, late.near, late.far],
            side_back=[reduce.step],
            last_back=[own[0].far],
            back_sent=[reduce.step, own[1].far],
            back={1: [own[2].far]},
            back_out=[reduce.step],
        )
        pairs = (
            (k.far_gate, k.gate),
            (k.far_up, k.up),
            (k.far_kv, k.kv),
            (k.far_in, k.w_in),
            (k.far_out, k.w_out),
        )
        loads = [
            pltpu.make_async_copy(far, near, k.load.at[n]) for n, (far, near) in enumerate(pairs)
        ]
        for load in loads:
            load.start()
        reduce.step()

        def wait(w):
            if w == 0:
                loads[0].wait()
                loads[1].wait()

        e = view(
            k,
            weights=(k.weight_0, k.weight_1, k.weight_2),
            gw=(k.gw_0, k.gw_1, k.gw_2),
            wait_weight=wait,
            dg=k.gate,
            du=k.up,
        )
        dm, grad_logits = experts_back(
            net, e, k.middle[...], k.grad_in[...], k.grad_logits_in[...], at
        )
        k.grad_logits[...] = grad_logits
        for load in loads[2:]:
            load.wait()
        x = k.tokens[...].astype(F32)
        k.grad[...] = attend_back(net, view(k, dkv_out=k.kv), x, dm, at)
        reduce.step()
        late.wait()
        for move in own:
            move.wait((False, True))

    kept = {**attend_kept(z), **experts_kept(z)}
    far = dict(far_gate=kept.pop("gate"), far_up=kept.pop("up"), far_kv=kept.pop("kv"))
    loaded = {name[4:]: pltpu.VMEM(v.shape, v.dtype) for name, v in far.items()}
    weights = dict(weights)
    large = dict(far_in=weights.pop("w_in"), far_out=weights.pop("w_out"))
    loaded.update(
        dict(
            w_in=pltpu.VMEM(large["far_in"].shape, BF), w_out=pltpu.VMEM(large["far_out"].shape, BF)
        )
    )
    ins = {**in_vmem(values), **in_vmem(tables), **in_vmem(weights)}
    ins.update(in_vmem({name: getattr(first, name) for name in kept}))
    ins.update(in_place({name: getattr(first, name[4:]) for name in far}))
    ins.update(in_place({**ups, **large, **dict(late=upper.gw_2)}))
    outs = back_outputs(z, {**sums, **dict(gw_0=landing(z), gw_1=landing(z))})
    outs.update(in_place(dict(grad_2=grad_landing(z), late_grad=grad_landing(z))))
    scratch = {
        **attend_back_scratch(z, False),
        **experts_scratch(z),
        **experts_back_scratch(z, False),
        **loaded,
        **buffers,
        **dict(load=pltpu.SemaphoreType.DMA((5,))),
    }
    _, expert, back = layer_sems(z)
    count = expert + back + 4 * z.nb + pieces_sems(z, pieces)
    return launch(body, 3, z, ins, outs, scratch, count)


def reduce_last(z, lower):
    ups, sums, buffers, pieces = sum_parts(z, lower)

    def body(k, net):
        reduce = Reduce(net, sum_pieces(z, k), buffers_of(k, pieces), k.mine)
        reduce.step()
        own = [
            GradMove(net, k.gw_0, k.grad_0),
            GradMove(net, k.gw_1, k.grad_1),
            GradMove(net, k.gw_2, k.grad_2),
        ]
        for move in own:
            move.near()
        for _ in range(5):
            reduce.step()
        for move in own:
            move.wait((True, False))

    half = dict(half_0=lower.grad_0, half_1=lower.grad_1, half_2=lower.grad_2)
    ins = in_place({**ups, **dict(gw_0=lower.gw_0, gw_1=lower.gw_1, gw_2=lower.gw_2), **half})
    whole = grad_landing(z)
    outs = {**in_place(dict(grad_0=whole, grad_1=whole, grad_2=whole)), **in_vmem(sums)}
    same = list(zip(half, outs))
    return launch(body, 4, z, ins, outs, buffers, 3 * z.nb + pieces_sems(z, pieces), same)


def finish(z, upper, lower, final):
    far = dict(
        far_0=final.grad_0,
        far_1=upper.grad_0,
        far_2=final.grad_1,
        far_3=upper.grad_1,
        far_4=final.grad_2,
        far_5=lower.late_grad,
    )
    given = dict(
        output_in=upper.output,
        grad_in=lower.grad,
        logits_in=lower.grad_logits,
        in_0=final.sum_in,
        in_1=lower.sum_in,
        out_0=final.sum_out,
        out_1=lower.sum_out,
        small_0=final.sum_small,
        small_1=lower.sum_small,
    )
    wide = struct((LAYERS, 2, z.drow, z.hidden), F32)
    made = dict(
        output=struct((z.rows, z.width), BF),
        grad=struct((z.rows, z.width), F32),
        logits=struct((NE, z.rows), F32),
        gains=struct((LAYERS, 2, z.shard), F32),
        sum_in=struct((LAYERS, z.shard, 3 * z.width), F32),
        sum_out=struct((LAYERS, z.shard, z.width), F32),
        router=struct((NE, LAYERS, z.shard), F32),
        mix=struct((LAYERS, 4, z.shard), F32),
        consts=struct((LAYERS, 2, z.shard), F32),
    )
    large = dict(gate=wide, up=wide, down=wide)
    ins = {**in_place(far), **in_vmem(given)}
    outs = {**in_vmem(made), **in_place(large)}
    scratch = dict(
        low=pltpu.VMEM((6, 2, z.drow, z.hidden), BF),
        high=pltpu.VMEM((6, 2, z.drow, z.hidden), F32),
        come=pltpu.SemaphoreType.DMA((6,)),
        go=pltpu.SemaphoreType.DMA((12,)),
    )
    names = list(ins) + list(outs) + list(scratch)

    def body(*refs):
        k = Names(**dict(zip(names, refs)))
        parts = (k.far_0, k.far_1, k.far_2, k.far_3, k.far_4, k.far_5)
        loads = [pltpu.make_async_copy(p, k.low.at[n], k.come.at[n]) for n, p in enumerate(parts)]
        for load in loads:
            load.start()
        stores = []
        for n, load in enumerate(loads):
            load.wait()
            whole = (k.gate, k.up, k.down)[n // 2]
            for e in range(2):
                k.high[n, e] = k.low[n, e].astype(F32)
                place = whole.at[n % 2, e]
                stores.append(pltpu.make_async_copy(k.high.at[n, e], place, k.go.at[2 * n + e]))
                stores[-1].start()
        k.output[...] = k.output_in[...]
        k.grad[...] = k.grad_in[...]
        same = eye(z.rows)
        for n in range(NE):
            column = k.logits_in[:, n : n + 1]
            k.logits[n : n + 1] = jnp.sum(jnp.where(same, column, 0.0), axis=0, keepdims=True)
        same = eye(z.shard)
        sums = ((k.in_0, k.out_0, k.small_0), (k.in_1, k.out_1, k.small_1))
        for layer, (sum_in, sum_out, small) in enumerate(sums):
            k.sum_in[layer] = sum_in[...]
            k.sum_out[layer] = sum_out[...]
            for n in range(NE + 8):
                row = jnp.sum(jnp.where(same, small[:, n : n + 1], 0.0), axis=0, keepdims=True)
                if n < NE:
                    k.router[n, layer : layer + 1] = row
                elif n < NE + 4:
                    k.mix[layer, n - NE : n - NE + 1] = row
                elif n < NE + 6:
                    k.gains[layer, n - NE - 4 : n - NE - 3] = row
                else:
                    k.consts[layer, n - NE - 6 : n - NE - 5] = row
        for store in stores:
            store.wait()

    results = pl.pallas_call(
        body,
        out_shape=[v[0] for v in outs.values()],
        in_specs=[v[1] for v in ins.values()],
        out_specs=[v[1] for v in outs.values()],
        scratch_shapes=list(scratch.values()),
        compiler_params=pltpu.CompilerParams(vmem_limit_bytes=VMEM_BYTES),
    )(*[v[0] for v in ins.values()])
    return Names(**dict(zip(outs, results)))


def local(
    tokens,
    prev_logits,
    norm_gains,
    attn_in_weight,
    attn_out_weight,
    router_weight,
    const_mix,
    const_values,
    expert_gate,
    expert_up,
    expert_down,
    routes,
    order,
    cotangent,
):
    rows, width = tokens.shape
    z = Shape(lax.axis_size("head"), lax.axis_size("blk"), rows, width, expert_gate.shape[3])
    lane = np.arange(128) % (HD // 2)
    freqs = np.float32(10000.0) ** (-(2 * lane).astype(np.float32) / np.float32(HD))
    shards = dict(attn_in=attn_in_weight, attn_out=attn_out_weight)
    little = dict(
        router=jnp.transpose(router_weight, (2, 0, 1)),
        mix=jnp.transpose(const_mix, (0, 2, 1)),
        gains=norm_gains,
        consts=const_values,
        routes=jnp.transpose(routes, (0, 2, 1)),
        order=jnp.transpose(order, (0, 2, 1)),
        prev=jnp.transpose(prev_logits),
        freqs=jnp.asarray(freqs.astype(np.float32))[None],
    )
    parts = dict(expert_0=expert_gate, expert_1=expert_up, expert_2=expert_down)
    made = gather_first(z, {**shards, **parts}, little)
    tables = dict(cq=made.cq, sq=made.sq)

    def flat(v):
        return v.reshape(width, v.shape[-1])

    weights = dict(
        w_in=flat(made.w_in),
        w_out=flat(made.w_out),
        small=flat(made.small_0),
    )
    near = dict(near_0=made.near_0, near_1=made.near_1, near_2=made.near_2)
    values = dict(tokens=tokens, logits_in=made.logits, plan=made.plan_0)
    first = layer_forward(z, values, tables, weights, near, shards, parts)
    weights_1 = dict(
        w_in=flat(first.next_in),
        w_out=flat(first.next_out),
        small=flat(made.small_1),
    )
    near = dict(near_0=first.next_0, near_1=first.next_1, near_2=first.next_2)
    values = dict(
        state=first.state, logits_in=first.logits, plan=made.plan_1, cotangent=cotangent
    )
    upper = layer_both(z, values, tables, weights_1, near, parts)
    weights.update(
        dict(weight_0=first.weight_0, weight_1=first.weight_1, weight_2=first.weight_2)
    )
    values = dict(
        tokens=tokens, plan=made.plan_0, grad_in=upper.grad, grad_logits_in=upper.grad_logits
    )
    lower = layer_back(z, values, tables, weights, first, upper)
    final = reduce_last(z, lower)
    done = finish(z, upper, lower, final)
    return (
        done.output,
        done.grad,
        jnp.transpose(done.logits),
        done.gains,
        done.sum_in,
        done.sum_out,
        jnp.transpose(done.router, (1, 2, 0)),
        jnp.transpose(done.mix, (0, 2, 1)),
        done.consts,
        done.gate,
        done.up,
        done.down,
    )


def solution(mesh):
    placed = (
        P(("head", "blk"), None),
        P(("head", "blk"), None),
        P(None, None, ("head", "blk")),
        P(None, ("head", "blk"), None),
        P(None, ("head", "blk"), None),
        P(None, ("head", "blk"), None),
        P(None, ("head", "blk"), None),
        P(None, None, ("head", "blk")),
        P(None, "head", "blk", None),
        P(None, "head", "blk", None),
        P(None, "head", "blk", None),
        P(None, ("head", "blk"), None),
        P(None, ("head", "blk"), None),
        P(("head", "blk"), None),
    )
    return jax.shard_map(
        local,
        mesh=mesh,
        in_specs=placed,
        out_specs=(
            P(("head", "blk"), None),
            P(("head", "blk"), None),
            P(("head", "blk"), None),
            P(None, None, ("head", "blk")),
            P(None, ("head", "blk"), None),
            P(None, ("head", "blk"), None),
            P(None, ("head", "blk"), None),
            P(None, ("head", "blk"), None),
            P(None, None, ("head", "blk")),
            P(None, "head", "blk", None),
            P(None, "head", "blk", None),
            P(None, "head", "blk", None),
        ),
        check_vma=False,
    )
```

```python
import jax
import jax.numpy as jnp
import numpy as np
from jax import lax
from jax.experimental import pallas as pl
from jax.experimental.pallas import tpu as pltpu
from jax.sharding import PartitionSpec as P

HEADS = 12
HD = 64
NF = 8
TOP = 2
LAYERS = 2
NE = 12
CAP = 26
SLOT = 32
GROUPS = 4
EPSILON = 1e-05
NEGATIVE = -1e30
SCALE = HD ** (-0.5)
VMEM_BYTES = 65200 * 1024

BF = jnp.bfloat16
F32 = jnp.float32
MESH = pl.DeviceIdType.MESH
VMEM = pl.BlockSpec(memory_space=pltpu.VMEM)
ANY = pl.BlockSpec(memory_space=pl.ANY)


def mm(a, b, ca=1, cb=0):
    return lax.dot_general(a, b, (((ca,), (cb,)), ((), ())), preferred_element_type=F32)


def split(v):
    high = v.astype(BF)
    return high, (v - high.astype(F32)).astype(BF)


def lanes(shape):
    return lax.broadcasted_iota(jnp.int32, shape, len(shape) - 1)


def lane_of(v, index):
    return jnp.sum(jnp.where(lanes(v.shape) == index, v, 0.0), axis=-1, keepdims=True)


def rows_of(small):
    pick = lax.broadcasted_iota(jnp.int32, (8, 128), 0) + 16 == lanes((8, 128))
    return mm(pick.astype(F32).astype(BF), small, 1, 1)


def swap_halves(v):
    width = v.shape[-1]
    low_half = lanes(v.shape) % HD < HD // 2
    return jnp.where(
        low_half, pltpu.roll(v, width - HD // 2, 1), pltpu.roll(v, HD // 2, 1)
    )


def rotate(v, cosine, sine):
    return v * cosine + swap_halves(v) * sine


def rotate_back(v, cosine, sine):
    return v * cosine - swap_halves(v) * sine


def norm_grad(v, root, gain, grad):
    scaled = grad * gain
    inner = jnp.mean(v * scaled, axis=-1, keepdims=True)
    return root * scaled - v * (root * root * root * inner)


class Shape:
    def __init__(self, nh, nb, rows, width, hidden):
        self.nh, self.nb, self.rows, self.width, self.hidden = nh, nb, rows, width, hidden
        self.hh = nh // 2
        self.splits = nb // GROUPS
        self.nq = 2 * self.splits
        self.experts = self.hh * GROUPS
        self.ffp = hidden // self.nq
        self.drow = width // nb
        self.shards = nh * nb
        self.shard = width // self.shards
        self.count = self.experts * SLOT


class Links:
    def __init__(self, z, send, recv):
        self.z, self.send, self.recv, self.used = z, send, recv, 0
        self.sent, self.sent_if = [], []
        h, b = lax.axis_index("head"), lax.axis_index("blk")
        self.h, self.b = h, b
        self.y, self.c = h // 2, lax.rem(h, 2)
        self.g, self.s = b // z.splits, lax.rem(b, z.splits)
        self.q = self.c * z.splits + self.s

    def device(self, y, c, g, s):
        return (y * 2 + c, g * self.z.splits + s)

    def near(self, dy=0, dc=0, dg=0, ds=0):
        z = self.z
        return self.device(
            lax.rem(self.y + dy, z.hh),
            lax.rem(self.c + dc, 2),
            lax.rem(self.g + dg, GROUPS),
            lax.rem(self.s + ds, z.splits),
        )

    def beside(self):
        low = lax.rem(self.g, 2)
        return self.device(self.y, self.c, self.g + 1 - 2 * low, self.s)

    def up(self, value, step, size):
        return lax.rem(value + step, size)

    def down(self, value, step, size):
        return lax.rem(value + size - step, size)

    def take(self, amount):
        first = self.used
        self.used += amount
        return first

    def remote(self, src, dst, device, send, recv):
        return pltpu.make_async_remote_copy(
            src_ref=src,
            dst_ref=dst,
            send_sem=self.send.at[send],
            recv_sem=self.recv.at[recv],
            device_id=device,
            device_id_type=MESH,
        )

    def push(self, src, dst, device):
        place = self.take(1)
        made = self.remote(src, dst, device, place, place)
        made.start()
        self.sent.append(made)
        return made

    def push_or_keep(self, src, dst, device, here, send, recv):
        made = self.remote(src, dst, device, send, recv)

        @pl.when(jnp.logical_not(here))
        def _():
            made.start()

        @pl.when(here)
        def _():
            pltpu.make_async_copy(src, dst, self.recv.at[recv]).start()

        self.sent_if.append((here, made))

    def arrived(self, place, recv):
        pltpu.make_async_copy(place, place, self.recv.at[recv]).wait()

    def settle(self):
        for made in self.sent:
            made.wait_send()
        for here, made in self.sent_if:

            @pl.when(jnp.logical_not(here))
            def _(made=made):
                made.wait_send()

        self.sent, self.sent_if = [], []


def greet(devices):
    barrier = pltpu.get_barrier_semaphore()
    for device in devices:
        pl.semaphore_signal(barrier, inc=1, device_id=device, device_id_type=MESH)
    pl.semaphore_wait(barrier, len(devices))


def greet_all(net):
    z = net.z
    known = [net.near(dg=dg, ds=ds) for dg in range(GROUPS) for ds in range(z.splits) if dg or ds]
    known += [
        net.near(dc=1, dg=dg, ds=ds) for dg in range(GROUPS) for ds in range(z.splits)
    ]
    known += [
        net.near(dy=dy, dg=dg) for dy in range(1, z.hh) for dg in range(GROUPS)
    ]
    greet(known)


class Names:
    def __init__(self, **more):
        self.__dict__.update(more)


class Beside:
    start = sent = mid = out = rows = side = last = ()
    rows_back = side_back = last_back = back_sent = back_out = ()
    back = {}

    def __init__(self, **more):
        self.__dict__.update(more)


def act(functions):
    for function in functions:
        function()


def launch(body, number, z, ins, outs, scratch, copies, same=()):
    names = list(ins) + list(outs) + list(scratch) + ["send", "recv"]

    def kernel(*refs):
        held = Names(**dict(zip(names, refs)))
        net = Links(z, held.send, held.recv)
        greet_all(net)
        body(held, net)
        net.settle()
        assert net.used <= copies, net.used

    made = pl.pallas_call(
        kernel,
        out_shape=[v[0] for v in outs.values()],
        in_specs=[v[1] for v in ins.values()],
        out_specs=[v[1] for v in outs.values()],
        scratch_shapes=list(scratch.values())
        + [pltpu.SemaphoreType.DMA((copies,)), pltpu.SemaphoreType.DMA((copies,))],
        input_output_aliases={list(ins).index(i): list(outs).index(o) for i, o in same},
        compiler_params=pltpu.CompilerParams(
            collective_id=number, has_side_effects=True, vmem_limit_bytes=VMEM_BYTES
        ),
    )(*[v[0] for v in ins.values()])
    return Names(**dict(zip(outs, made)))


def struct(shape, kind):
    return jax.ShapeDtypeStruct(shape, kind)


class NearWeights:
    def __init__(self, net, part, layer, landed):
        self.net, self.part, self.layer, self.landed = net, part, layer, landed
        self.first = net.take(GROUPS)

    def start(self):
        net = self.net
        for dc in range(2):
            for dl in range(2):
                device, src = weight_source(net, self.part, self.layer, dc, 0, dl)
                dst, place, at = self.landed.at[net.g], self.first + 2 * dc + dl, self.first + net.g
                if dc or dl:
                    made = net.remote(src, dst, device, place, at)
                    made.start()
                    net.sent.append(made)
                else:
                    net.push_or_keep(src, dst, device, net.g // 2 == net.c, place, at)

    def wait(self):
        for n in range(GROUPS):
            self.net.arrived(self.landed.at[n], self.first + n)


class FarWeights:
    def __init__(self, net, part, layer, near, landed):
        self.net, self.part, self.layer, self.landed = net, part, layer, landed
        self.first = net.take(net.z.nb)
        for n in range(GROUPS):
            at = n * net.z.splits + net.s
            pltpu.make_async_copy(near.at[n], landed.at[at], net.recv.at[self.first + at]).start()

    def start(self):
        net, z = self.net, self.net.z
        place = self.first
        for ds in range(1, z.splits):
            for dc in range(2):
                for dl in range(2):
                    device, src = weight_source(net, self.part, self.layer, dc, ds, dl)
                    dst = self.landed.at[net.b]
                    made = net.remote(src, dst, device, place, self.first + net.b)
                    made.start()
                    net.sent.append(made)
                    place += 1

    def wait(self):
        for n in range(self.net.z.nb):
            self.net.arrived(self.landed.at[n], self.first + n)


def weight_source(net, part, layer, dc, ds, dl):
    z = net.z
    e = lax.rem(net.g + dl, 2)
    c, s = net.up(net.c, dc, 2), net.up(net.s, ds, z.splits)
    cols = pl.ds(pl.multiple_of((c * z.splits + s) * z.ffp, 128), z.ffp)
    return net.device(net.y, c, 2 * net.c + e, s), part.at[layer, e, :, cols]


class GradMove:
    def __init__(self, net, grads, landed):
        self.net, self.grads, self.landed = net, grads, landed
        self.first = net.take(net.z.nb)

    def near(self):
        self.start([r for r in range(self.net.z.nb) if r % self.net.z.splits == 0])

    def far(self):
        self.start([r for r in range(self.net.z.nb) if r % self.net.z.splits])

    def start(self, steps):
        net, z = self.net, self.net.z
        e = lax.rem(net.g, 2)
        cols = pl.ds(pl.multiple_of(net.q * z.ffp, 128), z.ffp)
        at = self.first + e * z.nq + net.q
        for r in steps:
            t = net.up(net.b, r, z.nb)
            src, dst = self.grads.at[t], self.landed.at[e, :, cols]
            device = (net.y * 2 + net.g // 2, t)
            if r:
                made = net.remote(src, dst, device, self.first + r, at)
                made.start()
                net.sent.append(made)
            else:
                net.push_or_keep(src, dst, device, net.g // 2 == net.c, self.first, at)

    def wait(self, shares=(True, True)):
        net, z = self.net, self.net.z
        for e in range(2):
            for c in range(2):
                for ds in range(z.splits):
                    if shares[1 if ds else 0]:
                        n = c * z.splits + net.up(net.s, ds, z.splits)
                        cols = pl.ds(pl.multiple_of(n * z.ffp, 128), z.ffp)
                        net.arrived(self.landed.at[e, :, cols], self.first + e * z.nq + n)


def cuts_of(names, widths, size):
    return [
        (name, at, min(size, width - at))
        for name, width in zip(names, widths)
        for at in range(0, width, size)
    ]


class Gather:
    STEPS = 6

    def __init__(self, net, pieces, own_sems):
        self.net, self.pieces, self.stage = net, pieces, 0
        at = (net.y, net.c, net.g // 2, lax.rem(net.g, 2), net.s)
        self.keep = []
        for p in range(len(pieces)):
            self.keep.append(
                pltpu.make_async_copy(self.own(p), self.full(p, at), own_sems.at[p])
            )
            self.keep[-1].start()
        self.waiting = [[] for _ in pieces]

    def own(self, p):
        ref, _, first, columns = self.pieces[p]
        return ref.at[:, first : first + columns]

    def full(self, p, at):
        _, ref, first, columns = self.pieces[p]
        return ref.at[at + (slice(None), slice(first, first + columns))]

    def step(self):
        net, z, every = self.net, self.net.z, slice(None)
        y, c, s = net.y, net.c, net.s
        high, low = net.g // 2, lax.rem(net.g, 2)
        splits = [net.near(ds=d) for d in range(1, z.splits)]
        ys = [net.near(dy=d) for d in range(1, z.hh)]
        by_split = [((y, c, every, every, s), splits), ((y, c, every, every, every), ys)]
        by_y = [((y, c, every, every, s), ys), ((every, c, every, every, s), splits)]
        for p in range(len(self.pieces)):
            for made in self.waiting[p]:
                made.wait_recv()
            self.waiting[p] = []
            if self.stage == 1:
                self.keep[p].wait()
            if self.stage == 5:
                continue
            if self.stage == 0:
                at, peers = (y, c, high, low, s), [net.near(dg=2)]
            elif self.stage == 1:
                at, peers = (y, c, every, low, s), [net.beside()]
            elif self.stage == 4:
                at, peers = (every, c, every, every, every), [net.near(dc=1)]
            else:
                at, peers = (by_y if p % 2 else by_split)[self.stage - 2]
            place = self.full(p, at)
            src = self.own(p) if self.stage == 0 else place
            self.waiting[p] = [net.push(src, place, peer) for peer in peers]
        self.stage += 1


class Reduce:
    STEPS = 6

    def __init__(self, net, pieces, bufs, sems):
        self.net, self.pieces, self.bufs, self.stage = net, pieces, bufs, 0
        self.waiting = [[] for _ in pieces]
        self.mine = []
        for p, (full, _, lo, columns) in enumerate(pieces):
            own = full.at[:, net.c, :, :, :, :, slice(lo, lo + columns)]
            self.mine.append(pltpu.make_async_copy(own, bufs[p][5], sems.at[p]))

    def step(self):
        net, z = self.net, self.net.z
        y, c, s = net.y, net.c, net.s
        high, low = net.g // 2, lax.rem(net.g, 2)
        to_y = [(net.up(y, d, z.hh), net.near(dy=d)) for d in range(1, z.hh)]
        to_split = [(net.up(s, d, z.splits), net.near(ds=d)) for d in range(1, z.splits)]
        bits = [(i, j) for i in range(2) for j in range(2)]
        for p, (full, out, lo, columns) in enumerate(self.pieces):
            cut = slice(lo, lo + columns)
            one, two, three, four, five, own = self.bufs[p]
            kind = full.dtype
            for made in self.waiting[p]:
                made.wait_recv()
            moves = []
            split_first = p % 2 == 1
            firsts, seconds = (to_split, to_y) if split_first else (to_y, to_split)
            if self.stage == 0:
                moves = [(full.at[:, 1 - c, :, :, :, :, cut], one, net.near(dc=1))]
                self.mine[p].start()
            elif self.stage == 1:
                self.mine[p].wait()
                for a in range(z.hh):
                    for i, j in bits:
                        total = one[a, i, j].astype(F32) + own[a, i, j].astype(F32)
                        one[a, i, j] = total.astype(kind)
                for k, (t, peer) in enumerate(firsts):
                    moves.append((one.at[:, :, :, t] if split_first else one.at[t], two.at[k], peer))
            elif self.stage == 2:
                for i, j in bits:
                    for a in range(z.hh) if split_first else (0,):
                        at = (a, i, j) if split_first else (i, j)
                        total = (one[a, i, j, s] if split_first else one[y, i, j]).astype(F32)
                        for k in range(len(firsts)):
                            total = total + two[(k,) + at].astype(F32)
                        two[(0,) + at] = total.astype(kind)
                for k, (t, peer) in enumerate(seconds):
                    moves.append((two.at[0, t] if split_first else two.at[0, :, :, t], three.at[k], peer))
            elif self.stage == 3:
                for i, j in bits:
                    total = (two[0, y, i, j] if split_first else two[0, i, j, s]).astype(F32)
                    for k in range(len(seconds)):
                        total = total + three[k, i, j].astype(F32)
                    three[0, i, j] = total.astype(kind)
                moves = [(three.at[0, :, 1 - low], four, net.beside())]
            elif self.stage == 4:
                for i in range(2):
                    four[i] = (three[0, i, low].astype(F32) + four[i].astype(F32)).astype(kind)
                moves = [(four.at[1 - high], five, net.near(dg=2))]
            else:
                out[:, cut] = four[high].astype(F32) + five[...].astype(F32)
            self.waiting[p] = [net.push(*move) for move in moves]
        self.stage += 1


def reduce_buffers(z, columns_kinds):
    made = {}
    for p, (columns, kind) in enumerate(columns_kinds):
        block = (z.shard, columns)
        made[f"r{p}a"] = pltpu.VMEM((z.hh, 2, 2, z.splits) + block, kind)
        if p % 2 == 0:
            made[f"r{p}b"] = pltpu.VMEM((z.hh - 1, 2, 2, z.splits) + block, kind)
            made[f"r{p}c"] = pltpu.VMEM((z.splits - 1, 2, 2) + block, kind)
        else:
            made[f"r{p}b"] = pltpu.VMEM((z.splits - 1, z.hh, 2, 2) + block, kind)
            made[f"r{p}c"] = pltpu.VMEM((z.hh - 1, 2, 2) + block, kind)
        made[f"r{p}d"] = pltpu.VMEM((2,) + block, kind)
        made[f"r{p}e"] = pltpu.VMEM(block, kind)
        made[f"r{p}f"] = pltpu.VMEM((z.hh, 2, 2, z.splits) + block, kind)
    return made


def buffers_of(held, pieces):
    return [[getattr(held, f"r{p}{k}") for k in "abcdef"] for p in range(pieces)]


def head_masks(first):
    where_lane = lanes((1, 256))
    return [
        ((where_lane >= first + HD * j) & (where_lane < first + HD * (j + 1))).astype(F32)
        for j in range(3)
    ]


def window(v, g, shifted):
    start = 384 * (g // 2) + 128 * (g % 2)
    cut = v[:, start : start + 256]
    if shifted:
        if g % 2 == 0:
            cut = pltpu.roll(cut, HD, 1)
        return jnp.where(lanes(cut.shape) >= HD, cut, 0.0)
    if g % 2 == 1:
        cut = pltpu.roll(cut, 256 - HD, 1)
    return jnp.where(lanes(cut.shape) < 192, cut, 0.0)


def pack(v):
    half = v.shape[0] // 2
    last = v[:half, 128:] + pltpu.roll(v[half:, 128:], HD, 1)
    return v[:, :128].astype(BF), last.astype(BF)


def put_packed(ref, v):
    upper, last = pack(v)
    rows = v.shape[0]
    ref[:rows], ref[rows:] = upper, last


def unpack(packed):
    rows = packed.shape[0] * 2 // 3
    last = packed[rows:].astype(F32)
    keep = lanes(last.shape) < HD
    lower = jnp.concatenate(
        [jnp.where(keep, last, 0.0), jnp.where(keep, pltpu.roll(last, HD, 1), 0.0)], axis=0
    )
    return jnp.concatenate([packed[:rows].astype(F32), lower], axis=1)


def unwindow(even, odd):
    odd = pltpu.roll(odd, HD, 1)
    return [even[:, :128], even[:, 128:] + odd[:, :128], odd[:, 128:]]


def joined(key, value):
    return [key[:, :128], key[:, 128:] + value[:, :128], value[:, 128:]]


def places(net, first, last):
    z = net.z
    row = lax.broadcasted_iota(jnp.int32, ((last - first) * 3 * z.rows, 1), 0)
    block = first + row // (3 * z.rows)
    return (block * z.splits + net.s) * z.rows + row % z.rows


def attend(net, a, x, at):
    z = net.z
    act(at.start)
    gain = rows_of(a.small[...])[0:1]
    root = lax.rsqrt(jnp.mean(x * x, axis=-1, keepdims=True) + EPSILON)
    low = (x * root * gain).astype(BF)
    a.low[...] = low
    k = rotate(mm(low, a.w_in[:, z.width : 2 * z.width]), a.cq[...], a.sq[...])
    v = mm(low, a.w_in[:, 2 * z.width :])
    for n in range(GROUPS):
        for j, part in enumerate(joined(window(k, n, False), window(v, n, True))):
            a.kv_out[n, :, 128 * j : 128 * (j + 1)] = part.astype(BF)
    far = {}
    for dg in (2, 1, 3):
        t = net.up(net.g, dg, GROUPS)
        far[dg] = net.push(a.kv_out.at[t], a.kv.at[net.b], net.near(dg=dg))
    a.kv[net.b] = a.kv_out[net.g]
    q = rotate(mm(low, a.w_in[:, : z.width]), a.cq[...], a.sq[...])
    for n in range(GROUPS):
        put_packed(a.q_out.at[n], window(q, n, False))
    moved = []
    for dg in (2, 1, 3):
        t = net.up(net.g, dg, GROUPS)
        moved.append(net.push(a.q_out.at[t], a.q.at[net.g], net.near(dg=dg)))
    a.q[net.g] = a.q_out[net.g]
    act(at.sent)
    for dg in (0, 1, 3, 2):
        if dg:
            far[dg].wait_recv()
        place = a.kv.at[net.down(net.g, dg, GROUPS) * z.splits + net.s]
        for ds in range(1, z.splits):
            moved.append(net.push(place, place, net.near(ds=ds)))
    for made in moved:
        made.wait_recv()
    act(at.mid)
    q_masks = [m.astype(BF) for m in head_masks(0)]
    v_masks = head_masks(HD)
    first = net.take(GROUPS)
    chunk = z.nb * z.rows if z.nb * z.rows <= 1024 else 512
    for i in range(GROUPS):
        own = unpack(a.q[i]).astype(BF)
        q3 = jnp.concatenate([own * m for m in q_masks], axis=0)
        row = places(net, i, i + 1)
        peak = total = out = None
        for start in range(0, (i + 1) * z.splits * z.rows, chunk):
            keys = min(chunk, (i + 1) * z.splits * z.rows - start)
            kv = a.kv[start // z.rows : (start + keys) // z.rows].reshape(keys, 384)
            mask = lanes((1, keys)) + start <= row
            scores = jnp.where(mask, mm(q3, kv[:, 0:256], 1, 1) * SCALE, NEGATIVE)
            top = jnp.max(scores, axis=-1, keepdims=True)
            top = top if peak is None else jnp.maximum(top, peak)
            weights = jnp.exp(scores - top)
            more = jnp.sum(weights, axis=-1, keepdims=True)
            product = mm(weights.astype(BF), kv[:, 128:384])
            if peak is None:
                total, out = more, product
            else:
                factor = jnp.exp(peak - top)
                total, out = total * factor + more, out * factor + product
            peak = top
        out = out / total
        merged = sum(out[z.rows * j : z.rows * (j + 1)] * v_masks[j] for j in range(3))
        a.o[i] = merged
        put_packed(a.o_out.at[i], pltpu.roll(merged, 256 - HD, 1))
        a.lse[i] = peak + jnp.log(total)
        device = net.device(net.y, net.c, i, net.s)
        net.push_or_keep(
            a.o_out.at[i], a.ret.at[net.g], device, net.g == i, first + i, first + net.g
        )
    act(at.out)
    middle = x
    for n in range(GROUPS):
        net.arrived(a.ret.at[n], first + n)
        got = unpack(a.ret[n]).astype(BF)
        middle = middle + mm(got[:, 0:192], a.w_out[192 * n : 192 * (n + 1), :])
    a.middle[...] = middle
    return middle


def attend_back(net, a, x, dm, at):
    z = net.z
    branch = dm.astype(BF)
    grad_att = mm(branch, a.w_out[...], 1, 1)
    for n in range(GROUPS):
        put_packed(a.do_out.at[n], window(grad_att, n, False))
    moved = []
    for dg in (2, 1, 3):
        t = net.up(net.g, dg, GROUPS)
        moved.append(net.push(a.do_out.at[t], a.do.at[net.g], net.near(dg=dg)))
    a.do[net.g] = a.do_out[net.g]
    act(at.back_sent)
    per = 192 // z.shard
    for n in range(GROUPS):
        part = mm(unpack(a.ret[n]).astype(BF), branch, 0, 0)[0:192]
        for k in range(per):
            a.gout[n * per + k] = part[k * z.shard : (k + 1) * z.shard].astype(BF)
    q_masks = head_masks(0)
    v_masks = head_masks(HD)
    for i in range(GROUPS):
        own = unpack(a.q[i]).astype(BF)
        for j in range(3):
            a.q3[i, z.rows * j : z.rows * (j + 1)] = own * q_masks[j].astype(BF)
    a.dq_sum[...] = jnp.zeros(a.dq_sum.shape, F32)
    for made in moved:
        made.wait_recv()
    for i in range(GROUPS):
        own = pltpu.roll(unpack(a.do[i]), HD, 1)
        product = own * a.o[i]
        for j in range(3):
            span = slice(z.rows * j, z.rows * (j + 1))
            a.do3[i, span] = (own * v_masks[j]).astype(BF)
            a.delta[i, span] = jnp.sum(product * v_masks[j], axis=-1, keepdims=True)
    first_q, first_kv = net.take(GROUPS), net.take(GROUPS)
    between = {}
    size = 3 * z.rows

    def onward(i):
        total = a.dkv_out[i * z.splits + net.s].astype(F32)
        for ds, made in between[i]:
            made.wait_recv()
            total = total + a.dkv_got[ds - 1, i].astype(F32)
        a.dkv_sum[i] = total.astype(BF)
        device = net.device(net.y, net.c, i, net.s)
        net.push_or_keep(
            a.dkv_sum.at[i], a.dkv.at[net.g], device, net.g == i, first_kv + i, first_kv + net.g
        )

    some = min(4, z.splits)
    keys = some * z.rows
    for n in range(GROUPS):
        spans = [(n, GROUPS)] if keys <= 256 else [(i, i + 1) for i in range(n, GROUPS)]
        for block in range(n * z.splits, (n + 1) * z.splits, some):
            kv = a.kv[block : block + some].reshape(keys, 384)
            key, value = kv[:, 0:256], kv[:, 128:384]
            dk = jnp.zeros((keys, 256), F32)
            dv = jnp.zeros((keys, 256), F32)
            for lo, hi in spans:
                rows = (hi - lo) * size
                q3 = a.q3[lo:hi].reshape(rows, 256)
                do3 = a.do3[lo:hi].reshape(rows, 256)
                lse = a.lse[lo:hi].reshape(rows, 1)
                delta = a.delta[lo:hi].reshape(rows, 1)
                mask = lanes((1, keys)) + block * z.rows <= places(net, lo, hi)
                scores = mm(q3, key, 1, 1) * SCALE
                weights = jnp.where(mask, jnp.exp(scores - lse), 0.0)
                grad_scores = (weights * (mm(do3, value, 1, 1) - delta)).astype(BF)
                more = mm(grad_scores, key).reshape((hi - lo) * 3, z.rows, 256)
                for i in range(lo, hi):
                    at_i = 3 * (i - lo)
                    a.dq_sum[i] += sum(more[at_i + j] * q_masks[j] for j in range(3))
                dk = dk + mm(grad_scores, q3, 0, 0)
                dv = dv + mm(weights.astype(BF), do3, 0, 0)
            for j, part in enumerate(joined(dk * SCALE, dv)):
                a.dkv_out[block : block + some, :, 128 * j : 128 * (j + 1)] = part.astype(
                    BF
                ).reshape(some, z.rows, 128)
        between[n] = []
        for ds in range(1, z.splits):
            t = net.up(net.s, ds, z.splits)
            made = net.push(a.dkv_out.at[n * z.splits + t], a.dkv_got.at[ds - 1, n], net.near(ds=ds))
            between[n].append((ds, made))
        put_packed(a.dq_out.at[n], a.dq_sum[n] * SCALE)
        device = net.device(net.y, net.c, n, net.s)
        net.push_or_keep(
            a.dq_out.at[n], a.dq.at[net.g], device, net.g == n, first_q + n, first_q + net.g
        )
        if n:
            onward(n - 1)
        act(at.back.get(n, ()))
    onward(GROUPS - 1)
    act(at.back_out)
    own = a.low[...]
    grad_low = jnp.zeros((z.rows, z.width), F32)
    from_zero = lanes((1, 256)) < 192

    leaving = []

    def weigh(piece, start):
        slot = len(leaving) % 2
        if len(leaving) >= 2:
            leaving[-2].wait()
        part = mm(own, piece, 0, 0)
        for k in range(z.shards):
            a.gin_part[slot, k] = part[k * z.shard : (k + 1) * z.shard].astype(BF)
        place = a.gin.at[:, :, start : start + 384]
        leaving.append(pltpu.make_async_copy(a.gin_part.at[slot], place, a.gin_sem.at[slot]))
        leaving[-1].start()
        return mm(piece, a.w_in[:, start : start + 384], 1, 1)

    def turned(columns, n):
        cut = slice(192 * n, 192 * n + 384)
        return rotate_back(jnp.concatenate(columns, axis=1), a.cq[:, cut], a.sq[:, cut]).astype(BF)

    for n in range(0, GROUPS, 2):
        net.arrived(a.dq.at[n], first_q + n)
        net.arrived(a.dq.at[n + 1], first_q + n + 1)
        columns = unwindow(unpack(a.dq[n]), unpack(a.dq[n + 1]))
        grad_low = grad_low + weigh(turned(columns, n), 192 * n)
    for n in range(0, GROUPS, 2):
        pair = []
        for m in (n, n + 1):
            net.arrived(a.dkv.at[m], first_kv + m)
            both = a.dkv[m].astype(F32)
            key = jnp.where(from_zero, both[:, :256], 0.0)
            value = jnp.where(from_zero, pltpu.roll(both[:, 128:], 256 - HD, 1), 0.0)
            pair.append((key, value))
        columns = unwindow(pair[0][0], pair[1][0])
        grad_low = grad_low + weigh(turned(columns, n), z.width + 192 * n)
        columns = unwindow(pair[0][1], pair[1][1])
        piece = jnp.concatenate(columns, axis=1).astype(BF)
        grad_low = grad_low + weigh(piece, 2 * z.width + 192 * n)
    for copy in leaving[-2:]:
        copy.wait()
    gain = rows_of(a.small[...])[0:1]
    root = lax.rsqrt(jnp.mean(x * x, axis=-1, keepdims=True) + EPSILON)
    place = (lanes((z.rows, 128)) == 16).astype(F32).astype(BF)
    high, rest = split(grad_low * x * root)
    a.gsmall[...] += mm(high, place, 0, 0) + mm(rest, place, 0, 0)
    return dm + norm_grad(x, root, gain, grad_low)


class Mixing:
    def __init__(self, z, middle, small, plan):
        table = rows_of(small)
        self.gain, self.consts = table[1:2], (table[2:3], table[3:4])
        self.root = lax.rsqrt(jnp.mean(middle * middle, axis=-1, keepdims=True) + EPSILON)
        self.normed = middle * self.root * self.gain
        self.low, self.rest = split(self.normed)
        expert_of, slot_of = lanes((z.rows, 128)).astype(F32), lanes((z.rows, z.count)).astype(F32)
        self.picks = [(expert_of == plan[:, j : j + 1]).astype(F32) for j in range(TOP)]
        self.chosen = [(slot_of == plan[:, TOP + j : TOP + j + 1]).astype(F32) for j in range(TOP)]
        self.select = (self.chosen[0] + self.chosen[1]).astype(BF)
        self.small = small

    def share(self):
        self.product = mm(self.low, self.small)
        shares = self.product + mm(self.rest, self.small)
        self.shares = []
        for index in range(2):
            one, two = lane_of(shares, 12 + 2 * index), lane_of(shares, 13 + 2 * index)
            peak = jnp.maximum(one, two)
            one, two = jnp.exp(one - peak), jnp.exp(two - peak)
            self.shares.append((one / (one + two), two / (one + two)))

    def gate(self, logits):
        values = [jnp.sum(p * logits, axis=-1, keepdims=True) for p in self.picks]
        peak = jnp.maximum(values[0], values[1])
        powers = [jnp.exp(v - peak) for v in values]
        total = powers[0] + powers[1]
        self.gates = [p / total for p in powers]
        self.combine = self.gates[0] * self.chosen[0] + self.gates[1] * self.chosen[1]

    def weigh(self):
        spread = self.gates[0] * self.picks[0] + self.gates[1] * self.picks[1]
        self.const_weights = [lane_of(spread, NF + 2 + index) for index in range(2)]
        self.normed_weight = lane_of(spread, NF + 1)
        for index in range(2):
            self.normed_weight = (
                self.normed_weight + self.const_weights[index] * self.shares[index][0]
            )


class ExpertRun:
    def __init__(self, net, e, rows_ref, all_ref, chunk):
        self.net, self.e, self.rows_ref, self.all_ref, self.chunk = net, e, rows_ref, all_ref, chunk
        self.mine = net.y * GROUPS + net.g

    def send(self):
        net, z = self.net, self.net.z
        steps = [(dy, dg) for dg in (2, 1, 3, 0) for dy in range(z.hh) if dy or dg]
        first = []
        for dy, dg in steps:
            target = net.up(net.y, dy, z.hh) * GROUPS + net.up(net.g, dg, GROUPS)
            place = self.all_ref.at[net.q, self.mine]
            first.append(net.push(self.rows_ref.at[target], place, net.near(dy=dy, dg=dg)))
        self.all_ref[net.q, self.mine] = self.rows_ref[self.mine]
        self.sources = [(0, 0, None)] + [
            (dy, dg, made) for (dy, dg), made in zip(reversed(steps), reversed(first))
        ]

    def relay(self, while_first):
        net, z = self.net, self.net.z
        self.slots = []
        self.aside, self.across = [[] for _ in range(z.splits)], [[] for _ in range(z.splits)]
        for k, (dy, dg, made) in enumerate(self.sources):
            if made is not None:
                made.wait_recv()
            self.slots.append(net.down(net.y, dy, z.hh) * GROUPS + net.down(net.g, dg, GROUPS))
            place = self.all_ref.at[net.q, self.slots[k]]
            for ds in range(1, z.splits):
                self.aside[ds].append(net.push(place, place, net.near(ds=ds)))
            self.across[0].append(net.push(place, place, net.near(dc=1)))
            if k == 0:
                while_first()

    def compute(self, before_side=None):
        net, z, e = self.net, self.net.z, self.e
        block = (z.experts, SLOT, z.width)
        e.base[...] = self.chunk(net.q).reshape(block)
        other = 1 - net.c
        for ds in range(1, z.splits):
            s = net.down(net.s, ds, z.splits)
            for k, made in enumerate(self.aside[ds]):
                made.wait_recv()
                place = self.all_ref.at[net.c * z.splits + s, self.slots[k]]
                self.across[ds].append(net.push(place, place, net.near(dc=1)))
        self.halves = {}
        for ds in range(z.splits):
            s = net.down(net.s, ds, z.splits)
            for made in self.across[ds]:
                made.wait_recv()
            e.part[ds] = self.chunk(other * z.splits + s).astype(BF).reshape(block)
            to_core = net.push(e.part.at[ds], e.got.at[ds], net.near(dc=1))
            if ds == 0:
                self.first_core = to_core
                continue
            kept = self.chunk(net.c * z.splits + s)
            to_core.wait_recv()
            net.sent = [made for made in net.sent if made is not to_core]
            to_core.wait_send()
            e.part[ds] = (kept.reshape(block) + e.got[ds].astype(F32)).astype(BF)
            if before_side is not None and ds == 1:
                before_side()
            for dy in reversed(range(z.hh)):
                span = pl.ds(net.up(net.y, dy, z.hh) * GROUPS, GROUPS)
                device = net.near(ds=z.splits - ds)
                made = net.push(e.part.at[ds, span], e.side_got.at[ds - 1, span], device)
                self.halves[ds, dy] = made

    def give_back(self):
        net, z, e = self.net, self.net.z, self.e
        self.first_core.wait_recv()
        e.base[...] += e.got[0].astype(F32)
        self.last = []
        for dy in reversed(range(z.hh)):
            y = net.up(net.y, dy, z.hh)
            span = pl.ds(y * GROUPS, GROUPS)
            total = e.base[span]
            for ds in range(1, z.splits):
                self.halves[ds, dy].wait_recv()
                total = total + e.side_got[ds - 1, span].astype(F32)
            e.sum[span] = total.astype(BF)
            for dg in (2, 1, 3, 0):
                if dy or dg:
                    src = e.sum.at[y * GROUPS + net.up(net.g, dg, GROUPS)]
                    made = net.push(src, e.back.at[self.mine], net.near(dy=dy, dg=dg))
                    self.last.append(made)
        e.back[self.mine] = e.sum[self.mine]

    def wait(self):
        for made in self.last:
            made.wait_recv()


def weight_of(z, e, w):
    e.wait_weight(w)
    ref = e.weights[w]
    if z.drow % 16 == 0:
        return ref[...].reshape(z.width, z.ffp)
    return jnp.concatenate([ref[n].astype(F32) for n in range(z.nb)], axis=0).astype(BF)


def held_weights(net, e):
    held = {}

    def weight(w):
        if w not in held:
            held[w] = weight_of(net.z, e, w)
        return held[w]

    return weight


def forward_chunk(net, e, weight):
    z = net.z

    def chunk(part):
        rows = e.all[part].reshape(z.count, z.width)
        gate, up = mm(rows, weight(0)), mm(rows, weight(1))
        e.gate[part], e.up[part] = gate.astype(BF), up.astype(BF)
        hidden = (gate / (1.0 + jnp.exp(-gate)) * up).astype(BF)
        return mm(hidden, weight(2), 1, 1)

    return chunk


def backward_chunk(net, e, weight):
    z = net.z

    def chunk(part):
        weight(0), weight(1)
        rows = e.dall[part].reshape(z.count, z.width)
        grad_hidden = mm(rows, weight(2))
        gate, up = e.gate[part].astype(F32), e.up[part].astype(F32)
        sig = 1.0 / (1.0 + jnp.exp(-gate))
        silu = gate * sig
        e.hid[part] = (silu * up).astype(BF)
        up_low = (grad_hidden * silu).astype(BF)
        gate_low = (grad_hidden * up * (sig * (1.0 + gate * (1.0 - sig)))).astype(BF)
        e.du[part], e.dg[part] = up_low, gate_low
        return mm(gate_low, weight(0), 1, 1) + mm(up_low, weight(1), 1, 1)

    return chunk


def weight_grads(net, e):
    z = net.z
    step = min(4, z.nq)
    for w, one, two in ((0, e.all, e.dg), (1, e.all, e.du), (2, e.dall, e.hid)):
        product = None
        for first in range(0, z.nq, step):
            span = slice(first, first + step)
            left = one[span].reshape(step * z.count, z.width)
            more = mm(left, two[span].reshape(step * z.count, z.ffp), 0, 0)
            product = more if product is None else product + more
        for n in range(z.nb):
            e.gw[w][n] = product[n * z.drow : (n + 1) * z.drow].astype(BF)


def put_rows(mixing, e):
    e.rows[...] = mm(mixing.select, mixing.low, 0, 0).astype(BF).reshape(e.rows.shape)


def put_grad_rows(mixing, e, high, rest):
    weight_high, weight_rest = split(mixing.combine)
    slot_grad = mm(weight_high, high, 0, 0) + mm(weight_rest, high, 0, 0)
    slot_grad = slot_grad + mm(weight_high, rest, 0, 0)
    e.rows[...] = slot_grad.astype(BF).reshape(e.rows.shape)


def mixture(z, mixing, middle, results):
    high, rest = split(mixing.combine)
    mixed = mm(high, results) + mm(rest, results) + mixing.normed_weight * mixing.normed
    for index in range(2):
        weight = mixing.const_weights[index] * mixing.shares[index][1]
        mixed = mixed + weight * mixing.consts[index]
    return middle + mixed


def mixture_grads(z, mixing, grad, grad_logits, high, rest, results):
    where_lane = lanes((z.rows, 128))
    along = mm(high, results, 1, 1) + mm(rest, results, 1, 1)
    normed_dot = jnp.sum(grad * mixing.normed, axis=-1, keepdims=True)
    const_dots = [jnp.sum(grad * c, axis=-1, keepdims=True) for c in mixing.consts]
    gate_grads = []
    for j in range(TOP):
        value = jnp.sum(mixing.chosen[j] * along, axis=-1, keepdims=True)
        value = value + lane_of(mixing.picks[j], NF + 1) * normed_dot
        for index in range(2):
            share = mixing.shares[index]
            value = value + lane_of(mixing.picks[j], NF + 2 + index) * (
                share[0] * normed_dot + share[1] * const_dots[index]
            )
        gate_grads.append(value)
    inner = mixing.gates[0] * gate_grads[0] + mixing.gates[1] * gate_grads[1]
    logit_grad = grad_logits
    for j in range(TOP):
        logit_grad = logit_grad + mixing.picks[j] * (mixing.gates[j] * (gate_grads[j] - inner))
    column = jnp.zeros((z.rows, 128), F32)
    const_columns = jnp.zeros((z.rows, 128), F32)
    for index in range(2):
        share, weight = mixing.shares[index], mixing.const_weights[index]
        one, two = weight * normed_dot, weight * const_dots[index]
        mean = share[0] * one + share[1] * two
        column = column + jnp.where(where_lane == 12 + 2 * index, share[0] * (one - mean), 0.0)
        column = column + jnp.where(where_lane == 13 + 2 * index, share[1] * (two - mean), 0.0)
        const_columns = const_columns + jnp.where(where_lane == 18 + index, weight * share[1], 0.0)
    both_high, both_rest = split(logit_grad + column)
    grad_normed = mm(both_high, mixing.small, 1, 1) + mm(both_rest, mixing.small, 1, 1)
    grad_normed = grad_normed + mixing.normed_weight * grad
    gsmall = mm(mixing.low, both_high, 0, 0) + mm(mixing.low, both_rest, 0, 0)
    gsmall = gsmall + mm(mixing.rest, column.astype(BF), 0, 0)
    const_high, const_rest = split(const_columns)
    gsmall = gsmall + mm(high, const_high, 0, 0) + mm(rest, const_high, 0, 0)
    return logit_grad, grad_normed, gsmall + mm(high, const_rest, 0, 0)


def middle_grads(z, mixing, e, middle, grad, grad_normed, gsmall):
    grad_normed = grad_normed + mm(mixing.select, e.back[...].reshape(z.count, z.width))
    place = (lanes((z.rows, 128)) == 17).astype(F32).astype(BF)
    high, rest = split(grad_normed * middle * mixing.root)
    e.gsmall[...] = gsmall + mm(high, place, 0, 0) + mm(rest, place, 0, 0)
    return grad + norm_grad(middle, mixing.root, mixing.gain, grad_normed)


def experts(net, e, middle, logits_in, at):
    z = net.z
    mixing = Mixing(z, middle, e.small[...], e.plan[...])
    put_rows(mixing, e)
    run = ExpertRun(net, e, e.rows, e.all, forward_chunk(net, e, held_weights(net, e)))

    def while_first():
        mixing.share()
        logits = mixing.product + logits_in
        e.logits[...] = logits
        mixing.gate(logits)
        mixing.weigh()
        act(at.rows)

    run.send()
    run.relay(while_first)
    run.compute()
    act(at.side)
    run.give_back()
    act(at.last)
    run.wait()
    e.results[...] = e.back[...]
    return mixture(z, mixing, middle, e.back[...].reshape(z.count, z.width))


def experts_back(net, e, middle, grad, grad_logits, at):
    z = net.z
    mixing = Mixing(z, middle, e.small[...], e.plan[...])
    mixing.gate(e.logits[...])
    high, rest = split(grad)
    put_grad_rows(mixing, e, high, rest)
    run = ExpertRun(net, e, e.rows, e.dall, backward_chunk(net, e, held_weights(net, e)))
    made = []

    def while_first():
        mixing.share()
        mixing.weigh()
        results = e.results[...].reshape(z.count, z.width)
        made.extend(mixture_grads(z, mixing, grad, grad_logits, high, rest, results))
        act(at.rows_back)

    run.send()
    run.relay(while_first)
    run.compute()
    weight_grads(net, e)
    act(at.side_back)
    run.give_back()
    act(at.last_back)
    run.wait()
    logit_grad, grad_normed, gsmall = made
    return middle_grads(z, mixing, e, middle, grad, grad_normed, gsmall), logit_grad


def experts_both(net, e, later, middle, logits_in, grad, grad_logits, at):
    z = net.z
    mixing = Mixing(z, middle, e.small[...], e.plan[...])
    put_rows(mixing, e)
    weight = held_weights(net, e)
    run = ExpertRun(net, e, e.rows, e.all, forward_chunk(net, e, weight))
    back = ExpertRun(net, later, later.rows, e.dall, backward_chunk(net, e, weight))
    run.send()
    act(at.rows)
    mixing.share()
    mixing.gate(mixing.product + logits_in)
    high, rest = split(grad)
    put_grad_rows(mixing, later, high, rest)
    back.send()
    mixing.weigh()
    run.relay(lambda: None)
    run.compute(lambda: back.relay(lambda: None))
    back.compute()
    run.give_back()
    weight_grads(net, e)
    act(at.side_back)
    back.give_back()
    act(at.last_back)
    run.wait()
    results = e.back[...].reshape(z.count, z.width)
    result = mixture(z, mixing, middle, results)
    made = mixture_grads(z, mixing, grad, grad_logits, high, rest, results)
    back.wait()
    logit_grad, grad_normed, gsmall = made
    return result, middle_grads(z, mixing, later, middle, grad, grad_normed, gsmall), logit_grad


def attend_kept(z):
    return dict(
        middle=struct((z.rows, z.width), F32),
        low=struct((z.rows, z.width), BF),
        q=struct((GROUPS, 3 * z.rows // 2, 128), BF),
        kv=struct((z.nb, z.rows, 384), BF),
        o=struct((GROUPS, z.rows, 256), F32),
        lse=struct((GROUPS, 3 * z.rows, 1), F32),
        ret=struct((GROUPS, 3 * z.rows // 2, 128), BF),
    )


def experts_kept(z):
    block = (z.experts, SLOT, z.width)
    return dict(
        logits=struct((z.rows, 128), F32),
        results=struct(block, BF),
        all=struct((z.nq,) + block, BF),
        gate=struct((z.nq, z.count, z.ffp), BF),
        up=struct((z.nq, z.count, z.ffp), BF),
    )


def attend_scratch(z):
    return dict(
        q_out=pltpu.VMEM((GROUPS, 3 * z.rows // 2, 128), BF),
        kv_out=pltpu.VMEM((GROUPS, z.rows, 384), BF),
        o_out=pltpu.VMEM((GROUPS, 3 * z.rows // 2, 128), BF),
    )


def attend_back_scratch(z, own_output=True):
    one = pltpu.VMEM((GROUPS, 3 * z.rows // 2, 128), BF)
    three = pltpu.VMEM((GROUPS, 3 * z.rows, 256), BF)
    two = pltpu.VMEM((GROUPS, z.rows, 384), BF)
    made = dict(
        do_out=one,
        do=one,
        dq_out=one,
        dq=one,
        dkv_out=pltpu.VMEM((z.nb, z.rows, 384), BF),
        dkv_got=pltpu.VMEM((z.splits - 1, GROUPS, z.rows, 384), BF),
        dkv_sum=two,
        dkv=two,
        q3=three,
        do3=three,
        dq_sum=pltpu.VMEM((GROUPS, z.rows, 256), F32),
        gin_part=pltpu.VMEM((2, z.shards, z.shard, 384), BF),
        gin_sem=pltpu.SemaphoreType.DMA((2,)),
        delta=pltpu.VMEM((GROUPS, 3 * z.rows, 1), F32),
    )
    if not own_output:
        del made["dkv_out"]
    return made


def experts_scratch(z):
    block = (z.experts, SLOT, z.width)
    flat = pltpu.VMEM((z.splits,) + block, BF)
    return dict(
        rows=pltpu.VMEM(block, BF),
        part=flat,
        got=flat,
        side_got=pltpu.VMEM((z.splits - 1,) + block, BF),
        base=pltpu.VMEM(block, F32),
        sum=pltpu.VMEM(block, BF),
        back=pltpu.VMEM(block, BF),
    )


def experts_back_scratch(z, both=True):
    part = pltpu.VMEM((z.nq, z.count, z.ffp), BF)
    block = (z.experts, SLOT, z.width)
    made = dict(dall=pltpu.VMEM((z.nq,) + block, BF), hid=part)
    if both:
        made.update(dict(dg=part, du=part))
    return made


def scratch_of(kept):
    return {name: pltpu.VMEM(v.shape, v.dtype) for name, v in kept.items()}


def view(held, **more):
    return Names(**{**held.__dict__, **more})


def landing(z):
    return struct((z.nb, z.drow, z.ffp), BF)


def near_landing(z):
    return struct((GROUPS, z.drow, z.ffp), BF)


def grad_landing(z):
    return struct((2, z.drow, z.hidden), BF)


def nothing():
    pass


CUT = 384


def in_vmem(arrays):
    return {name: (array, VMEM) for name, array in arrays.items()}


def in_place(arrays):
    return {name: (array, ANY) for name, array in arrays.items()}


def weight_pieces(z, owns, wholes):
    widths = (3 * z.width, z.width)
    return [
        (owns[which], wholes[which], first, columns)
        for which, first, columns in cuts_of((0, 1), widths, CUT)
    ]


def pieces_sems(z, pieces):
    return pieces * (2 + z.splits + z.hh)


def eye(size):
    shape = (size, size)
    return lax.broadcasted_iota(jnp.int32, shape, 0) == lax.broadcasted_iota(jnp.int32, shape, 1)


def upright(row, same):
    return jnp.sum(jnp.where(same, row, 0.0), axis=1, keepdims=True)


def plan_of(z, routes, order):
    same, lane = eye(z.rows), lanes((z.rows, 128))
    ids, ranks = routes.astype(F32), order.astype(F32)
    plan = jnp.zeros((z.rows, 128), F32)
    for j in range(TOP):
        own, rank = upright(ids[j : j + 1], same), upright(ranks[j : j + 1], same)
        before = jnp.zeros((z.rows, 1), F32)
        for k in range(TOP):
            counts = (own == ids[k : k + 1]) & (ranks[k : k + 1] < rank)
            before = before + jnp.sum(counts.astype(F32), axis=1, keepdims=True)
        slot = jnp.where((own < NF) & (before < CAP), own * SLOT + before, -1.0)
        plan = plan + jnp.where(lane == j, own, 0.0) + jnp.where(lane == TOP + j, slot, 0.0)
    return plan


def grid_of(z):
    return (z.hh, 2, 2, 2, z.splits, z.shard)


def gather_first(z, large, little):
    def body(k, net):
        owns, wholes = (k.attn_in.at[0], k.attn_out.at[0]), (k.w_in, k.w_out)
        pieces = weight_pieces(z, owns, wholes)
        gather = Gather(net, pieces, k.own)
        gather.step()
        moves = [
            NearWeights(net, k.expert_0, 0, k.near_0),
            NearWeights(net, k.expert_1, 0, k.near_1),
            NearWeights(net, k.expert_2, 0, k.near_2),
        ]
        same, lane = eye(z.shard), lanes((z.shard, 128))
        for layer in range(LAYERS):
            rows = [k.router[n][layer : layer + 1] for n in range(NE)]
            rows += [k.mix[layer][n : n + 1] for n in range(4)]
            rows += [k.gains[layer][n : n + 1] for n in range(2)]
            rows += [k.consts[layer][n : n + 1] for n in range(2)]
            table = jnp.zeros((z.shard, 128), F32)
            for n, row in enumerate(rows):
                table = table + jnp.where(lane == n, upright(row.astype(F32), same), 0.0)
            k.small_own[layer] = table.astype(BF)
        smalls = [
            (k.small_own.at[layer], whole, 0, 128)
            for layer, whole in enumerate((k.small_0, k.small_1))
        ]
        other = Gather(net, smalls, k.own_too)
        other.step()
        gather.step()
        moves[0].start()
        for layer, plan in enumerate((k.plan_0, k.plan_1)):
            plan[...] = plan_of(z, k.routes[layer], k.order[layer])
        same, lane = eye(z.rows), lanes((z.rows, 128))
        table = jnp.zeros((z.rows, 128), F32)
        for n in range(NE):
            table = table + jnp.where(lane == n, upright(k.prev[n : n + 1], same), 0.0)
        k.logits[...] = table
        gather.step()
        other.step()
        moves[1].start()
        moves[2].start()
        row = lax.broadcasted_iota(jnp.int32, (z.rows, 1), 0) + net.b * z.rows
        angles = row.astype(F32) * k.freqs[...]
        cosine, sine = jnp.cos(angles), jnp.sin(angles)
        sine = jnp.where(lane % HD < HD // 2, -sine, sine)
        for n in range(z.width // 128):
            k.cq[:, 128 * n : 128 * (n + 1)] = cosine
            k.sq[:, 128 * n : 128 * (n + 1)] = sine
        for _ in range(3):
            gather.step()
            other.step()
        other.step()
        for move in moves:
            move.wait()

    ins = {**in_place(large), **in_vmem(little)}
    outs = in_place(
        dict(
            w_in=struct(grid_of(z) + (3 * z.width,), BF),
            w_out=struct(grid_of(z) + (z.width,), BF),
            small_0=struct(grid_of(z) + (128,), BF),
            small_1=struct(grid_of(z) + (128,), BF),
            near_0=near_landing(z),
            near_1=near_landing(z),
            near_2=near_landing(z),
        )
    )
    table, wide = struct((z.rows, 128), F32), struct((z.rows, z.width), F32)
    outs.update(in_vmem(dict(plan_0=table, plan_1=table, logits=table, cq=wide, sq=wide)))
    pieces = len(weight_pieces(z, (0, 0), (0, 0)))
    scratch = dict(
        small_own=pltpu.VMEM((LAYERS, z.shard, 128), BF),
        own=pltpu.SemaphoreType.DMA((pieces,)),
        own_too=pltpu.SemaphoreType.DMA((LAYERS,)),
    )
    return launch(body, 0, z, ins, outs, scratch, pieces_sems(z, pieces + LAYERS) + 3 * GROUPS)


def layer_sems(z):
    attention = 6 + GROUPS * (z.splits - 1) + GROUPS
    expert = (z.experts - 1) * 2 + z.experts * (2 * z.splits - 1) + z.splits + z.hh * z.splits
    back = 3 + GROUPS * (z.splits - 1) + 2 * GROUPS
    return attention, expert, back


def waiting(*moves):
    held = list(moves)

    def wait(w):
        if held[w] is not None:
            held[w].wait()
            held[w] = None

    return wait


def layer_forward(z, values, tables, weights, near, shards, parts):
    def body(k, net):
        owns, wholes = (k.attn_in.at[1], k.attn_out.at[1]), (k.next_in, k.next_out)
        gather = Gather(net, weight_pieces(z, owns, wholes), k.own)
        far = [
            FarWeights(net, k.expert_0, 0, k.near_0, k.weight_0),
            FarWeights(net, k.expert_1, 0, k.near_1, k.weight_1),
            FarWeights(net, k.expert_2, 0, k.near_2, k.weight_2),
        ]
        ahead = [
            NearWeights(net, k.expert_0, 1, k.next_0),
            NearWeights(net, k.expert_1, 1, k.next_1),
            NearWeights(net, k.expert_2, 1, k.next_2),
        ]
        at = Beside(
            start=[gather.step, far[0].start],
            sent=[gather.step, far[1].start],
            mid=[gather.step],
            out=[far[2].start],
            rows=[ahead[0].start],
            side=[gather.step, ahead[1].start],
            last=[ahead[2].start],
        )
        middle = attend(net, k, k.tokens[...].astype(F32), at)
        e = view(k, weights=(k.weight_0, k.weight_1, k.weight_2), wait_weight=waiting(*far))
        k.state[...] = experts(net, e, middle, k.logits_in[...], at)
        gather.step()
        gather.step()
        for move in ahead:
            move.wait()

    ins = {**in_vmem(values), **in_vmem(tables), **in_vmem(weights)}
    ins.update({**in_place(shards), **in_place(parts), **in_place(near)})
    whole = landing(z)
    outs = dict(state=struct((z.rows, z.width), F32))
    outs.update(dict(weight_0=whole, weight_1=whole, weight_2=whole))
    outs = in_vmem({**outs, **attend_kept(z), **experts_kept(z)})
    ahead = dict(
        next_in=struct(grid_of(z) + (3 * z.width,), BF),
        next_out=struct(grid_of(z) + (z.width,), BF),
        next_0=near_landing(z),
        next_1=near_landing(z),
        next_2=near_landing(z),
    )
    outs.update(in_place(ahead))
    pieces = len(weight_pieces(z, (0, 0), (0, 0)))
    own = dict(own=pltpu.SemaphoreType.DMA((pieces,)))
    scratch = {**attend_scratch(z), **experts_scratch(z), **own}
    attention, expert, _ = layer_sems(z)
    count = attention + expert + pieces_sems(z, pieces) + 3 * z.nb + 3 * GROUPS
    return launch(body, 1, z, ins, outs, scratch, count)


def back_outputs(z, more):
    outs = dict(
        grad=struct((z.rows, z.width), F32),
        grad_logits=struct((z.rows, 128), F32),
        gout=struct((z.shards, z.shard, z.width), BF),
        gsmall=struct((z.width, 128), F32),
        gw_2=landing(z),
    )
    rest = dict(
        gin=struct((z.shards, z.shard, 3 * z.width), BF),
        grad_0=grad_landing(z),
        grad_1=grad_landing(z),
    )
    return {**in_vmem({**outs, **more}), **in_place(rest)}


def layer_both(z, values, tables, weights, near, parts):
    together = z.nb <= 8

    def body(k, net):
        far = [
            FarWeights(net, k.expert_0, 1, k.near_0, k.weight_0),
            FarWeights(net, k.expert_1, 1, k.near_1, k.weight_1),
            FarWeights(net, k.expert_2, 1, k.near_2, k.weight_2),
        ]
        grads = [GradMove(net, k.gw_0, k.grad_0), GradMove(net, k.gw_1, k.grad_1)]
        at = Beside(
            start=[far[0].start],
            sent=[far[1].start],
            out=[far[2].start],
            side_back=[grads[0].near],
            last_back=[grads[0].far],
            back_sent=[grads[1].near],
            back_out=[grads[1].far],
        )
        middle = attend(net, k, k.state[...], at)
        e = view(
            k,
            weights=(k.weight_0, k.weight_1, k.weight_2),
            gw=(k.gw_0, k.gw_1, k.gw_2),
            wait_weight=waiting(*far),
            dg=k.gate,
            du=k.up,
        )
        none = jnp.zeros((z.rows, 128), F32)
        grad = k.cotangent[...].astype(F32)
        if together:
            later = view(
                e,
                rows=k.rows_2,
                part=k.part_2,
                got=k.got_2,
                side_got=k.side_got_2,
                base=k.base_2,
                sum=k.sum_2,
                back=k.back_2,
            )
            result, dm, grad_logits = experts_both(
                net, e, later, middle, k.logits_in[...], grad, none, at
            )
        else:
            result = experts(net, e, middle, k.logits_in[...], at)
            net.settle()
            dm, grad_logits = experts_back(net, e, k.middle[...], grad, none, at)
        k.output[...] = result.astype(BF)
        k.grad_logits[...] = grad_logits
        net.settle()
        k.grad[...] = attend_back(net, view(k, dkv_out=k.kv), k.state[...], dm, at)
        for move in grads:
            move.wait()

    ins = {**in_vmem(values), **in_vmem(tables), **in_vmem(weights)}
    ins.update({**in_place(parts), **in_place(near)})
    outs = back_outputs(z, dict(output=struct((z.rows, z.width), BF)))
    scratch = {
        **scratch_of(attend_kept(z)),
        **scratch_of(experts_kept(z)),
        **attend_scratch(z),
        **attend_back_scratch(z, False),
        **experts_scratch(z),
        **experts_back_scratch(z, False),
    }
    if together:
        scratch.update({name + "_2": memory for name, memory in experts_scratch(z).items()})
    place = pltpu.VMEM(landing(z).shape, BF)
    scratch.update(dict(weight_0=place, weight_1=place, weight_2=place, gw_0=place, gw_1=place))
    attention, expert, back = layer_sems(z)
    count = attention + 2 * expert + back + 5 * z.nb
    return launch(body, 2, z, ins, outs, scratch, count)


def sum_pieces(z, k):
    wholes, sums = (k.up_in, k.up_out), (k.sum_in, k.sum_out)
    return weight_pieces(z, wholes, sums) + [(k.up_small, k.sum_small, 0, 128)]


def sum_parts(z, made):
    def grid(v):
        return v.reshape(grid_of(z) + (v.shape[-1],))

    ins = dict(up_in=grid(made.gin), up_out=grid(made.gout), up_small=grid(made.gsmall))
    outs = dict(
        sum_in=struct((z.shard, 3 * z.width), F32),
        sum_out=struct((z.shard, z.width), F32),
        sum_small=struct((z.shard, 128), F32),
    )
    columns = [(c, BF) for _, _, _, c in weight_pieces(z, (0, 0), (0, 0))] + [(128, F32)]
    buffers = reduce_buffers(z, columns)
    buffers.update(dict(mine=pltpu.SemaphoreType.DMA((len(columns),))))
    return ins, outs, buffers, len(columns)


def layer_back(z, values, tables, weights, first, upper):
    ups, sums, buffers, pieces = sum_parts(z, upper)

    def body(k, net):
        reduce = Reduce(net, sum_pieces(z, k), buffers_of(k, pieces), k.mine)
        late = GradMove(net, k.late, k.late_grad)
        own = [
            GradMove(net, k.gw_0, k.grad_0),
            GradMove(net, k.gw_1, k.grad_1),
            GradMove(net, k.gw_2, k.grad_2),
        ]
        at = Beside(
            rows_back=[reduce.step, late.near],
            side_back=[reduce.step, late.far],
            last_back=[own[0].far],
            back_sent=[reduce.step, own[1].far],
            back={1: [own[2].far]},
            back_out=[reduce.step],
        )
        pairs = (
            (k.far_gate, k.gate),
            (k.far_up, k.up),
            (k.far_kv, k.kv),
            (k.far_in, k.w_in),
            (k.far_out, k.w_out),
        )
        loads = [
            pltpu.make_async_copy(far, near, k.load.at[n]) for n, (far, near) in enumerate(pairs)
        ]
        for load in loads:
            load.start()
        reduce.step()

        def wait(w):
            if w == 0:
                loads[0].wait()
                loads[1].wait()

        e = view(
            k,
            weights=(k.weight_0, k.weight_1, k.weight_2),
            gw=(k.gw_0, k.gw_1, k.gw_2),
            wait_weight=wait,
            dg=k.gate,
            du=k.up,
        )
        dm, grad_logits = experts_back(
            net, e, k.middle[...], k.grad_in[...], k.grad_logits_in[...], at
        )
        k.grad_logits[...] = grad_logits
        for load in loads[2:]:
            load.wait()
        x = k.tokens[...].astype(F32)
        k.grad[...] = attend_back(net, view(k, dkv_out=k.kv), x, dm, at)
        reduce.step()
        late.wait()
        for move in own:
            move.wait((False, True))

    kept = {**attend_kept(z), **experts_kept(z)}
    far = dict(far_gate=kept.pop("gate"), far_up=kept.pop("up"), far_kv=kept.pop("kv"))
    loaded = {name[4:]: pltpu.VMEM(v.shape, v.dtype) for name, v in far.items()}
    weights = dict(weights)
    large = dict(far_in=weights.pop("w_in"), far_out=weights.pop("w_out"))
    loaded.update(
        dict(
            w_in=pltpu.VMEM(large["far_in"].shape, BF), w_out=pltpu.VMEM(large["far_out"].shape, BF)
        )
    )
    ins = {**in_vmem(values), **in_vmem(tables), **in_vmem(weights)}
    ins.update(in_vmem({name: getattr(first, name) for name in kept}))
    ins.update(in_place({name: getattr(first, name[4:]) for name in far}))
    ins.update(in_place({**ups, **large, **dict(late=upper.gw_2)}))
    outs = back_outputs(z, {**sums, **dict(gw_0=landing(z), gw_1=landing(z))})
    outs.update(in_place(dict(grad_2=grad_landing(z), late_grad=grad_landing(z))))
    scratch = {
        **attend_back_scratch(z, False),
        **experts_scratch(z),
        **experts_back_scratch(z, False),
        **loaded,
        **buffers,
        **dict(load=pltpu.SemaphoreType.DMA((5,))),
    }
    _, expert, back = layer_sems(z)
    count = expert + back + 4 * z.nb + pieces_sems(z, pieces)
    return launch(body, 3, z, ins, outs, scratch, count)


def reduce_last(z, lower):
    ups, sums, buffers, pieces = sum_parts(z, lower)

    def body(k, net):
        reduce = Reduce(net, sum_pieces(z, k), buffers_of(k, pieces), k.mine)
        reduce.step()
        own = [
            GradMove(net, k.gw_0, k.grad_0),
            GradMove(net, k.gw_1, k.grad_1),
            GradMove(net, k.gw_2, k.grad_2),
        ]
        for move in own:
            move.near()
        for _ in range(5):
            reduce.step()
        for move in own:
            move.wait((True, False))

    half = dict(half_0=lower.grad_0, half_1=lower.grad_1, half_2=lower.grad_2)
    ins = in_place({**ups, **dict(gw_0=lower.gw_0, gw_1=lower.gw_1, gw_2=lower.gw_2), **half})
    whole = grad_landing(z)
    outs = {**in_place(dict(grad_0=whole, grad_1=whole, grad_2=whole)), **in_vmem(sums)}
    same = list(zip(half, outs))
    return launch(body, 4, z, ins, outs, buffers, 3 * z.nb + pieces_sems(z, pieces), same)


def finish(z, upper, lower, final):
    far = dict(
        far_0=final.grad_0,
        far_1=upper.grad_0,
        far_2=final.grad_1,
        far_3=upper.grad_1,
        far_4=final.grad_2,
        far_5=lower.late_grad,
    )
    given = dict(
        output_in=upper.output,
        grad_in=lower.grad,
        logits_in=lower.grad_logits,
        in_0=final.sum_in,
        in_1=lower.sum_in,
        out_0=final.sum_out,
        out_1=lower.sum_out,
        small_0=final.sum_small,
        small_1=lower.sum_small,
    )
    wide = struct((LAYERS, 2, z.drow, z.hidden), F32)
    made = dict(
        output=struct((z.rows, z.width), BF),
        grad=struct((z.rows, z.width), F32),
        logits=struct((NE, z.rows), F32),
        gains=struct((LAYERS, 2, z.shard), F32),
        sum_in=struct((LAYERS, z.shard, 3 * z.width), F32),
        sum_out=struct((LAYERS, z.shard, z.width), F32),
        router=struct((NE, LAYERS, z.shard), F32),
        mix=struct((LAYERS, 4, z.shard), F32),
        consts=struct((LAYERS, 2, z.shard), F32),
    )
    large = dict(gate=wide, up=wide, down=wide)
    ins = {**in_place(far), **in_vmem(given)}
    outs = {**in_vmem(made), **in_place(large)}
    scratch = dict(
        low=pltpu.VMEM((6, 2, z.drow, z.hidden), BF),
        high=pltpu.VMEM((6, 2, z.drow, z.hidden), F32),
        come=pltpu.SemaphoreType.DMA((6,)),
        go=pltpu.SemaphoreType.DMA((12,)),
    )
    names = list(ins) + list(outs) + list(scratch)

    def body(*refs):
        k = Names(**dict(zip(names, refs)))
        parts = (k.far_0, k.far_1, k.far_2, k.far_3, k.far_4, k.far_5)
        loads = [pltpu.make_async_copy(p, k.low.at[n], k.come.at[n]) for n, p in enumerate(parts)]
        for load in loads:
            load.start()
        stores = []
        for n, load in enumerate(loads):
            load.wait()
            whole = (k.gate, k.up, k.down)[n // 2]
            for e in range(2):
                k.high[n, e] = k.low[n, e].astype(F32)
                place = whole.at[n % 2, e]
                stores.append(pltpu.make_async_copy(k.high.at[n, e], place, k.go.at[2 * n + e]))
                stores[-1].start()
        k.output[...] = k.output_in[...]
        k.grad[...] = k.grad_in[...]
        same = eye(z.rows)
        for n in range(NE):
            column = k.logits_in[:, n : n + 1]
            k.logits[n : n + 1] = jnp.sum(jnp.where(same, column, 0.0), axis=0, keepdims=True)
        same = eye(z.shard)
        sums = ((k.in_0, k.out_0, k.small_0), (k.in_1, k.out_1, k.small_1))
        for layer, (sum_in, sum_out, small) in enumerate(sums):
            k.sum_in[layer] = sum_in[...]
            k.sum_out[layer] = sum_out[...]
            for n in range(NE + 8):
                row = jnp.sum(jnp.where(same, small[:, n : n + 1], 0.0), axis=0, keepdims=True)
                if n < NE:
                    k.router[n, layer : layer + 1] = row
                elif n < NE + 4:
                    k.mix[layer, n - NE : n - NE + 1] = row
                elif n < NE + 6:
                    k.gains[layer, n - NE - 4 : n - NE - 3] = row
                else:
                    k.consts[layer, n - NE - 6 : n - NE - 5] = row
        for store in stores:
            store.wait()

    results = pl.pallas_call(
        body,
        out_shape=[v[0] for v in outs.values()],
        in_specs=[v[1] for v in ins.values()],
        out_specs=[v[1] for v in outs.values()],
        scratch_shapes=list(scratch.values()),
        compiler_params=pltpu.CompilerParams(vmem_limit_bytes=VMEM_BYTES),
    )(*[v[0] for v in ins.values()])
    return Names(**dict(zip(outs, results)))


def local(
    tokens,
    prev_logits,
    norm_gains,
    attn_in_weight,
    attn_out_weight,
    router_weight,
    const_mix,
    const_values,
    expert_gate,
    expert_up,
    expert_down,
    routes,
    order,
    cotangent,
):
    rows, width = tokens.shape
    z = Shape(lax.axis_size("head"), lax.axis_size("blk"), rows, width, expert_gate.shape[3])
    lane = np.arange(128) % (HD // 2)
    freqs = np.float32(10000.0) ** (-(2 * lane).astype(np.float32) / np.float32(HD))
    shards = dict(attn_in=attn_in_weight, attn_out=attn_out_weight)
    little = dict(
        router=jnp.transpose(router_weight, (2, 0, 1)),
        mix=jnp.transpose(const_mix, (0, 2, 1)),
        gains=norm_gains,
        consts=const_values,
        routes=jnp.transpose(routes, (0, 2, 1)),
        order=jnp.transpose(order, (0, 2, 1)),
        prev=jnp.transpose(prev_logits),
        freqs=jnp.asarray(freqs.astype(np.float32))[None],
    )
    parts = dict(expert_0=expert_gate, expert_1=expert_up, expert_2=expert_down)
    made = gather_first(z, {**shards, **parts}, little)
    tables = dict(cq=made.cq, sq=made.sq)

    def flat(v):
        return v.reshape(width, v.shape[-1])

    weights = dict(
        w_in=flat(made.w_in),
        w_out=flat(made.w_out),
        small=flat(made.small_0),
    )
    near = dict(near_0=made.near_0, near_1=made.near_1, near_2=made.near_2)
    values = dict(tokens=tokens, logits_in=made.logits, plan=made.plan_0)
    first = layer_forward(z, values, tables, weights, near, shards, parts)
    weights_1 = dict(
        w_in=flat(first.next_in),
        w_out=flat(first.next_out),
        small=flat(made.small_1),
    )
    near = dict(near_0=first.next_0, near_1=first.next_1, near_2=first.next_2)
    values = dict(
        state=first.state, logits_in=first.logits, plan=made.plan_1, cotangent=cotangent
    )
    upper = layer_both(z, values, tables, weights_1, near, parts)
    weights.update(
        dict(weight_0=first.weight_0, weight_1=first.weight_1, weight_2=first.weight_2)
    )
    values = dict(
        tokens=tokens, plan=made.plan_0, grad_in=upper.grad, grad_logits_in=upper.grad_logits
    )
    lower = layer_back(z, values, tables, weights, first, upper)
    final = reduce_last(z, lower)
    done = finish(z, upper, lower, final)
    return (
        done.output,
        done.grad,
        jnp.transpose(done.logits),
        done.gains,
        done.sum_in,
        done.sum_out,
        jnp.transpose(done.router, (1, 2, 0)),
        jnp.transpose(done.mix, (0, 2, 1)),
        done.consts,
        done.gate,
        done.up,
        done.down,
    )


def solution(mesh):
    placed = (
        P(("head", "blk"), None),
        P(("head", "blk"), None),
        P(None, None, ("head", "blk")),
        P(None, ("head", "blk"), None),
        P(None, ("head", "blk"), None),
        P(None, ("head", "blk"), None),
        P(None, ("head", "blk"), None),
        P(None, None, ("head", "blk")),
        P(None, "head", "blk", None),
        P(None, "head", "blk", None),
        P(None, "head", "blk", None),
        P(None, ("head", "blk"), None),
        P(None, ("head", "blk"), None),
        P(("head", "blk"), None),
    )
    return jax.shard_map(
        local,
        mesh=mesh,
        in_specs=placed,
        out_specs=(
            P(("head", "blk"), None),
            P(("head", "blk"), None),
            P(("head", "blk"), None),
            P(None, None, ("head", "blk")),
            P(None, ("head", "blk"), None),
            P(None, ("head", "blk"), None),
            P(None, ("head", "blk"), None),
            P(None, ("head", "blk"), None),
            P(None, None, ("head", "blk")),
            P(None, "head", "blk", None),
            P(None, "head", "blk", None),
            P(None, "head", "blk", None),
        ),
        check_vma=False,
    )
```

```python
import jax
import jax.numpy as jnp
import numpy as np
from jax import lax
from jax.experimental import pallas as pl
from jax.experimental.pallas import tpu as pltpu
from jax.sharding import PartitionSpec as P

HEADS = 12
HD = 64
NF = 8
TOP = 2
LAYERS = 2
NE = 12
CAP = 26
SLOT = 32
GROUPS = 4
EPSILON = 1e-05
NEGATIVE = -1e30
SCALE = HD ** (-0.5)
VMEM_BYTES = 65200 * 1024

BF = jnp.bfloat16
F32 = jnp.float32
MESH = pl.DeviceIdType.MESH
VMEM = pl.BlockSpec(memory_space=pltpu.VMEM)
ANY = pl.BlockSpec(memory_space=pl.ANY)


def mm(a, b, ca=1, cb=0):
    return lax.dot_general(a, b, (((ca,), (cb,)), ((), ())), preferred_element_type=F32)


def split(v):
    high = v.astype(BF)
    return high, (v - high.astype(F32)).astype(BF)


def lanes(shape):
    return lax.broadcasted_iota(jnp.int32, shape, len(shape) - 1)


def lane_of(v, index):
    return jnp.sum(jnp.where(lanes(v.shape) == index, v, 0.0), axis=-1, keepdims=True)


def rows_of(small):
    pick = lax.broadcasted_iota(jnp.int32, (8, 128), 0) + 16 == lanes((8, 128))
    return mm(pick.astype(F32).astype(BF), small, 1, 1)


def swap_halves(v):
    width = v.shape[-1]
    low_half = lanes(v.shape) % HD < HD // 2
    return jnp.where(
        low_half, pltpu.roll(v, width - HD // 2, 1), pltpu.roll(v, HD // 2, 1)
    )


def rotate(v, cosine, sine):
    return v * cosine + swap_halves(v) * sine


def rotate_back(v, cosine, sine):
    return v * cosine - swap_halves(v) * sine


def norm_grad(v, root, gain, grad):
    scaled = grad * gain
    inner = jnp.mean(v * scaled, axis=-1, keepdims=True)
    return root * scaled - v * (root * root * root * inner)


class Shape:
    def __init__(self, nh, nb, rows, width, hidden):
        self.nh, self.nb, self.rows, self.width, self.hidden = nh, nb, rows, width, hidden
        self.hh = nh // 2
        self.splits = nb // GROUPS
        self.nq = 2 * self.splits
        self.experts = self.hh * GROUPS
        self.ffp = hidden // self.nq
        self.drow = width // nb
        self.shards = nh * nb
        self.shard = width // self.shards
        self.count = self.experts * SLOT


class Links:
    def __init__(self, z, send, recv):
        self.z, self.send, self.recv, self.used = z, send, recv, 0
        self.sent, self.sent_if = [], []
        h, b = lax.axis_index("head"), lax.axis_index("blk")
        self.h, self.b = h, b
        self.y, self.c = h // 2, lax.rem(h, 2)
        self.g, self.s = b // z.splits, lax.rem(b, z.splits)
        self.q = self.c * z.splits + self.s

    def device(self, y, c, g, s):
        return (y * 2 + c, g * self.z.splits + s)

    def near(self, dy=0, dc=0, dg=0, ds=0):
        z = self.z
        return self.device(
            lax.rem(self.y + dy, z.hh),
            lax.rem(self.c + dc, 2),
            lax.rem(self.g + dg, GROUPS),
            lax.rem(self.s + ds, z.splits),
        )

    def beside(self):
        low = lax.rem(self.g, 2)
        return self.device(self.y, self.c, self.g + 1 - 2 * low, self.s)

    def up(self, value, step, size):
        return lax.rem(value + step, size)

    def down(self, value, step, size):
        return lax.rem(value + size - step, size)

    def take(self, amount):
        first = self.used
        self.used += amount
        return first

    def remote(self, src, dst, device, send, recv):
        return pltpu.make_async_remote_copy(
            src_ref=src,
            dst_ref=dst,
            send_sem=self.send.at[send],
            recv_sem=self.recv.at[recv],
            device_id=device,
            device_id_type=MESH,
        )

    def push(self, src, dst, device):
        place = self.take(1)
        made = self.remote(src, dst, device, place, place)
        made.start()
        self.sent.append(made)
        return made

    def push_or_keep(self, src, dst, device, here, send, recv):
        made = self.remote(src, dst, device, send, recv)

        @pl.when(jnp.logical_not(here))
        def _():
            made.start()

        @pl.when(here)
        def _():
            pltpu.make_async_copy(src, dst, self.recv.at[recv]).start()

        self.sent_if.append((here, made))

    def arrived(self, place, recv):
        pltpu.make_async_copy(place, place, self.recv.at[recv]).wait()

    def settle(self):
        for made in self.sent:
            made.wait_send()
        for here, made in self.sent_if:

            @pl.when(jnp.logical_not(here))
            def _(made=made):
                made.wait_send()

        self.sent, self.sent_if = [], []


def greet(devices):
    barrier = pltpu.get_barrier_semaphore()
    for device in devices:
        pl.semaphore_signal(barrier, inc=1, device_id=device, device_id_type=MESH)
    pl.semaphore_wait(barrier, len(devices))


def greet_all(net):
    z = net.z
    known = [net.near(dg=dg, ds=ds) for dg in range(GROUPS) for ds in range(z.splits) if dg or ds]
    known += [
        net.near(dc=1, dg=dg, ds=ds) for dg in range(GROUPS) for ds in range(z.splits)
    ]
    known += [
        net.near(dy=dy, dg=dg) for dy in range(1, z.hh) for dg in range(GROUPS)
    ]
    greet(known)


class Names:
    def __init__(self, **more):
        self.__dict__.update(more)


class Beside:
    start = sent = mid = out = rows = side = last = ()
    rows_back = side_back = last_back = back_sent = back_out = ()
    back = {}

    def __init__(self, **more):
        self.__dict__.update(more)


def act(functions):
    for function in functions:
        function()


def launch(body, number, z, ins, outs, scratch, copies, same=()):
    names = list(ins) + list(outs) + list(scratch) + ["send", "recv"]

    def kernel(*refs):
        held = Names(**dict(zip(names, refs)))
        net = Links(z, held.send, held.recv)
        greet_all(net)
        body(held, net)
        net.settle()
        assert net.used <= copies, net.used

    made = pl.pallas_call(
        kernel,
        out_shape=[v[0] for v in outs.values()],
        in_specs=[v[1] for v in ins.values()],
        out_specs=[v[1] for v in outs.values()],
        scratch_shapes=list(scratch.values())
        + [pltpu.SemaphoreType.DMA((copies,)), pltpu.SemaphoreType.DMA((copies,))],
        input_output_aliases={list(ins).index(i): list(outs).index(o) for i, o in same},
        compiler_params=pltpu.CompilerParams(
            collective_id=number, has_side_effects=True, vmem_limit_bytes=VMEM_BYTES
        ),
    )(*[v[0] for v in ins.values()])
    return Names(**dict(zip(outs, made)))


def struct(shape, kind):
    return jax.ShapeDtypeStruct(shape, kind)


class NearWeights:
    def __init__(self, net, part, layer, landed):
        self.net, self.part, self.layer, self.landed = net, part, layer, landed
        self.first = net.take(GROUPS)

    def start(self):
        net = self.net
        for dc in range(2):
            for dl in range(2):
                device, src = weight_source(net, self.part, self.layer, dc, 0, dl)
                dst, place, at = self.landed.at[net.g], self.first + 2 * dc + dl, self.first + net.g
                if dc or dl:
                    made = net.remote(src, dst, device, place, at)
                    made.start()
                    net.sent.append(made)
                else:
                    net.push_or_keep(src, dst, device, net.g // 2 == net.c, place, at)

    def wait(self):
        for n in range(GROUPS):
            self.net.arrived(self.landed.at[n], self.first + n)


class FarWeights:
    def __init__(self, net, part, layer, near, landed):
        self.net, self.part, self.layer, self.landed = net, part, layer, landed
        self.first = net.take(net.z.nb)
        for n in range(GROUPS):
            at = n * net.z.splits + net.s
            pltpu.make_async_copy(near.at[n], landed.at[at], net.recv.at[self.first + at]).start()

    def start(self):
        net, z = self.net, self.net.z
        place = self.first
        for ds in range(1, z.splits):
            for dc in range(2):
                for dl in range(2):
                    device, src = weight_source(net, self.part, self.layer, dc, ds, dl)
                    dst = self.landed.at[net.b]
                    made = net.remote(src, dst, device, place, self.first + net.b)
                    made.start()
                    net.sent.append(made)
                    place += 1

    def wait(self):
        for n in range(self.net.z.nb):
            self.net.arrived(self.landed.at[n], self.first + n)


def weight_source(net, part, layer, dc, ds, dl):
    z = net.z
    e = lax.rem(net.g + dl, 2)
    c, s = net.up(net.c, dc, 2), net.up(net.s, ds, z.splits)
    cols = pl.ds(pl.multiple_of((c * z.splits + s) * z.ffp, 128), z.ffp)
    return net.device(net.y, c, 2 * net.c + e, s), part.at[layer, e, :, cols]


class GradMove:
    def __init__(self, net, grads, landed):
        self.net, self.grads, self.landed = net, grads, landed
        self.first = net.take(net.z.nb)

    def near(self):
        self.start([r for r in range(self.net.z.nb) if r % self.net.z.splits == 0])

    def far(self):
        self.start([r for r in range(self.net.z.nb) if r % self.net.z.splits])

    def start(self, steps):
        net, z = self.net, self.net.z
        e = lax.rem(net.g, 2)
        cols = pl.ds(pl.multiple_of(net.q * z.ffp, 128), z.ffp)
        at = self.first + e * z.nq + net.q
        for r in steps:
            t = net.up(net.b, r, z.nb)
            src, dst = self.grads.at[t], self.landed.at[e, :, cols]
            device = (net.y * 2 + net.g // 2, t)
            if r:
                made = net.remote(src, dst, device, self.first + r, at)
                made.start()
                net.sent.append(made)
            else:
                net.push_or_keep(src, dst, device, net.g // 2 == net.c, self.first, at)

    def wait(self, shares=(True, True)):
        net, z = self.net, self.net.z
        for e in range(2):
            for c in range(2):
                for ds in range(z.splits):
                    if shares[1 if ds else 0]:
                        n = c * z.splits + net.up(net.s, ds, z.splits)
                        cols = pl.ds(pl.multiple_of(n * z.ffp, 128), z.ffp)
                        net.arrived(self.landed.at[e, :, cols], self.first + e * z.nq + n)


def cuts_of(names, widths, size):
    return [
        (name, at, min(size, width - at))
        for name, width in zip(names, widths)
        for at in range(0, width, size)
    ]


class Gather:
    STEPS = 6

    def __init__(self, net, pieces, own_sems):
        self.net, self.pieces, self.stage = net, pieces, 0
        at = (net.y, net.c, net.g // 2, lax.rem(net.g, 2), net.s)
        self.keep = []
        for p in range(len(pieces)):
            self.keep.append(
                pltpu.make_async_copy(self.own(p), self.full(p, at), own_sems.at[p])
            )
            self.keep[-1].start()
        self.waiting = [[] for _ in pieces]

    def own(self, p):
        ref, _, first, columns = self.pieces[p]
        return ref.at[:, first : first + columns]

    def full(self, p, at):
        _, ref, first, columns = self.pieces[p]
        return ref.at[at + (slice(None), slice(first, first + columns))]

    def step(self):
        net, z, every = self.net, self.net.z, slice(None)
        y, c, s = net.y, net.c, net.s
        high, low = net.g // 2, lax.rem(net.g, 2)
        splits = [net.near(ds=d) for d in range(1, z.splits)]
        ys = [net.near(dy=d) for d in range(1, z.hh)]
        by_split = [((y, c, every, every, s), splits), ((y, c, every, every, every), ys)]
        by_y = [((y, c, every, every, s), ys), ((every, c, every, every, s), splits)]
        for p in range(len(self.pieces)):
            for made in self.waiting[p]:
                made.wait_recv()
            self.waiting[p] = []
            if self.stage == 1:
                self.keep[p].wait()
            if self.stage == 5:
                continue
            if self.stage == 0:
                at, peers = (y, c, high, low, s), [net.near(dg=2)]
            elif self.stage == 1:
                at, peers = (y, c, every, low, s), [net.beside()]
            elif self.stage == 4:
                at, peers = (every, c, every, every, every), [net.near(dc=1)]
            else:
                at, peers = (by_y if p % 2 else by_split)[self.stage - 2]
            place = self.full(p, at)
            src = self.own(p) if self.stage == 0 else place
            self.waiting[p] = [net.push(src, place, peer) for peer in peers]
        self.stage += 1


class Reduce:
    STEPS = 6

    def __init__(self, net, pieces, bufs, sems):
        self.net, self.pieces, self.bufs, self.stage = net, pieces, bufs, 0
        self.waiting = [[] for _ in pieces]
        self.mine = []
        for p, (full, _, lo, columns) in enumerate(pieces):
            own = full.at[:, net.c, :, :, :, :, slice(lo, lo + columns)]
            self.mine.append(pltpu.make_async_copy(own, bufs[p][5], sems.at[p]))

    def step(self):
        net, z = self.net, self.net.z
        y, c, s = net.y, net.c, net.s
        high, low = net.g // 2, lax.rem(net.g, 2)
        to_y = [(net.up(y, d, z.hh), net.near(dy=d)) for d in range(1, z.hh)]
        to_split = [(net.up(s, d, z.splits), net.near(ds=d)) for d in range(1, z.splits)]
        bits = [(i, j) for i in range(2) for j in range(2)]
        for p, (full, out, lo, columns) in enumerate(self.pieces):
            cut = slice(lo, lo + columns)
            one, two, three, four, five, own = self.bufs[p]
            kind = full.dtype
            for made in self.waiting[p]:
                made.wait_recv()
            moves = []
            split_first = p % 2 == 1
            firsts, seconds = (to_split, to_y) if split_first else (to_y, to_split)
            if self.stage == 0:
                moves = [(full.at[:, 1 - c, :, :, :, :, cut], one, net.near(dc=1))]
                self.mine[p].start()
            elif self.stage == 1:
                self.mine[p].wait()
                for a in range(z.hh):
                    for i, j in bits:
                        total = one[a, i, j].astype(F32) + own[a, i, j].astype(F32)
                        one[a, i, j] = total.astype(kind)
                for k, (t, peer) in enumerate(firsts):
                    moves.append((one.at[:, :, :, t] if split_first else one.at[t], two.at[k], peer))
            elif self.stage == 2:
                for i, j in bits:
                    for a in range(z.hh) if split_first else (0,):
                        at = (a, i, j) if split_first else (i, j)
                        total = (one[a, i, j, s] if split_first else one[y, i, j]).astype(F32)
                        for k in range(len(firsts)):
                            total = total + two[(k,) + at].astype(F32)
                        two[(0,) + at] = total.astype(kind)
                for k, (t, peer) in enumerate(seconds):
                    moves.append((two.at[0, t] if split_first else two.at[0, :, :, t], three.at[k], peer))
            elif self.stage == 3:
                for i, j in bits:
                    total = (two[0, y, i, j] if split_first else two[0, i, j, s]).astype(F32)
                    for k in range(len(seconds)):
                        total = total + three[k, i, j].astype(F32)
                    three[0, i, j] = total.astype(kind)
                moves = [(three.at[0, :, 1 - low], four, net.beside())]
            elif self.stage == 4:
                for i in range(2):
                    four[i] = (three[0, i, low].astype(F32) + four[i].astype(F32)).astype(kind)
                moves = [(four.at[1 - high], five, net.near(dg=2))]
            else:
                out[:, cut] = four[high].astype(F32) + five[...].astype(F32)
            self.waiting[p] = [net.push(*move) for move in moves]
        self.stage += 1


def reduce_buffers(z, columns_kinds):
    made = {}
    for p, (columns, kind) in enumerate(columns_kinds):
        block = (z.shard, columns)
        made[f"r{p}a"] = pltpu.VMEM((z.hh, 2, 2, z.splits) + block, kind)
        if p % 2 == 0:
            made[f"r{p}b"] = pltpu.VMEM((z.hh - 1, 2, 2, z.splits) + block, kind)
            made[f"r{p}c"] = pltpu.VMEM((z.splits - 1, 2, 2) + block, kind)
        else:
            made[f"r{p}b"] = pltpu.VMEM((z.splits - 1, z.hh, 2, 2) + block, kind)
            made[f"r{p}c"] = pltpu.VMEM((z.hh - 1, 2, 2) + block, kind)
        made[f"r{p}d"] = pltpu.VMEM((2,) + block, kind)
        made[f"r{p}e"] = pltpu.VMEM(block, kind)
        made[f"r{p}f"] = pltpu.VMEM((z.hh, 2, 2, z.splits) + block, kind)
    return made


def buffers_of(held, pieces):
    return [[getattr(held, f"r{p}{k}") for k in "abcdef"] for p in range(pieces)]


def head_masks(first):
    where_lane = lanes((1, 256))
    return [
        ((where_lane >= first + HD * j) & (where_lane < first + HD * (j + 1))).astype(F32)
        for j in range(3)
    ]


def window(v, g, shifted):
    start = 384 * (g // 2) + 128 * (g % 2)
    cut = v[:, start : start + 256]
    if shifted:
        if g % 2 == 0:
            cut = pltpu.roll(cut, HD, 1)
        return jnp.where(lanes(cut.shape) >= HD, cut, 0.0)
    if g % 2 == 1:
        cut = pltpu.roll(cut, 256 - HD, 1)
    return jnp.where(lanes(cut.shape) < 192, cut, 0.0)


def pack(v):
    half = v.shape[0] // 2
    last = v[:half, 128:] + pltpu.roll(v[half:, 128:], HD, 1)
    return v[:, :128].astype(BF), last.astype(BF)


def put_packed(ref, v):
    upper, last = pack(v)
    rows = v.shape[0]
    ref[:rows], ref[rows:] = upper, last


def unpack(packed):
    rows = packed.shape[0] * 2 // 3
    last = packed[rows:].astype(F32)
    keep = lanes(last.shape) < HD
    lower = jnp.concatenate(
        [jnp.where(keep, last, 0.0), jnp.where(keep, pltpu.roll(last, HD, 1), 0.0)], axis=0
    )
    return jnp.concatenate([packed[:rows].astype(F32), lower], axis=1)


def unwindow(even, odd):
    odd = pltpu.roll(odd, HD, 1)
    return [even[:, :128], even[:, 128:] + odd[:, :128], odd[:, 128:]]


def joined(key, value):
    return [key[:, :128], key[:, 128:] + value[:, :128], value[:, 128:]]


def places(net, first, last):
    z = net.z
    row = lax.broadcasted_iota(jnp.int32, ((last - first) * 3 * z.rows, 1), 0)
    block = first + row // (3 * z.rows)
    return (block * z.splits + net.s) * z.rows + row % z.rows


def attend(net, a, x, at):
    z = net.z
    act(at.start)
    gain = rows_of(a.small[...])[0:1]
    root = lax.rsqrt(jnp.mean(x * x, axis=-1, keepdims=True) + EPSILON)
    low = (x * root * gain).astype(BF)
    a.low[...] = low
    k = rotate(mm(low, a.w_in[:, z.width : 2 * z.width]), a.cq[...], a.sq[...])
    v = mm(low, a.w_in[:, 2 * z.width :])
    for n in range(GROUPS):
        for j, part in enumerate(joined(window(k, n, False), window(v, n, True))):
            a.kv_out[n, :, 128 * j : 128 * (j + 1)] = part.astype(BF)
    far = {}
    for dg in (2, 1, 3):
        t = net.up(net.g, dg, GROUPS)
        far[dg] = net.push(a.kv_out.at[t], a.kv.at[net.b], net.near(dg=dg))
    a.kv[net.b] = a.kv_out[net.g]
    q = rotate(mm(low, a.w_in[:, : z.width]), a.cq[...], a.sq[...])
    for n in range(GROUPS):
        put_packed(a.q_out.at[n], window(q, n, False))
    moved = []
    for dg in (2, 1, 3):
        t = net.up(net.g, dg, GROUPS)
        moved.append(net.push(a.q_out.at[t], a.q.at[net.g], net.near(dg=dg)))
    a.q[net.g] = a.q_out[net.g]
    act(at.sent)
    for dg in (0, 1, 3, 2):
        if dg:
            far[dg].wait_recv()
        place = a.kv.at[net.down(net.g, dg, GROUPS) * z.splits + net.s]
        for ds in range(1, z.splits):
            moved.append(net.push(place, place, net.near(ds=ds)))
    for made in moved:
        made.wait_recv()
    act(at.mid)
    q_masks = [m.astype(BF) for m in head_masks(0)]
    v_masks = head_masks(HD)
    first = net.take(GROUPS)
    chunk = z.nb * z.rows if z.nb * z.rows <= 1024 else 512
    for i in range(GROUPS):
        own = unpack(a.q[i]).astype(BF)
        q3 = jnp.concatenate([own * m for m in q_masks], axis=0)
        row = places(net, i, i + 1)
        peak = total = out = None
        for start in range(0, (i + 1) * z.splits * z.rows, chunk):
            keys = min(chunk, (i + 1) * z.splits * z.rows - start)
            kv = a.kv[start // z.rows : (start + keys) // z.rows].reshape(keys, 384)
            mask = lanes((1, keys)) + start <= row
            scores = jnp.where(mask, mm(q3, kv[:, 0:256], 1, 1) * SCALE, NEGATIVE)
            top = jnp.max(scores, axis=-1, keepdims=True)
            top = top if peak is None else jnp.maximum(top, peak)
            weights = jnp.exp(scores - top)
            more = jnp.sum(weights, axis=-1, keepdims=True)
            product = mm(weights.astype(BF), kv[:, 128:384])
            if peak is None:
                total, out = more, product
            else:
                factor = jnp.exp(peak - top)
                total, out = total * factor + more, out * factor + product
            peak = top
        out = out / total
        merged = sum(out[z.rows * j : z.rows * (j + 1)] * v_masks[j] for j in range(3))
        a.o[i] = merged
        put_packed(a.o_out.at[i], pltpu.roll(merged, 256 - HD, 1))
        a.lse[i] = peak + jnp.log(total)
        device = net.device(net.y, net.c, i, net.s)
        net.push_or_keep(
            a.o_out.at[i], a.ret.at[net.g], device, net.g == i, first + i, first + net.g
        )
    act(at.out)
    middle = x
    for n in range(GROUPS):
        net.arrived(a.ret.at[n], first + n)
        got = unpack(a.ret[n]).astype(BF)
        middle = middle + mm(got[:, 0:192], a.w_out[192 * n : 192 * (n + 1), :])
    a.middle[...] = middle
    return middle


def attend_back(net, a, x, dm, at):
    z = net.z
    branch = dm.astype(BF)
    grad_att = mm(branch, a.w_out[...], 1, 1)
    for n in range(GROUPS):
        put_packed(a.do_out.at[n], window(grad_att, n, False))
    moved = []
    for dg in (2, 1, 3):
        t = net.up(net.g, dg, GROUPS)
        moved.append(net.push(a.do_out.at[t], a.do.at[net.g], net.near(dg=dg)))
    a.do[net.g] = a.do_out[net.g]
    act(at.back_sent)
    per = 192 // z.shard
    for n in range(GROUPS):
        part = mm(unpack(a.ret[n]).astype(BF), branch, 0, 0)[0:192]
        for k in range(per):
            a.gout[n * per + k] = part[k * z.shard : (k + 1) * z.shard].astype(BF)
    q_masks = head_masks(0)
    v_masks = head_masks(HD)
    for i in range(GROUPS):
        own = unpack(a.q[i]).astype(BF)
        for j in range(3):
            a.q3[i, z.rows * j : z.rows * (j + 1)] = own * q_masks[j].astype(BF)
    a.dq_sum[...] = jnp.zeros(a.dq_sum.shape, F32)
    for made in moved:
        made.wait_recv()
    for i in range(GROUPS):
        own = pltpu.roll(unpack(a.do[i]), HD, 1)
        product = own * a.o[i]
        for j in range(3):
            span = slice(z.rows * j, z.rows * (j + 1))
            a.do3[i, span] = (own * v_masks[j]).astype(BF)
            a.delta[i, span] = jnp.sum(product * v_masks[j], axis=-1, keepdims=True)
    first_q, first_kv = net.take(GROUPS), net.take(GROUPS)
    between = {}
    size = 3 * z.rows

    def onward(i):
        total = a.dkv_out[i * z.splits + net.s].astype(F32)
        for ds, made in between[i]:
            made.wait_recv()
            total = total + a.dkv_got[ds - 1, i].astype(F32)
        a.dkv_sum[i] = total.astype(BF)
        device = net.device(net.y, net.c, i, net.s)
        net.push_or_keep(
            a.dkv_sum.at[i], a.dkv.at[net.g], device, net.g == i, first_kv + i, first_kv + net.g
        )

    some = min(4, z.splits)
    keys = some * z.rows
    for n in range(GROUPS):
        spans = [(n, GROUPS)] if keys <= 256 else [(i, i + 1) for i in range(n, GROUPS)]
        for block in range(n * z.splits, (n + 1) * z.splits, some):
            kv = a.kv[block : block + some].reshape(keys, 384)
            key, value = kv[:, 0:256], kv[:, 128:384]
            dk = jnp.zeros((keys, 256), F32)
            dv = jnp.zeros((keys, 256), F32)
            for lo, hi in spans:
                rows = (hi - lo) * size
                q3 = a.q3[lo:hi].reshape(rows, 256)
                do3 = a.do3[lo:hi].reshape(rows, 256)
                lse = a.lse[lo:hi].reshape(rows, 1)
                delta = a.delta[lo:hi].reshape(rows, 1)
                mask = lanes((1, keys)) + block * z.rows <= places(net, lo, hi)
                scores = mm(q3, key, 1, 1) * SCALE
                weights = jnp.where(mask, jnp.exp(scores - lse), 0.0)
                grad_scores = (weights * (mm(do3, value, 1, 1) - delta)).astype(BF)
                more = mm(grad_scores, key).reshape((hi - lo) * 3, z.rows, 256)
                for i in range(lo, hi):
                    at_i = 3 * (i - lo)
                    a.dq_sum[i] += sum(more[at_i + j] * q_masks[j] for j in range(3))
                dk = dk + mm(grad_scores, q3, 0, 0)
                dv = dv + mm(weights.astype(BF), do3, 0, 0)
            for j, part in enumerate(joined(dk * SCALE, dv)):
                a.dkv_out[block : block + some, :, 128 * j : 128 * (j + 1)] = part.astype(
                    BF
                ).reshape(some, z.rows, 128)
        between[n] = []
        for ds in range(1, z.splits):
            t = net.up(net.s, ds, z.splits)
            made = net.push(a.dkv_out.at[n * z.splits + t], a.dkv_got.at[ds - 1, n], net.near(ds=ds))
            between[n].append((ds, made))
        put_packed(a.dq_out.at[n], a.dq_sum[n] * SCALE)
        device = net.device(net.y, net.c, n, net.s)
        net.push_or_keep(
            a.dq_out.at[n], a.dq.at[net.g], device, net.g == n, first_q + n, first_q + net.g
        )
        if n:
            onward(n - 1)
        act(at.back.get(n, ()))
    onward(GROUPS - 1)
    act(at.back_out)
    own = a.low[...]
    grad_low = jnp.zeros((z.rows, z.width), F32)
    from_zero = lanes((1, 256)) < 192

    leaving = []

    def weigh(piece, start):
        slot = len(leaving) % 2
        if len(leaving) >= 2:
            leaving[-2].wait()
        part = mm(own, piece, 0, 0)
        for k in range(z.shards):
            a.gin_part[slot, k] = part[k * z.shard : (k + 1) * z.shard].astype(BF)
        place = a.gin.at[:, :, start : start + 384]
        leaving.append(pltpu.make_async_copy(a.gin_part.at[slot], place, a.gin_sem.at[slot]))
        leaving[-1].start()
        return mm(piece, a.w_in[:, start : start + 384], 1, 1)

    def turned(columns, n):
        cut = slice(192 * n, 192 * n + 384)
        return rotate_back(jnp.concatenate(columns, axis=1), a.cq[:, cut], a.sq[:, cut]).astype(BF)

    for n in range(0, GROUPS, 2):
        net.arrived(a.dq.at[n], first_q + n)
        net.arrived(a.dq.at[n + 1], first_q + n + 1)
        columns = unwindow(unpack(a.dq[n]), unpack(a.dq[n + 1]))
        grad_low = grad_low + weigh(turned(columns, n), 192 * n)
    for n in range(0, GROUPS, 2):
        pair = []
        for m in (n, n + 1):
            net.arrived(a.dkv.at[m], first_kv + m)
            both = a.dkv[m].astype(F32)
            key = jnp.where(from_zero, both[:, :256], 0.0)
            value = jnp.where(from_zero, pltpu.roll(both[:, 128:], 256 - HD, 1), 0.0)
            pair.append((key, value))
        columns = unwindow(pair[0][0], pair[1][0])
        grad_low = grad_low + weigh(turned(columns, n), z.width + 192 * n)
        columns = unwindow(pair[0][1], pair[1][1])
        piece = jnp.concatenate(columns, axis=1).astype(BF)
        grad_low = grad_low + weigh(piece, 2 * z.width + 192 * n)
    for copy in leaving[-2:]:
        copy.wait()
    gain = rows_of(a.small[...])[0:1]
    root = lax.rsqrt(jnp.mean(x * x, axis=-1, keepdims=True) + EPSILON)
    place = (lanes((z.rows, 128)) == 16).astype(F32).astype(BF)
    high, rest = split(grad_low * x * root)
    a.gsmall[...] += mm(high, place, 0, 0) + mm(rest, place, 0, 0)
    return dm + norm_grad(x, root, gain, grad_low)


class Mixing:
    def __init__(self, z, middle, small, plan):
        table = rows_of(small)
        self.gain, self.consts = table[1:2], (table[2:3], table[3:4])
        self.root = lax.rsqrt(jnp.mean(middle * middle, axis=-1, keepdims=True) + EPSILON)
        self.normed = middle * self.root * self.gain
        self.low, self.rest = split(self.normed)
        expert_of, slot_of = lanes((z.rows, 128)).astype(F32), lanes((z.rows, z.count)).astype(F32)
        self.picks = [(expert_of == plan[:, j : j + 1]).astype(F32) for j in range(TOP)]
        self.chosen = [(slot_of == plan[:, TOP + j : TOP + j + 1]).astype(F32) for j in range(TOP)]
        self.select = (self.chosen[0] + self.chosen[1]).astype(BF)
        self.small = small

    def share(self):
        self.product = mm(self.low, self.small)
        shares = self.product + mm(self.rest, self.small)
        self.shares = []
        for index in range(2):
            one, two = lane_of(shares, 12 + 2 * index), lane_of(shares, 13 + 2 * index)
            peak = jnp.maximum(one, two)
            one, two = jnp.exp(one - peak), jnp.exp(two - peak)
            self.shares.append((one / (one + two), two / (one + two)))

    def gate(self, logits):
        values = [jnp.sum(p * logits, axis=-1, keepdims=True) for p in self.picks]
        peak = jnp.maximum(values[0], values[1])
        powers = [jnp.exp(v - peak) for v in values]
        total = powers[0] + powers[1]
        self.gates = [p / total for p in powers]
        self.combine = self.gates[0] * self.chosen[0] + self.gates[1] * self.chosen[1]

    def weigh(self):
        spread = self.gates[0] * self.picks[0] + self.gates[1] * self.picks[1]
        self.const_weights = [lane_of(spread, NF + 2 + index) for index in range(2)]
        self.normed_weight = lane_of(spread, NF + 1)
        for index in range(2):
            self.normed_weight = (
                self.normed_weight + self.const_weights[index] * self.shares[index][0]
            )


class ExpertRun:
    def __init__(self, net, e, rows_ref, all_ref, chunk):
        self.net, self.e, self.rows_ref, self.all_ref, self.chunk = net, e, rows_ref, all_ref, chunk
        self.mine = net.y * GROUPS + net.g

    def send(self):
        net, z = self.net, self.net.z
        steps = [(dy, dg) for dg in (2, 1, 3, 0) for dy in range(z.hh) if dy or dg]
        first = []
        for dy, dg in steps:
            target = net.up(net.y, dy, z.hh) * GROUPS + net.up(net.g, dg, GROUPS)
            place = self.all_ref.at[net.q, self.mine]
            first.append(net.push(self.rows_ref.at[target], place, net.near(dy=dy, dg=dg)))
        self.all_ref[net.q, self.mine] = self.rows_ref[self.mine]
        self.sources = [(0, 0, None)] + [
            (dy, dg, made) for (dy, dg), made in zip(reversed(steps), reversed(first))
        ]

    def relay(self, while_first):
        net, z = self.net, self.net.z
        self.slots = []
        self.aside, self.across = [[] for _ in range(z.splits)], [[] for _ in range(z.splits)]
        for k, (dy, dg, made) in enumerate(self.sources):
            if made is not None:
                made.wait_recv()
            self.slots.append(net.down(net.y, dy, z.hh) * GROUPS + net.down(net.g, dg, GROUPS))
            place = self.all_ref.at[net.q, self.slots[k]]
            for ds in range(1, z.splits):
                self.aside[ds].append(net.push(place, place, net.near(ds=ds)))
            self.across[0].append(net.push(place, place, net.near(dc=1)))
            if k == 0:
                while_first()

    def compute(self, before_side=None):
        net, z, e = self.net, self.net.z, self.e
        block = (z.experts, SLOT, z.width)
        e.base[...] = self.chunk(net.q).reshape(block)
        other = 1 - net.c
        for ds in range(1, z.splits):
            s = net.down(net.s, ds, z.splits)
            for k, made in enumerate(self.aside[ds]):
                made.wait_recv()
                place = self.all_ref.at[net.c * z.splits + s, self.slots[k]]
                self.across[ds].append(net.push(place, place, net.near(dc=1)))
        self.halves = {}
        for ds in range(z.splits):
            s = net.down(net.s, ds, z.splits)
            for made in self.across[ds]:
                made.wait_recv()
            e.part[ds] = self.chunk(other * z.splits + s).astype(BF).reshape(block)
            to_core = net.push(e.part.at[ds], e.got.at[ds], net.near(dc=1))
            if ds == 0:
                self.first_core = to_core
                continue
            kept = self.chunk(net.c * z.splits + s)
            to_core.wait_recv()
            net.sent = [made for made in net.sent if made is not to_core]
            to_core.wait_send()
            e.part[ds] = (kept.reshape(block) + e.got[ds].astype(F32)).astype(BF)
            if before_side is not None and ds == 1:
                before_side()
            for dy in reversed(range(z.hh)):
                span = pl.ds(net.up(net.y, dy, z.hh) * GROUPS, GROUPS)
                device = net.near(ds=z.splits - ds)
                made = net.push(e.part.at[ds, span], e.side_got.at[ds - 1, span], device)
                self.halves[ds, dy] = made

    def give_back(self):
        net, z, e = self.net, self.net.z, self.e
        self.first_core.wait_recv()
        e.base[...] += e.got[0].astype(F32)
        self.last = []
        for dy in reversed(range(z.hh)):
            y = net.up(net.y, dy, z.hh)
            span = pl.ds(y * GROUPS, GROUPS)
            total = e.base[span]
            for ds in range(1, z.splits):
                self.halves[ds, dy].wait_recv()
                total = total + e.side_got[ds - 1, span].astype(F32)
            e.sum[span] = total.astype(BF)
            for dg in (2, 1, 3, 0):
                if dy or dg:
                    src = e.sum.at[y * GROUPS + net.up(net.g, dg, GROUPS)]
                    made = net.push(src, e.back.at[self.mine], net.near(dy=dy, dg=dg))
                    self.last.append(made)
        e.back[self.mine] = e.sum[self.mine]

    def wait(self):
        for made in self.last:
            made.wait_recv()


def weight_of(z, e, w):
    e.wait_weight(w)
    ref = e.weights[w]
    if z.drow % 16 == 0:
        return ref[...].reshape(z.width, z.ffp)
    return jnp.concatenate([ref[n].astype(F32) for n in range(z.nb)], axis=0).astype(BF)


def held_weights(net, e):
    held = {}

    def weight(w):
        if w not in held:
            held[w] = weight_of(net.z, e, w)
        return held[w]

    return weight


def forward_chunk(net, e, weight):
    z = net.z

    def chunk(part):
        rows = e.all[part].reshape(z.count, z.width)
        gate, up = mm(rows, weight(0)), mm(rows, weight(1))
        e.gate[part], e.up[part] = gate.astype(BF), up.astype(BF)
        hidden = (gate / (1.0 + jnp.exp(-gate)) * up).astype(BF)
        return mm(hidden, weight(2), 1, 1)

    return chunk


def backward_chunk(net, e, weight):
    z = net.z

    def chunk(part):
        weight(0), weight(1)
        rows = e.dall[part].reshape(z.count, z.width)
        grad_hidden = mm(rows, weight(2))
        gate, up = e.gate[part].astype(F32), e.up[part].astype(F32)
        sig = 1.0 / (1.0 + jnp.exp(-gate))
        silu = gate * sig
        e.hid[part] = (silu * up).astype(BF)
        up_low = (grad_hidden * silu).astype(BF)
        gate_low = (grad_hidden * up * (sig * (1.0 + gate * (1.0 - sig)))).astype(BF)
        e.du[part], e.dg[part] = up_low, gate_low
        return mm(gate_low, weight(0), 1, 1) + mm(up_low, weight(1), 1, 1)

    return chunk


def weight_grads(net, e):
    z = net.z
    step = min(4, z.nq)
    for w, one, two in ((0, e.all, e.dg), (1, e.all, e.du), (2, e.dall, e.hid)):
        product = None
        for first in range(0, z.nq, step):
            span = slice(first, first + step)
            left = one[span].reshape(step * z.count, z.width)
            more = mm(left, two[span].reshape(step * z.count, z.ffp), 0, 0)
            product = more if product is None else product + more
        for n in range(z.nb):
            e.gw[w][n] = product[n * z.drow : (n + 1) * z.drow].astype(BF)


def put_rows(mixing, e):
    e.rows[...] = mm(mixing.select, mixing.low, 0, 0).astype(BF).reshape(e.rows.shape)


def put_grad_rows(mixing, e, high, rest):
    weight_high, weight_rest = split(mixing.combine)
    slot_grad = mm(weight_high, high, 0, 0) + mm(weight_rest, high, 0, 0)
    slot_grad = slot_grad + mm(weight_high, rest, 0, 0)
    e.rows[...] = slot_grad.astype(BF).reshape(e.rows.shape)


def mixture(z, mixing, middle, results):
    high, rest = split(mixing.combine)
    mixed = mm(high, results) + mm(rest, results) + mixing.normed_weight * mixing.normed
    for index in range(2):
        weight = mixing.const_weights[index] * mixing.shares[index][1]
        mixed = mixed + weight * mixing.consts[index]
    return middle + mixed


def mixture_grads(z, mixing, grad, grad_logits, high, rest, results):
    where_lane = lanes((z.rows, 128))
    along = mm(high, results, 1, 1) + mm(rest, results, 1, 1)
    normed_dot = jnp.sum(grad * mixing.normed, axis=-1, keepdims=True)
    const_dots = [jnp.sum(grad * c, axis=-1, keepdims=True) for c in mixing.consts]
    gate_grads = []
    for j in range(TOP):
        value = jnp.sum(mixing.chosen[j] * along, axis=-1, keepdims=True)
        value = value + lane_of(mixing.picks[j], NF + 1) * normed_dot
        for index in range(2):
            share = mixing.shares[index]
            value = value + lane_of(mixing.picks[j], NF + 2 + index) * (
                share[0] * normed_dot + share[1] * const_dots[index]
            )
        gate_grads.append(value)
    inner = mixing.gates[0] * gate_grads[0] + mixing.gates[1] * gate_grads[1]
    logit_grad = grad_logits
    for j in range(TOP):
        logit_grad = logit_grad + mixing.picks[j] * (mixing.gates[j] * (gate_grads[j] - inner))
    column = jnp.zeros((z.rows, 128), F32)
    const_columns = jnp.zeros((z.rows, 128), F32)
    for index in range(2):
        share, weight = mixing.shares[index], mixing.const_weights[index]
        one, two = weight * normed_dot, weight * const_dots[index]
        mean = share[0] * one + share[1] * two
        column = column + jnp.where(where_lane == 12 + 2 * index, share[0] * (one - mean), 0.0)
        column = column + jnp.where(where_lane == 13 + 2 * index, share[1] * (two - mean), 0.0)
        const_columns = const_columns + jnp.where(where_lane == 18 + index, weight * share[1], 0.0)
    both_high, both_rest = split(logit_grad + column)
    grad_normed = mm(both_high, mixing.small, 1, 1) + mm(both_rest, mixing.small, 1, 1)
    grad_normed = grad_normed + mixing.normed_weight * grad
    gsmall = mm(mixing.low, both_high, 0, 0) + mm(mixing.low, both_rest, 0, 0)
    gsmall = gsmall + mm(mixing.rest, column.astype(BF), 0, 0)
    const_high, const_rest = split(const_columns)
    gsmall = gsmall + mm(high, const_high, 0, 0) + mm(rest, const_high, 0, 0)
    return logit_grad, grad_normed, gsmall + mm(high, const_rest, 0, 0)


def middle_grads(z, mixing, e, middle, grad, grad_normed, gsmall):
    grad_normed = grad_normed + mm(mixing.select, e.back[...].reshape(z.count, z.width))
    place = (lanes((z.rows, 128)) == 17).astype(F32).astype(BF)
    high, rest = split(grad_normed * middle * mixing.root)
    e.gsmall[...] = gsmall + mm(high, place, 0, 0) + mm(rest, place, 0, 0)
    return grad + norm_grad(middle, mixing.root, mixing.gain, grad_normed)


def experts(net, e, middle, logits_in, at):
    z = net.z
    mixing = Mixing(z, middle, e.small[...], e.plan[...])
    put_rows(mixing, e)
    run = ExpertRun(net, e, e.rows, e.all, forward_chunk(net, e, held_weights(net, e)))

    def while_first():
        mixing.share()
        logits = mixing.product + logits_in
        e.logits[...] = logits
        mixing.gate(logits)
        mixing.weigh()
        act(at.rows)

    run.send()
    run.relay(while_first)
    run.compute()
    act(at.side)
    run.give_back()
    act(at.last)
    run.wait()
    e.results[...] = e.back[...]
    return mixture(z, mixing, middle, e.back[...].reshape(z.count, z.width))


def experts_back(net, e, middle, grad, grad_logits, at):
    z = net.z
    mixing = Mixing(z, middle, e.small[...], e.plan[...])
    mixing.gate(e.logits[...])
    high, rest = split(grad)
    put_grad_rows(mixing, e, high, rest)
    run = ExpertRun(net, e, e.rows, e.dall, backward_chunk(net, e, held_weights(net, e)))
    made = []

    def while_first():
        mixing.share()
        mixing.weigh()
        results = e.results[...].reshape(z.count, z.width)
        made.extend(mixture_grads(z, mixing, grad, grad_logits, high, rest, results))
        act(at.rows_back)

    run.send()
    run.relay(while_first)
    run.compute()
    weight_grads(net, e)
    act(at.side_back)
    run.give_back()
    act(at.last_back)
    run.wait()
    logit_grad, grad_normed, gsmall = made
    return middle_grads(z, mixing, e, middle, grad, grad_normed, gsmall), logit_grad


def experts_both(net, e, later, middle, logits_in, grad, grad_logits, at):
    z = net.z
    mixing = Mixing(z, middle, e.small[...], e.plan[...])
    put_rows(mixing, e)
    weight = held_weights(net, e)
    run = ExpertRun(net, e, e.rows, e.all, forward_chunk(net, e, weight))
    back = ExpertRun(net, later, later.rows, e.dall, backward_chunk(net, e, weight))
    run.send()
    act(at.rows)
    mixing.share()
    mixing.gate(mixing.product + logits_in)
    high, rest = split(grad)
    put_grad_rows(mixing, later, high, rest)
    back.send()
    mixing.weigh()
    run.relay(lambda: None)
    run.compute(lambda: back.relay(lambda: None))
    back.compute()
    run.give_back()
    weight_grads(net, e)
    act(at.side_back)
    back.give_back()
    act(at.last_back)
    run.wait()
    results = e.back[...].reshape(z.count, z.width)
    result = mixture(z, mixing, middle, results)
    made = mixture_grads(z, mixing, grad, grad_logits, high, rest, results)
    back.wait()
    logit_grad, grad_normed, gsmall = made
    return result, middle_grads(z, mixing, later, middle, grad, grad_normed, gsmall), logit_grad


def attend_kept(z):
    return dict(
        middle=struct((z.rows, z.width), F32),
        low=struct((z.rows, z.width), BF),
        q=struct((GROUPS, 3 * z.rows // 2, 128), BF),
        kv=struct((z.nb, z.rows, 384), BF),
        o=struct((GROUPS, z.rows, 256), F32),
        lse=struct((GROUPS, 3 * z.rows, 1), F32),
        ret=struct((GROUPS, 3 * z.rows // 2, 128), BF),
    )


def experts_kept(z):
    block = (z.experts, SLOT, z.width)
    return dict(
        logits=struct((z.rows, 128), F32),
        results=struct(block, BF),
        all=struct((z.nq,) + block, BF),
        gate=struct((z.nq, z.count, z.ffp), BF),
        up=struct((z.nq, z.count, z.ffp), BF),
    )


def attend_scratch(z):
    return dict(
        q_out=pltpu.VMEM((GROUPS, 3 * z.rows // 2, 128), BF),
        kv_out=pltpu.VMEM((GROUPS, z.rows, 384), BF),
        o_out=pltpu.VMEM((GROUPS, 3 * z.rows // 2, 128), BF),
    )


def attend_back_scratch(z, own_output=True):
    one = pltpu.VMEM((GROUPS, 3 * z.rows // 2, 128), BF)
    three = pltpu.VMEM((GROUPS, 3 * z.rows, 256), BF)
    two = pltpu.VMEM((GROUPS, z.rows, 384), BF)
    made = dict(
        do_out=one,
        do=one,
        dq_out=one,
        dq=one,
        dkv_out=pltpu.VMEM((z.nb, z.rows, 384), BF),
        dkv_got=pltpu.VMEM((z.splits - 1, GROUPS, z.rows, 384), BF),
        dkv_sum=two,
        dkv=two,
        q3=three,
        do3=three,
        dq_sum=pltpu.VMEM((GROUPS, z.rows, 256), F32),
        gin_part=pltpu.VMEM((2, z.shards, z.shard, 384), BF),
        gin_sem=pltpu.SemaphoreType.DMA((2,)),
        delta=pltpu.VMEM((GROUPS, 3 * z.rows, 1), F32),
    )
    if not own_output:
        del made["dkv_out"]
    return made


def experts_scratch(z):
    block = (z.experts, SLOT, z.width)
    flat = pltpu.VMEM((z.splits,) + block, BF)
    return dict(
        rows=pltpu.VMEM(block, BF),
        part=flat,
        got=flat,
        side_got=pltpu.VMEM((z.splits - 1,) + block, BF),
        base=pltpu.VMEM(block, F32),
        sum=pltpu.VMEM(block, BF),
        back=pltpu.VMEM(block, BF),
    )


def experts_back_scratch(z, both=True):
    part = pltpu.VMEM((z.nq, z.count, z.ffp), BF)
    block = (z.experts, SLOT, z.width)
    made = dict(dall=pltpu.VMEM((z.nq,) + block, BF), hid=part)
    if both:
        made.update(dict(dg=part, du=part))
    return made


def scratch_of(kept):
    return {name: pltpu.VMEM(v.shape, v.dtype) for name, v in kept.items()}


def view(held, **more):
    return Names(**{**held.__dict__, **more})


def landing(z):
    return struct((z.nb, z.drow, z.ffp), BF)


def near_landing(z):
    return struct((GROUPS, z.drow, z.ffp), BF)


def grad_landing(z):
    return struct((2, z.drow, z.hidden), BF)


def nothing():
    pass


CUT = 256


def in_vmem(arrays):
    return {name: (array, VMEM) for name, array in arrays.items()}


def in_place(arrays):
    return {name: (array, ANY) for name, array in arrays.items()}


def weight_pieces(z, owns, wholes):
    widths = (3 * z.width, z.width)
    return [
        (owns[which], wholes[which], first, columns)
        for which, first, columns in cuts_of((0, 1), widths, CUT)
    ]


def pieces_sems(z, pieces):
    return pieces * (2 + z.splits + z.hh)


def eye(size):
    shape = (size, size)
    return lax.broadcasted_iota(jnp.int32, shape, 0) == lax.broadcasted_iota(jnp.int32, shape, 1)


def upright(row, same):
    return jnp.sum(jnp.where(same, row, 0.0), axis=1, keepdims=True)


def plan_of(z, routes, order):
    same, lane = eye(z.rows), lanes((z.rows, 128))
    ids, ranks = routes.astype(F32), order.astype(F32)
    plan = jnp.zeros((z.rows, 128), F32)
    for j in range(TOP):
        own, rank = upright(ids[j : j + 1], same), upright(ranks[j : j + 1], same)
        before = jnp.zeros((z.rows, 1), F32)
        for k in range(TOP):
            counts = (own == ids[k : k + 1]) & (ranks[k : k + 1] < rank)
            before = before + jnp.sum(counts.astype(F32), axis=1, keepdims=True)
        slot = jnp.where((own < NF) & (before < CAP), own * SLOT + before, -1.0)
        plan = plan + jnp.where(lane == j, own, 0.0) + jnp.where(lane == TOP + j, slot, 0.0)
    return plan


def grid_of(z):
    return (z.hh, 2, 2, 2, z.splits, z.shard)


def gather_first(z, large, little):
    def body(k, net):
        owns, wholes = (k.attn_in.at[0], k.attn_out.at[0]), (k.w_in, k.w_out)
        pieces = weight_pieces(z, owns, wholes)
        gather = Gather(net, pieces, k.own)
        gather.step()
        moves = [
            NearWeights(net, k.expert_0, 0, k.near_0),
            NearWeights(net, k.expert_1, 0, k.near_1),
            NearWeights(net, k.expert_2, 0, k.near_2),
        ]
        same, lane = eye(z.shard), lanes((z.shard, 128))
        for layer in range(LAYERS):
            rows = [k.router[n][layer : layer + 1] for n in range(NE)]
            rows += [k.mix[layer][n : n + 1] for n in range(4)]
            rows += [k.gains[layer][n : n + 1] for n in range(2)]
            rows += [k.consts[layer][n : n + 1] for n in range(2)]
            table = jnp.zeros((z.shard, 128), F32)
            for n, row in enumerate(rows):
                table = table + jnp.where(lane == n, upright(row.astype(F32), same), 0.0)
            k.small_own[layer] = table.astype(BF)
        smalls = [
            (k.small_own.at[layer], whole, 0, 128)
            for layer, whole in enumerate((k.small_0, k.small_1))
        ]
        other = Gather(net, smalls, k.own_too)
        other.step()
        gather.step()
        moves[0].start()
        for layer, plan in enumerate((k.plan_0, k.plan_1)):
            plan[...] = plan_of(z, k.routes[layer], k.order[layer])
        same, lane = eye(z.rows), lanes((z.rows, 128))
        table = jnp.zeros((z.rows, 128), F32)
        for n in range(NE):
            table = table + jnp.where(lane == n, upright(k.prev[n : n + 1], same), 0.0)
        k.logits[...] = table
        gather.step()
        other.step()
        moves[1].start()
        moves[2].start()
        row = lax.broadcasted_iota(jnp.int32, (z.rows, 1), 0) + net.b * z.rows
        angles = row.astype(F32) * k.freqs[...]
        cosine, sine = jnp.cos(angles), jnp.sin(angles)
        sine = jnp.where(lane % HD < HD // 2, -sine, sine)
        for n in range(z.width // 128):
            k.cq[:, 128 * n : 128 * (n + 1)] = cosine
            k.sq[:, 128 * n : 128 * (n + 1)] = sine
        for _ in range(3):
            gather.step()
            other.step()
        other.step()
        for move in moves:
            move.wait()

    ins = {**in_place(large), **in_vmem(little)}
    outs = in_place(
        dict(
            w_in=struct(grid_of(z) + (3 * z.width,), BF),
            w_out=struct(grid_of(z) + (z.width,), BF),
            small_0=struct(grid_of(z) + (128,), BF),
            small_1=struct(grid_of(z) + (128,), BF),
            near_0=near_landing(z),
            near_1=near_landing(z),
            near_2=near_landing(z),
        )
    )
    table, wide = struct((z.rows, 128), F32), struct((z.rows, z.width), F32)
    outs.update(in_vmem(dict(plan_0=table, plan_1=table, logits=table, cq=wide, sq=wide)))
    pieces = len(weight_pieces(z, (0, 0), (0, 0)))
    scratch = dict(
        small_own=pltpu.VMEM((LAYERS, z.shard, 128), BF),
        own=pltpu.SemaphoreType.DMA((pieces,)),
        own_too=pltpu.SemaphoreType.DMA((LAYERS,)),
    )
    return launch(body, 0, z, ins, outs, scratch, pieces_sems(z, pieces + LAYERS) + 3 * GROUPS)


def layer_sems(z):
    attention = 6 + GROUPS * (z.splits - 1) + GROUPS
    expert = (z.experts - 1) * 2 + z.experts * (2 * z.splits - 1) + z.splits + z.hh * z.splits
    back = 3 + GROUPS * (z.splits - 1) + 2 * GROUPS
    return attention, expert, back


def waiting(*moves):
    held = list(moves)

    def wait(w):
        if held[w] is not None:
            held[w].wait()
            held[w] = None

    return wait


def layer_forward(z, values, tables, weights, near, shards, parts):
    def body(k, net):
        owns, wholes = (k.attn_in.at[1], k.attn_out.at[1]), (k.next_in, k.next_out)
        gather = Gather(net, weight_pieces(z, owns, wholes), k.own)
        far = [
            FarWeights(net, k.expert_0, 0, k.near_0, k.weight_0),
            FarWeights(net, k.expert_1, 0, k.near_1, k.weight_1),
            FarWeights(net, k.expert_2, 0, k.near_2, k.weight_2),
        ]
        ahead = [
            NearWeights(net, k.expert_0, 1, k.next_0),
            NearWeights(net, k.expert_1, 1, k.next_1),
            NearWeights(net, k.expert_2, 1, k.next_2),
        ]
        at = Beside(
            start=[gather.step, far[0].start],
            sent=[gather.step, far[1].start],
            mid=[gather.step],
            out=[far[2].start],
            rows=[ahead[0].start],
            side=[gather.step, ahead[1].start],
            last=[ahead[2].start],
        )
        middle = attend(net, k, k.tokens[...].astype(F32), at)
        e = view(k, weights=(k.weight_0, k.weight_1, k.weight_2), wait_weight=waiting(*far))
        k.state[...] = experts(net, e, middle, k.logits_in[...], at)
        gather.step()
        gather.step()
        for move in ahead:
            move.wait()

    ins = {**in_vmem(values), **in_vmem(tables), **in_vmem(weights)}
    ins.update({**in_place(shards), **in_place(parts), **in_place(near)})
    whole = landing(z)
    outs = dict(state=struct((z.rows, z.width), F32))
    outs.update(dict(weight_0=whole, weight_1=whole, weight_2=whole))
    outs = in_vmem({**outs, **attend_kept(z), **experts_kept(z)})
    ahead = dict(
        next_in=struct(grid_of(z) + (3 * z.width,), BF),
        next_out=struct(grid_of(z) + (z.width,), BF),
        next_0=near_landing(z),
        next_1=near_landing(z),
        next_2=near_landing(z),
    )
    outs.update(in_place(ahead))
    pieces = len(weight_pieces(z, (0, 0), (0, 0)))
    own = dict(own=pltpu.SemaphoreType.DMA((pieces,)))
    scratch = {**attend_scratch(z), **experts_scratch(z), **own}
    attention, expert, _ = layer_sems(z)
    count = attention + expert + pieces_sems(z, pieces) + 3 * z.nb + 3 * GROUPS
    return launch(body, 1, z, ins, outs, scratch, count)


def back_outputs(z, more):
    outs = dict(
        grad=struct((z.rows, z.width), F32),
        grad_logits=struct((z.rows, 128), F32),
        gout=struct((z.shards, z.shard, z.width), BF),
        gsmall=struct((z.width, 128), F32),
        gw_2=landing(z),
    )
    rest = dict(
        gin=struct((z.shards, z.shard, 3 * z.width), BF),
        grad_0=grad_landing(z),
        grad_1=grad_landing(z),
    )
    return {**in_vmem({**outs, **more}), **in_place(rest)}


def layer_both(z, values, tables, weights, near, parts):
    together = z.nb <= 8

    def body(k, net):
        far = [
            FarWeights(net, k.expert_0, 1, k.near_0, k.weight_0),
            FarWeights(net, k.expert_1, 1, k.near_1, k.weight_1),
            FarWeights(net, k.expert_2, 1, k.near_2, k.weight_2),
        ]
        grads = [GradMove(net, k.gw_0, k.grad_0), GradMove(net, k.gw_1, k.grad_1)]
        at = Beside(
            start=[far[0].start],
            sent=[far[1].start],
            out=[far[2].start],
            side_back=[grads[0].near],
            last_back=[grads[0].far],
            back_sent=[grads[1].near],
            back_out=[grads[1].far],
        )
        middle = attend(net, k, k.state[...], at)
        e = view(
            k,
            weights=(k.weight_0, k.weight_1, k.weight_2),
            gw=(k.gw_0, k.gw_1, k.gw_2),
            wait_weight=waiting(*far),
            dg=k.gate,
            du=k.up,
        )
        none = jnp.zeros((z.rows, 128), F32)
        grad = k.cotangent[...].astype(F32)
        if together:
            later = view(
                e,
                rows=k.rows_2,
                part=k.part_2,
                got=k.got_2,
                side_got=k.side_got_2,
                base=k.base_2,
                sum=k.sum_2,
                back=k.back_2,
            )
            result, dm, grad_logits = experts_both(
                net, e, later, middle, k.logits_in[...], grad, none, at
            )
        else:
            result = experts(net, e, middle, k.logits_in[...], at)
            net.settle()
            dm, grad_logits = experts_back(net, e, k.middle[...], grad, none, at)
        k.output[...] = result.astype(BF)
        k.grad_logits[...] = grad_logits
        net.settle()
        k.grad[...] = attend_back(net, view(k, dkv_out=k.kv), k.state[...], dm, at)
        for move in grads:
            move.wait()

    ins = {**in_vmem(values), **in_vmem(tables), **in_vmem(weights)}
    ins.update({**in_place(parts), **in_place(near)})
    outs = back_outputs(z, dict(output=struct((z.rows, z.width), BF)))
    scratch = {
        **scratch_of(attend_kept(z)),
        **scratch_of(experts_kept(z)),
        **attend_scratch(z),
        **attend_back_scratch(z, False),
        **experts_scratch(z),
        **experts_back_scratch(z, False),
    }
    if together:
        scratch.update({name + "_2": memory for name, memory in experts_scratch(z).items()})
    place = pltpu.VMEM(landing(z).shape, BF)
    scratch.update(dict(weight_0=place, weight_1=place, weight_2=place, gw_0=place, gw_1=place))
    attention, expert, back = layer_sems(z)
    count = attention + 2 * expert + back + 5 * z.nb
    return launch(body, 2, z, ins, outs, scratch, count)


def sum_pieces(z, k):
    wholes, sums = (k.up_in, k.up_out), (k.sum_in, k.sum_out)
    return weight_pieces(z, wholes, sums) + [(k.up_small, k.sum_small, 0, 128)]


def sum_parts(z, made):
    def grid(v):
        return v.reshape(grid_of(z) + (v.shape[-1],))

    ins = dict(up_in=grid(made.gin), up_out=grid(made.gout), up_small=grid(made.gsmall))
    outs = dict(
        sum_in=struct((z.shard, 3 * z.width), F32),
        sum_out=struct((z.shard, z.width), F32),
        sum_small=struct((z.shard, 128), F32),
    )
    columns = [(c, BF) for _, _, _, c in weight_pieces(z, (0, 0), (0, 0))] + [(128, F32)]
    buffers = reduce_buffers(z, columns)
    buffers.update(dict(mine=pltpu.SemaphoreType.DMA((len(columns),))))
    return ins, outs, buffers, len(columns)


def layer_back(z, values, tables, weights, first, upper):
    ups, sums, buffers, pieces = sum_parts(z, upper)

    def body(k, net):
        reduce = Reduce(net, sum_pieces(z, k), buffers_of(k, pieces), k.mine)
        late = GradMove(net, k.late, k.late_grad)
        own = [
            GradMove(net, k.gw_0, k.grad_0),
            GradMove(net, k.gw_1, k.grad_1),
            GradMove(net, k.gw_2, k.grad_2),
        ]
        at = Beside(
            rows_back=[reduce.step, late.near],
            side_back=[reduce.step, late.far],
            last_back=[own[0].far],
            back_sent=[reduce.step, own[1].far],
            back={1: [own[2].far]},
            back_out=[reduce.step],
        )
        pairs = (
            (k.far_gate, k.gate),
            (k.far_up, k.up),
            (k.far_kv, k.kv),
            (k.far_in, k.w_in),
            (k.far_out, k.w_out),
        )
        loads = [
            pltpu.make_async_copy(far, near, k.load.at[n]) for n, (far, near) in enumerate(pairs)
        ]
        for load in loads:
            load.start()
        reduce.step()

        def wait(w):
            if w == 0:
                loads[0].wait()
                loads[1].wait()

        e = view(
            k,
            weights=(k.weight_0, k.weight_1, k.weight_2),
            gw=(k.gw_0, k.gw_1, k.gw_2),
            wait_weight=wait,
            dg=k.gate,
            du=k.up,
        )
        dm, grad_logits = experts_back(
            net, e, k.middle[...], k.grad_in[...], k.grad_logits_in[...], at
        )
        k.grad_logits[...] = grad_logits
        for load in loads[2:]:
            load.wait()
        x = k.tokens[...].astype(F32)
        k.grad[...] = attend_back(net, view(k, dkv_out=k.kv), x, dm, at)
        reduce.step()
        late.wait()
        for move in own:
            move.wait((False, True))

    kept = {**attend_kept(z), **experts_kept(z)}
    far = dict(far_gate=kept.pop("gate"), far_up=kept.pop("up"), far_kv=kept.pop("kv"))
    loaded = {name[4:]: pltpu.VMEM(v.shape, v.dtype) for name, v in far.items()}
    weights = dict(weights)
    large = dict(far_in=weights.pop("w_in"), far_out=weights.pop("w_out"))
    loaded.update(
        dict(
            w_in=pltpu.VMEM(large["far_in"].shape, BF), w_out=pltpu.VMEM(large["far_out"].shape, BF)
        )
    )
    ins = {**in_vmem(values), **in_vmem(tables), **in_vmem(weights)}
    ins.update(in_vmem({name: getattr(first, name) for name in kept}))
    ins.update(in_place({name: getattr(first, name[4:]) for name in far}))
    ins.update(in_place({**ups, **large, **dict(late=upper.gw_2)}))
    outs = back_outputs(z, {**sums, **dict(gw_0=landing(z), gw_1=landing(z))})
    outs.update(in_place(dict(grad_2=grad_landing(z), late_grad=grad_landing(z))))
    scratch = {
        **attend_back_scratch(z, False),
        **experts_scratch(z),
        **experts_back_scratch(z, False),
        **loaded,
        **buffers,
        **dict(load=pltpu.SemaphoreType.DMA((5,))),
    }
    _, expert, back = layer_sems(z)
    count = expert + back + 4 * z.nb + pieces_sems(z, pieces)
    return launch(body, 3, z, ins, outs, scratch, count)


def reduce_last(z, lower):
    ups, sums, buffers, pieces = sum_parts(z, lower)

    def body(k, net):
        reduce = Reduce(net, sum_pieces(z, k), buffers_of(k, pieces), k.mine)
        reduce.step()
        own = [
            GradMove(net, k.gw_0, k.grad_0),
            GradMove(net, k.gw_1, k.grad_1),
            GradMove(net, k.gw_2, k.grad_2),
        ]
        for move in own:
            move.near()
        for _ in range(5):
            reduce.step()
        for move in own:
            move.wait((True, False))

    half = dict(half_0=lower.grad_0, half_1=lower.grad_1, half_2=lower.grad_2)
    ins = in_place({**ups, **dict(gw_0=lower.gw_0, gw_1=lower.gw_1, gw_2=lower.gw_2), **half})
    whole = grad_landing(z)
    outs = {**in_place(dict(grad_0=whole, grad_1=whole, grad_2=whole)), **in_vmem(sums)}
    same = list(zip(half, outs))
    return launch(body, 4, z, ins, outs, buffers, 3 * z.nb + pieces_sems(z, pieces), same)


def finish(z, upper, lower, final):
    far = dict(
        far_0=final.grad_0,
        far_1=upper.grad_0,
        far_2=final.grad_1,
        far_3=upper.grad_1,
        far_4=final.grad_2,
        far_5=lower.late_grad,
    )
    given = dict(
        output_in=upper.output,
        grad_in=lower.grad,
        logits_in=lower.grad_logits,
        in_0=final.sum_in,
        in_1=lower.sum_in,
        out_0=final.sum_out,
        out_1=lower.sum_out,
        small_0=final.sum_small,
        small_1=lower.sum_small,
    )
    wide = struct((LAYERS, 2, z.drow, z.hidden), F32)
    made = dict(
        output=struct((z.rows, z.width), BF),
        grad=struct((z.rows, z.width), F32),
        logits=struct((NE, z.rows), F32),
        gains=struct((LAYERS, 2, z.shard), F32),
        sum_in=struct((LAYERS, z.shard, 3 * z.width), F32),
        sum_out=struct((LAYERS, z.shard, z.width), F32),
        router=struct((NE, LAYERS, z.shard), F32),
        mix=struct((LAYERS, 4, z.shard), F32),
        consts=struct((LAYERS, 2, z.shard), F32),
    )
    large = dict(gate=wide, up=wide, down=wide)
    ins = {**in_place(far), **in_vmem(given)}
    outs = {**in_vmem(made), **in_place(large)}
    scratch = dict(
        low=pltpu.VMEM((6, 2, z.drow, z.hidden), BF),
        high=pltpu.VMEM((6, 2, z.drow, z.hidden), F32),
        come=pltpu.SemaphoreType.DMA((6,)),
        go=pltpu.SemaphoreType.DMA((12,)),
    )
    names = list(ins) + list(outs) + list(scratch)

    def body(*refs):
        k = Names(**dict(zip(names, refs)))
        parts = (k.far_0, k.far_1, k.far_2, k.far_3, k.far_4, k.far_5)
        loads = [pltpu.make_async_copy(p, k.low.at[n], k.come.at[n]) for n, p in enumerate(parts)]
        for load in loads:
            load.start()
        stores = []
        for n, load in enumerate(loads):
            load.wait()
            whole = (k.gate, k.up, k.down)[n // 2]
            for e in range(2):
                k.high[n, e] = k.low[n, e].astype(F32)
                place = whole.at[n % 2, e]
                stores.append(pltpu.make_async_copy(k.high.at[n, e], place, k.go.at[2 * n + e]))
                stores[-1].start()
        k.output[...] = k.output_in[...]
        k.grad[...] = k.grad_in[...]
        same = eye(z.rows)
        for n in range(NE):
            column = k.logits_in[:, n : n + 1]
            k.logits[n : n + 1] = jnp.sum(jnp.where(same, column, 0.0), axis=0, keepdims=True)
        same = eye(z.shard)
        sums = ((k.in_0, k.out_0, k.small_0), (k.in_1, k.out_1, k.small_1))
        for layer, (sum_in, sum_out, small) in enumerate(sums):
            k.sum_in[layer] = sum_in[...]
            k.sum_out[layer] = sum_out[...]
            for n in range(NE + 8):
                row = jnp.sum(jnp.where(same, small[:, n : n + 1], 0.0), axis=0, keepdims=True)
                if n < NE:
                    k.router[n, layer : layer + 1] = row
                elif n < NE + 4:
                    k.mix[layer, n - NE : n - NE + 1] = row
                elif n < NE + 6:
                    k.gains[layer, n - NE - 4 : n - NE - 3] = row
                else:
                    k.consts[layer, n - NE - 6 : n - NE - 5] = row
        for store in stores:
            store.wait()

    results = pl.pallas_call(
        body,
        out_shape=[v[0] for v in outs.values()],
        in_specs=[v[1] for v in ins.values()],
        out_specs=[v[1] for v in outs.values()],
        scratch_shapes=list(scratch.values()),
        compiler_params=pltpu.CompilerParams(vmem_limit_bytes=VMEM_BYTES),
    )(*[v[0] for v in ins.values()])
    return Names(**dict(zip(outs, results)))


def local(
    tokens,
    prev_logits,
    norm_gains,
    attn_in_weight,
    attn_out_weight,
    router_weight,
    const_mix,
    const_values,
    expert_gate,
    expert_up,
    expert_down,
    routes,
    order,
    cotangent,
):
    rows, width = tokens.shape
    z = Shape(lax.axis_size("head"), lax.axis_size("blk"), rows, width, expert_gate.shape[3])
    lane = np.arange(128) % (HD // 2)
    freqs = np.float32(10000.0) ** (-(2 * lane).astype(np.float32) / np.float32(HD))
    shards = dict(attn_in=attn_in_weight, attn_out=attn_out_weight)
    little = dict(
        router=jnp.transpose(router_weight, (2, 0, 1)),
        mix=jnp.transpose(const_mix, (0, 2, 1)),
        gains=norm_gains,
        consts=const_values,
        routes=jnp.transpose(routes, (0, 2, 1)),
        order=jnp.transpose(order, (0, 2, 1)),
        prev=jnp.transpose(prev_logits),
        freqs=jnp.asarray(freqs.astype(np.float32))[None],
    )
    parts = dict(expert_0=expert_gate, expert_1=expert_up, expert_2=expert_down)
    made = gather_first(z, {**shards, **parts}, little)
    tables = dict(cq=made.cq, sq=made.sq)

    def flat(v):
        return v.reshape(width, v.shape[-1])

    weights = dict(
        w_in=flat(made.w_in),
        w_out=flat(made.w_out),
        small=flat(made.small_0),
    )
    near = dict(near_0=made.near_0, near_1=made.near_1, near_2=made.near_2)
    values = dict(tokens=tokens, logits_in=made.logits, plan=made.plan_0)
    first = layer_forward(z, values, tables, weights, near, shards, parts)
    weights_1 = dict(
        w_in=flat(first.next_in),
        w_out=flat(first.next_out),
        small=flat(made.small_1),
    )
    near = dict(near_0=first.next_0, near_1=first.next_1, near_2=first.next_2)
    values = dict(
        state=first.state, logits_in=first.logits, plan=made.plan_1, cotangent=cotangent
    )
    upper = layer_both(z, values, tables, weights_1, near, parts)
    weights.update(
        dict(weight_0=first.weight_0, weight_1=first.weight_1, weight_2=first.weight_2)
    )
    values = dict(
        tokens=tokens, plan=made.plan_0, grad_in=upper.grad, grad_logits_in=upper.grad_logits
    )
    lower = layer_back(z, values, tables, weights, first, upper)
    final = reduce_last(z, lower)
    done = finish(z, upper, lower, final)
    return (
        done.output,
        done.grad,
        jnp.transpose(done.logits),
        done.gains,
        done.sum_in,
        done.sum_out,
        jnp.transpose(done.router, (1, 2, 0)),
        jnp.transpose(done.mix, (0, 2, 1)),
        done.consts,
        done.gate,
        done.up,
        done.down,
    )


def solution(mesh):
    placed = (
        P(("head", "blk"), None),
        P(("head", "blk"), None),
        P(None, None, ("head", "blk")),
        P(None, ("head", "blk"), None),
        P(None, ("head", "blk"), None),
        P(None, ("head", "blk"), None),
        P(None, ("head", "blk"), None),
        P(None, None, ("head", "blk")),
        P(None, "head", "blk", None),
        P(None, "head", "blk", None),
        P(None, "head", "blk", None),
        P(None, ("head", "blk"), None),
        P(None, ("head", "blk"), None),
        P(("head", "blk"), None),
    )
    return jax.shard_map(
        local,
        mesh=mesh,
        in_specs=placed,
        out_specs=(
            P(("head", "blk"), None),
            P(("head", "blk"), None),
            P(("head", "blk"), None),
            P(None, None, ("head", "blk")),
            P(None, ("head", "blk"), None),
            P(None, ("head", "blk"), None),
            P(None, ("head", "blk"), None),
            P(None, ("head", "blk"), None),
            P(None, None, ("head", "blk")),
            P(None, "head", "blk", None),
            P(None, "head", "blk", None),
            P(None, "head", "blk", None),
        ),
        check_vma=False,
    )
```
